32 devices in a mesh: case: 8 (over z, x), bx: 2 (over y), by: 2 (over core).
Axes of the slice: x: 2, y: 2, z: 4, core: 2. Of those that a mesh axis runs over, the one named last changes fastest.
Arguments:
- displacements: bfloat16 [16, 3, 16, 16, 256], P('case', None, 'bx', 'by'), may hold values from -6 to 6
- material_ids: int32 [16, 16, 256], P('bx', 'by'), may hold values from 0 to 7
- lame: float32 [2, 8], replicated, may hold values from 0.5 to 2
- slab_bounds: int32 [2, 16], P(None, 'bx'), may hold values from 0 to 256, as said below
- load_history: bfloat16 [1024, 16], replicated, may hold values from -1.5 to 1.5
Outputs:
- vm_peak: float32 [16, 16, 256], P('bx', 'by', 'case')
- hyd_range: float32 [16, 16, 256], P('bx', 'by', 'case')
The draws below stay inside these ranges and needn't reach their ends.
Inputs may be any that keep to these rules, and one draw needn't show every extreme that they name: `slab_bounds`: row 0 lies below 64 and row 1 above 192 for every x.
All inputs are finite; a program needn't handle non-finite values.
Results may differ from the reference program's by a relative error of at most 0.00097.
Values may be sent and summed in bfloat16 or wider, within the bound.
No kernel may reach another device: no remote copies, remote signals or barrier semaphores. Data moves between devices by JAX's collectives and lax.ppermute only.
A program may use at most 64 MiB of HBM per device.

```python
import math
import jax
import jax.numpy as jnp
from jax import lax

NZ = 256
TIME = 1024
MATS = 8
CASES = 16
NX = 16
NY = 16


def draw_slab_bounds(key, part):
    lower_key = jax.random.fold_in(key, 11)
    upper_key = jax.random.fold_in(key, 23)
    lower = jax.random.randint(lower_key, (NX,), 0, NZ // 4, dtype=jnp.int32)
    upper = jax.random.randint(upper_key, (NX,), 3 * NZ // 4 + 1, NZ + 1, dtype=jnp.int32)
    lower = lower.at[0].set(0)
    upper = upper.at[NX - 1].set(NZ)
    return jnp.stack([lower, upper]).astype(jnp.int32)


def touch_ends(array, own_key, least, high):
    extent = array.shape
    spot = [jax.random.randint(jax.random.fold_in(own_key, axis), (), 0, extent[axis]) for axis in range(len(extent))]
    array = array.at[tuple(spot)].set(least)
    longest = extent.index(max(extent))
    spot[longest] = (spot[longest] + 1) % extent[longest]
    return array.at[tuple(spot)].set(high)


def levels(key, extent, cuts, smallest, largest):
    loudness = 1.0
    for position, shards_of in cuts:
        heights = jax.random.uniform(jax.random.fold_in(jax.random.fold_in(key, 6), position), (shards_of,), jnp.float32, smallest / len(cuts), largest / len(cuts))
        loudness = loudness * jnp.repeat(jnp.exp(heights), extent[position] // shards_of).reshape((-1,) + (1,) * (len(extent) - 1 - position))
    return loudness


def bell_draw(rng, dims, width, bound, cuts=(), kind=jnp.bfloat16):
    array = width * jax.random.normal(rng, dims, jnp.float32)
    if cuts:
        array = array * levels(rng, dims, cuts, -0.22, 0.18)
    return jnp.clip(array, -bound, bound).astype(kind)


def setup_inputs(seed: int = 0) -> dict:
    keys = jax.random.split(jax.random.key(seed), 6)
    displacements = bell_draw(keys[0], (CASES, 3, NX, NY, NZ), 1.0, 6.0, ((0, 8), (2, 2), (3, 2)))
    material_ids = touch_ends(jax.random.randint(keys[1], (NX, NY, NZ), 0, MATS), jax.random.fold_in(keys[1], 1), 0, MATS - 1).astype(jnp.int32)
    lame = jnp.clip(jnp.exp(jax.random.uniform(keys[2], (2, MATS), jnp.float32, math.log(0.5), math.log(2.0))), 0.5, 2.0)
    slab_bounds = draw_slab_bounds(jax.random.fold_in(keys[5], 71), 0)
    load_history = bell_draw(keys[4], (TIME, CASES), CASES ** -0.5, 1.5)
    return {"displacements": displacements, "material_ids": material_ids, "lame": lame, "slab_bounds": slab_bounds, "load_history": load_history}


def derivative(extended, comp, along):
    field = extended[..., comp, :, :, :]
    if along == 0:
        return 0.5 * (field[..., 2:, 1:-1, 1:-1] - field[..., :-2, 1:-1, 1:-1])
    if along == 1:
        return 0.5 * (field[..., 1:-1, 2:, 1:-1] - field[..., 1:-1, :-2, 1:-1])
    return 0.5 * (field[..., 1:-1, 1:-1, 2:] - field[..., 1:-1, 1:-1, :-2])

def stress_field(extended, shear_mod, lame_first, weight):
    extended = extended.astype(jnp.float32)
    grads = [[derivative(extended, comp, along) for along in range(3)] for comp in range(3)]
    trace = grads[0][0] + grads[1][1] + grads[2][2]
    normal_x = (lame_first * trace + 2.0 * shear_mod * grads[0][0]) * weight
    normal_y = (lame_first * trace + 2.0 * shear_mod * grads[1][1]) * weight
    normal_z = (lame_first * trace + 2.0 * shear_mod * grads[2][2]) * weight
    shear_xy = shear_mod * (grads[0][1] + grads[1][0]) * weight
    shear_yz = shear_mod * (grads[1][2] + grads[2][1]) * weight
    shear_zx = shear_mod * (grads[2][0] + grads[0][2]) * weight
    return jnp.stack([normal_x, normal_y, normal_z, shear_xy, shear_yz, shear_zx], axis=-4)

def invariants(history):
    diff_one = history[:, 0] - history[:, 1]
    diff_two = history[:, 1] - history[:, 2]
    diff_three = history[:, 2] - history[:, 0]
    mises2 = 0.5 * (diff_one * diff_one + diff_two * diff_two + diff_three * diff_three)
    mises2 = mises2 + 3.0 * (history[:, 3] * history[:, 3] + history[:, 4] * history[:, 4] + history[:, 5] * history[:, 5])
    hydro = (history[:, 0] + history[:, 1] + history[:, 2]) / 3.0
    return (mises2, hydro)

def reference(displacements, material_ids, lame, slab_bounds, load_history):
    shear_mod = lame[0][material_ids]
    lame_first = lame[1][material_ids]
    depth = jnp.arange(NZ, dtype=jnp.int32)
    inside = (slab_bounds[0][:, None] <= depth[None, :]) & (depth[None, :] < slab_bounds[1][:, None])
    weight = inside.astype(jnp.float32)[:, None, :]

    def one_case(field):
        extended = jnp.pad(field.astype(jnp.float32), ((0, 0), (1, 1), (1, 1), (1, 1)))
        return stress_field(extended, shear_mod, lame_first, weight).astype(jnp.bfloat16)
    stress = lax.map(one_case, displacements)
    factors = load_history.astype(jnp.float32)

    def per_row(index):
        sheet = lax.dynamic_index_in_dim(stress, index, 2, keepdims=False)
        flat = sheet.reshape(sheet.shape[0], -1).astype(jnp.float32)
        history = jnp.dot(factors, flat, preferred_element_type=jnp.float32).reshape(TIME, 6, NY, NZ)
        mises2, hydro = invariants(history)
        return (jnp.sqrt(lax.optimization_barrier(jnp.max(mises2, axis=0))), lax.optimization_barrier(jnp.max(hydro, axis=0)) - lax.optimization_barrier(jnp.min(hydro, axis=0)))
    vm_peak, hyd_range = lax.map(per_row, jnp.arange(NX, dtype=jnp.int32))
    return (vm_peak, hyd_range)
```

```python
import functools
import math

import jax
import jax.numpy as jnp
import numpy as np
from jax import lax
from jax.experimental import pallas as pl
from jax.experimental.pallas import tpu as pltpu
from jax.sharding import PartitionSpec as P


def extended_2(cells, sides, width):
    for axis, dim in sides:
        count = lax.axis_size(axis)
        ends = count - 1
        head = lax.slice_in_dim(cells, 0, width, axis=dim)
        tail = lax.slice_in_dim(cells, cells.shape[dim] - width, cells.shape[dim], axis=dim)
        cells = jnp.concatenate(
            [
                lax.ppermute(tail, axis, [(i, (i + 1) % count) for i in range(ends)]),
                cells,
                lax.ppermute(head, axis, [((i + 1) % count, i) for i in range(ends)]),
            ],
            axis=dim,
        )
    return cells


def derivative(extended, comp, along):
    field = extended[..., comp, :, :, :]
    if along == 0:
        return 0.5 * (field[..., 2:, 1:-1, 1:-1] - field[..., :-2, 1:-1, 1:-1])
    if along == 1:
        return 0.5 * (field[..., 1:-1, 2:, 1:-1] - field[..., 1:-1, :-2, 1:-1])
    return 0.5 * (field[..., 1:-1, 1:-1, 2:] - field[..., 1:-1, 1:-1, :-2])


def combine_stress(grads, shear_mod, lame_first, weight):
    trace = grads[0][0] + grads[1][1] + grads[2][2]
    normal_x = (lame_first * trace + 2.0 * shear_mod * grads[0][0]) * weight
    normal_y = (lame_first * trace + 2.0 * shear_mod * grads[1][1]) * weight
    normal_z = (lame_first * trace + 2.0 * shear_mod * grads[2][2]) * weight
    shear_xy = shear_mod * (grads[0][1] + grads[1][0]) * weight
    shear_yz = shear_mod * (grads[1][2] + grads[2][1]) * weight
    shear_zx = shear_mod * (grads[2][0] + grads[0][2]) * weight
    return jnp.stack([normal_x, normal_y, normal_z, shear_xy, shear_yz, shear_zx], axis=-4)


def stress_field(extended, shear_mod, lame_first, weight):
    extended = extended.astype(jnp.float32)
    grads = [[derivative(extended, comp, along) for along in range(3)] for comp in range(3)]
    return combine_stress(grads, shear_mod, lame_first, weight)


def material_moduli(material_ids, lame):
    shear_mod = jnp.zeros(material_ids.shape, jnp.float32)
    lame_first = jnp.zeros(material_ids.shape, jnp.float32)
    for material in range(lame.shape[1]):
        picked = material_ids == material
        shear_mod = jnp.where(picked, lame[0, material], shear_mod)
        lame_first = jnp.where(picked, lame[1, material], lame_first)
    return (shear_mod, lame_first)


def histories(load_history, blocks):
    cases, comps, rows, cols, single, slab = blocks.shape
    flat = blocks.reshape(cases, comps * rows * cols * single * slab)
    total = load_history.shape[0]
    step_len = min(128, total)
    top_mises = None
    for begin in range(0, total, step_len):
        factors = load_history[begin : begin + step_len]
        history = jnp.dot(factors, flat, preferred_element_type=jnp.float32).reshape(
            step_len, comps, -1
        )
        diff_one = history[:, 0] - history[:, 1]
        diff_two = history[:, 1] - history[:, 2]
        diff_three = history[:, 2] - history[:, 0]
        mises2 = 0.5 * (diff_one * diff_one + diff_two * diff_two + diff_three * diff_three)
        mises2 = mises2 + 3.0 * (
            history[:, 3] * history[:, 3]
            + history[:, 4] * history[:, 4]
            + history[:, 5] * history[:, 5]
        )
        hydro = (history[:, 0] + history[:, 1] + history[:, 2]) / 3.0
        block_mises = jnp.max(mises2, axis=0)
        block_high = jnp.max(hydro, axis=0)
        block_low = jnp.min(hydro, axis=0)
        if top_mises is None:
            top_mises, high, low = (block_mises, block_high, block_low)
        else:
            top_mises = jnp.maximum(top_mises, block_mises)
            high = jnp.maximum(high, block_high)
            low = jnp.minimum(low, block_low)
    peak = jnp.sqrt(top_mises).reshape(rows, cols, slab)
    spread = (high - low).reshape(rows, cols, slab)
    return (peak, spread)


def shards(displacements, material_ids, lame, slab_bounds, load_history):
    cases_here = displacements.shape[0]
    rows = displacements.shape[2]
    cols = displacements.shape[3]
    depth = displacements.shape[4]
    groups = lax.axis_size("case")
    slab = depth // groups
    shear_mod, lame_first = material_moduli(material_ids, lame)
    levels = jnp.arange(depth, dtype=jnp.int32)
    inside = (slab_bounds[0][:, None] <= levels[None, :]) & (
        levels[None, :] < slab_bounds[1][:, None]
    )
    weight = inside.astype(jnp.float32)[:, None, :]
    bordered = extended_2(displacements, (("bx", 2), ("by", 3)), 1)
    extended = jnp.pad(bordered, ((0, 0), (0, 0), (0, 0), (0, 0), (1, 1)))
    stress = stress_field(extended, shear_mod, lame_first, weight).astype(jnp.bfloat16)
    blocks = stress.reshape(cases_here, 6, rows, cols, groups, slab)
    peak, spread = histories(
        load_history, lax.all_to_all(blocks, "case", split_axis=4, concat_axis=0, tiled=True)
    )
    return (peak, spread)


F32 = jnp.float32
BF16 = jnp.bfloat16
TILE = 128
ROWS = 16
SIDES = 2


def pair_table(cases, groups):
    per = cases // groups
    place = np.array([(j % groups) * per + j // groups for j in range(cases)])
    shifts = cases // 2 + 1
    width = shifts * cases
    total = -(-3 * width // 256) * 256
    first = np.zeros((cases, total), np.float32)
    second = np.zeros((cases, total), np.float32)
    plain = np.zeros((cases, TILE), np.float32)
    for copy in range(3):
        for s in range(shifts):
            for j in range(cases):
                col = copy * width + s * cases + j
                first[place[j], col] = 1.0
                second[place[(j + s) % cases], col] = 1.0 if s in (0, cases // 2) else 2.0
        for j in range(cases):
            plain[place[j], copy * cases + j] = 1.0
    return shifts, width, total, first, second, plain


def prepare_kernel(width, slab, loads, first, second, plain, ids, lame, bounds, pairs, linear, moduli):
    over = (((0,), (0,)), ((), ()))
    table = loads[...]
    prod = lax.dot_general(table, first[...], over, preferred_element_type=F32)
    prod = prod * lax.dot_general(table, second[...], over, preferred_element_type=F32)
    high = prod.astype(BF16)
    low = (prod - high.astype(F32)).astype(BF16)
    col = lax.broadcasted_iota(jnp.int32, prod.shape, 1)
    pairs[...] = jnp.where(col < 2 * width, high.astype(F32), low.astype(F32)).astype(BF16)
    linear[...] = lax.dot_general(table, plain[...], over, preferred_element_type=F32).astype(BF16)
    group = lax.axis_index("case")
    rows, depth = ids.shape
    cols = ROWS // 2
    depth_first = pltpu.roll(ids[...], (depth - group * slab) % depth, 1)[:, :TILE]
    lane = lax.broadcasted_iota(jnp.int32, (ROWS, TILE), 1)
    row = lax.broadcasted_iota(jnp.int32, (ROWS, TILE), 0)
    level = group * slab + lane % slab
    tile = jnp.zeros((ROWS, TILE), jnp.int32)
    lower = jnp.zeros((ROWS, TILE), jnp.int32)
    upper = jnp.zeros((ROWS, TILE), jnp.int32)
    for i in range(TILE // slab):
        here = lane // slab == i
        piece = depth_first[i * ROWS : (i + 1) * ROWS]
        tile = jnp.where(here, piece if i == 0 else pltpu.roll(piece, i * slab, 1), tile)
        for p in range(2):
            spot = here & (row // cols == p)
            lower = jnp.where(spot, bounds[0, 2 * i + p], lower)
            upper = jnp.where(spot, bounds[1, 2 * i + p], upper)
    weight = jnp.where((lower <= level) & (level < upper), 1.0, 0.0).astype(F32)
    for part in range(2):
        value = jnp.zeros((ROWS, TILE), F32)
        for material in range(lame.shape[1]):
            value = jnp.where(tile == material, lame[part, material], value)
        moduli[part] = value * weight


def pack_kernel(slab, field, face_x, face_y, out):
    groups = out.shape[0]
    depth = field.shape[1]
    quarters = TILE // slab
    channels = field.shape[0] // (quarters * ROWS)
    parts = [
        [field[(m * quarters + i) * ROWS : (m * quarters + i + 1) * ROWS, :].astype(F32) for i in range(quarters)]
        for m in range(channels)
    ]
    lane = lax.broadcasted_iota(jnp.int32, (ROWS, depth), 1)
    ends = []
    for i in range(quarters):
        mixed = jnp.zeros((ROWS, depth), F32)
        for m in range(channels):
            below = pltpu.roll(parts[m][i], 2 * m + 1, 1)
            above = pltpu.roll(parts[m][i], (2 * m + 1 - slab) % depth, 1)
            mixed = jnp.where((lane % slab == 2 * m) & (lane >= slab), below, mixed)
            mixed = jnp.where((lane % slab == 2 * m + 1) & (lane < depth - slab), above, mixed)
        ends.append(mixed)
    half = ROWS // 2
    faces = [
        jnp.concatenate([face_x[m * half : (m + 1) * half, :].astype(F32), face_y[m * half : (m + 1) * half, :].astype(F32)], axis=0)
        for m in range(channels)
    ]
    for g in range(groups):
        cut = slice(g * slab, (g + 1) * slab)
        short = slice(g * slab, g * slab + slab // 2)
        for m in range(channels):
            out[g, m * ROWS : (m + 1) * ROWS, :] = jnp.concatenate([parts[m][i][:, cut] for i in range(quarters)], axis=1).astype(BF16)
        top = channels * ROWS
        out[g, top : top + ROWS, :] = jnp.concatenate([faces[q][:, cut] for q in range(4)], axis=1).astype(BF16)
        out[g, top + ROWS : top + 2 * ROWS, :] = jnp.concatenate(
            [faces[4][:, cut], faces[5][:, cut]] + [ends[i][:, short] for i in range(quarters)], axis=1
        ).astype(BF16)


def stress_kernel(shifts, slab, got, pairs, linear, moduli, peak, spread, plain, tiles, rhs, sums, best, high, low):
    groups, rows, _ = got.shape
    quarters = TILE // slab
    channels = rows // ROWS - 2
    per = channels // 3
    cases = per * groups
    cols = ROWS // 2
    width = shifts * cases
    has_lower_x = lax.axis_index("bx") == 1
    has_lower_y = lax.axis_index("by") == 1
    for g in range(groups):
        plain[g * rows : (g + 1) * rows, :] = got[g].astype(F32)

    def gather(row):
        return plain[pl.ds(row, groups, stride=rows), :]

    lane = lax.broadcasted_iota(jnp.int32, (groups, TILE), 1)
    quarter = lane // slab
    for k in range(3):
        for c in range(per):
            m = c * 3 + k
            here = slice(c * groups, (c + 1) * groups)
            for p in range(2):
                for y in range(cols):
                    tiles[k, p, y + 1, here, :] = gather(m * ROWS + p * cols + y)
                edge = jnp.zeros((groups, TILE), F32)
                for i in range(quarters):
                    face = gather((channels + m // 4) * ROWS + cols + 2 * i + p)
                    edge = jnp.where(quarter == i, pltpu.roll(face, (i - m % 4) * slab % TILE, 1), edge)
                tiles[k, p, 0, here, :] = jnp.where(has_lower_y, edge, 0.0)
                tiles[k, p, cols + 1, here, :] = jnp.where(has_lower_y, 0.0, edge)
    rhs[3 * width :, :] = jnp.zeros((rhs.shape[0] - 3 * width, 2 * TILE), BF16)
    wide = lax.broadcasted_iota(jnp.int32, (cases, TILE), 1)

    def both(pieces):
        return jnp.concatenate(pieces, axis=0)

    def column(y, carry):
        stack = []
        face_rows = [gather((channels + j) * ROWS + y) for j in range(2)]
        for p in range(2):
            ends = gather((channels + 1) * ROWS + p * cols + y)
            spaced = jnp.zeros((groups, TILE), F32)
            for i in range(quarters):
                spaced = jnp.where(quarter == i, pltpu.roll(ends, (i * slab - TILE // 2 - i * (slab // 2)) % TILE, 1), spaced)
            grads = []
            for k in range(3):
                mine = tiles[k, p, y + 1]
                other = tiles[k, 1 - p, y + 1]
                beside = [face_rows[(c * 3 + k) // 4] for c in range(per)]
                if p == 0:
                    edge = both([pltpu.roll(beside[c], -((c * 3 + k) % 4) * slab % TILE, 1) for c in range(per)])
                    edge = jnp.where(has_lower_x, edge, 0.0)
                    before = jnp.where(wide < slab, edge, pltpu.roll(other, slab, 1))
                    after = other
                else:
                    edge = both([pltpu.roll(beside[c], (quarters - 1 - (c * 3 + k) % 4) * slab % TILE, 1) for c in range(per)])
                    edge = jnp.where(has_lower_x, 0.0, edge)
                    before = other
                    after = jnp.where(wide >= TILE - slab, edge, pltpu.roll(other, TILE - slab, 1))
                grad_x = 0.5 * (after - before)
                grad_y = 0.5 * (tiles[k, p, y + 2] - tiles[k, p, y])
                below = both([pltpu.roll(spaced, -2 * (c * 3 + k) % TILE, 1) for c in range(per)])
                above = both([pltpu.roll(spaced, (slab - 2 - 2 * (c * 3 + k)) % TILE, 1) for c in range(per)])
                below = jnp.where(wide % slab == 0, below, pltpu.roll(mine, 1, 1))
                above = jnp.where(wide % slab == slab - 1, above, pltpu.roll(mine, TILE - 1, 1))
                grads.append((grad_x, grad_y, 0.5 * (above - below)))
            shear = moduli[0, pl.ds(p * cols + y, 1), :]
            first = moduli[1, pl.ds(p * cols + y, 1), :]
            volume = first * (grads[0][0] + grads[1][1] + grads[2][2])
            twice = 2.0 * shear
            stack.append(
                [
                    volume + twice * grads[0][0],
                    volume + twice * grads[1][1],
                    volume + twice * grads[2][2],
                    shear * (grads[0][1] + grads[1][0]),
                    shear * (grads[1][2] + grads[2][1]),
                    shear * (grads[2][0] + grads[0][2]),
                ]
            )
        stress = [jnp.concatenate([stack[0][n], stack[1][n]], axis=1).astype(BF16) for n in range(6)]
        for n in range(3):
            sums[n * cases : (n + 1) * cases, :] = stress[n]
        exact = [s.astype(F32) for s in stress]
        root = math.sqrt(3.0)
        parts = [
            (0.5 * root) * (exact[0] - exact[1]),
            0.5 * (exact[0] + exact[1]) - exact[2],
            root * exact[3],
            root * exact[4],
            root * exact[5],
        ]
        for s in range(shifts):
            form = None
            for part in parts:
                term = part * (part if s == 0 else pltpu.roll(part, cases - s, 0))
                form = term if form is None else form + term
            upper = form.astype(BF16)
            lower = (form - upper.astype(F32)).astype(BF16)
            at = s * cases
            rhs[at : at + cases, :] = upper
            rhs[width + at : width + at + cases, :] = lower
            rhs[2 * width + at : 2 * width + at + cases, :] = upper
        mises2 = jnp.dot(pairs[...], rhs[...], preferred_element_type=F32)
        top = jnp.max(mises2, axis=0, keepdims=True)
        hydro = jnp.dot(linear[:, : 3 * cases], sums[...], preferred_element_type=F32)
        most = jnp.max(hydro, axis=0, keepdims=True)
        least = jnp.min(hydro, axis=0, keepdims=True)
        for p in range(2):
            cut = slice(p * TILE, (p + 1) * TILE)
            best[p, pl.ds(y, 1), :] = top[:, cut]
            high[p, pl.ds(y, 1), :] = most[:, cut]
            low[p, pl.ds(y, 1), :] = least[:, cut]
        return carry

    lax.fori_loop(0, cols, column, 0)
    for p in range(2):
        vm = jnp.sqrt(jnp.maximum(best[p], 0.0))
        hyd = high[p] * (1.0 / 3.0) - low[p] * (1.0 / 3.0)
        for i in range(quarters):
            cut = slice(i * slab, (i + 1) * slab)
            peak[2 * i + p] = vm[:, cut]
            spread[2 * i + p] = hyd[:, cut]


def swapped_faces(field):
    received = []
    for axis, dim in (("bx", 2), ("by", 3)):
        size = field.shape[dim]
        first = lax.slice_in_dim(field, 0, 1, axis=dim)
        last = lax.slice_in_dim(field, size - 1, size, axis=dim)
        face = jnp.where(lax.axis_index(axis) == 0, last, first)
        face = face.reshape(face.shape[0] * 3 * 8, -1)
        received.append(lax.ppermute(face, axis, [(0, 1), (1, 0)]))
    return received


def tiled_shards(displacements, material_ids, lame, slab_bounds, load_history):
    per, _, rows, cols, depth = displacements.shape
    groups = lax.axis_size("case")
    slab = depth // groups
    cases = per * groups
    steps = load_history.shape[0]
    channels = per * 3
    vmem = pl.BlockSpec(memory_space=pltpu.VMEM)
    smem = pl.BlockSpec(memory_space=pltpu.SMEM)
    shifts, width, total, first, second, plain = pair_table(cases, groups)
    params = pltpu.CompilerParams(vmem_limit_bytes=32 * 1024 * 1024)
    with jax.named_scope("prepare"):
        pairs, linear, moduli = pl.pallas_call(
            functools.partial(prepare_kernel, width, slab),
            out_shape=(
                jax.ShapeDtypeStruct((steps, total), BF16),
                jax.ShapeDtypeStruct((steps, TILE), BF16),
                jax.ShapeDtypeStruct((2, ROWS, TILE), F32),
            ),
            in_specs=[vmem] * 5 + [smem] * 2,
            out_specs=(vmem,) * 3,
            compiler_params=params,
        )(
            load_history.T,
            jnp.asarray(first, BF16),
            jnp.asarray(second, BF16),
            jnp.asarray(plain, BF16),
            material_ids.reshape(rows * cols, depth),
            lame,
            slab_bounds,
        )
    face_x, face_y = swapped_faces(displacements)
    lines = (channels + 2) * ROWS
    with jax.named_scope("pack"):
        packed = pl.pallas_call(
            functools.partial(pack_kernel, slab),
            out_shape=jax.ShapeDtypeStruct((groups, lines, TILE), BF16),
            in_specs=[vmem] * 3,
            out_specs=vmem,
            compiler_params=params,
        )(displacements.reshape(channels * rows * cols, depth), face_x, face_y)
    got = lax.all_to_all(packed, "case", split_axis=0, concat_axis=0, tiled=True)
    with jax.named_scope("stress"):
        return pl.pallas_call(
            functools.partial(stress_kernel, shifts, slab),
            out_shape=(jax.ShapeDtypeStruct((rows, cols, slab), F32),) * 2,
            in_specs=[vmem] * 4,
            out_specs=(vmem,) * 2,
            scratch_shapes=[
                pltpu.VMEM((groups * lines, TILE), F32),
                pltpu.VMEM((3, 2, cols + 2, cases, TILE), F32),
                pltpu.VMEM((total, 2 * TILE), BF16),
                pltpu.VMEM((3 * cases, 2 * TILE), BF16),
                pltpu.VMEM((2, cols, TILE), F32),
                pltpu.VMEM((2, cols, TILE), F32),
                pltpu.VMEM((2, cols, TILE), F32),
            ],
            compiler_params=params,
        )(got, pairs, linear, moduli)


def fits_tiles(mesh, displacements, load_history):
    groups, bricks_x, bricks_y = (mesh.shape[a] for a in ("case", "bx", "by"))
    cases, comps, rows, cols, depth = displacements.shape
    if bricks_x != 2 or bricks_y != 2 or cases % groups or depth % groups:
        return False
    per, rows, cols, slab = cases // groups, rows // 2, cols // 2, depth // groups
    return (
        groups == 8 and per == 2 and comps == 3 and rows == 8 and cols == 8 and slab == 32
        and load_history.shape[0] % 16 == 0
    )


def solution(mesh):
    in_specs = (P("case", None, "bx", "by", None), P("bx", "by", None), P(), P(None, "bx"), P())
    out_specs = (P("bx", "by", "case"), P("bx", "by", "case"))

    def run(displacements, material_ids, lame, slab_bounds, load_history):
        body = tiled_shards if fits_tiles(mesh, displacements, load_history) else shards
        placed = jax.shard_map(body, mesh=mesh, in_specs=in_specs, out_specs=out_specs, check_vma=False)
        return placed(displacements, material_ids, lame, slab_bounds, load_history)

    return run
```

```python
import functools
import math

import jax
import jax.numpy as jnp
import numpy as np
from jax import lax
from jax.experimental import pallas as pl
from jax.experimental.pallas import tpu as pltpu
from jax.sharding import PartitionSpec as P


def extended_2(cells, sides, width):
    for axis, dim in sides:
        count = lax.axis_size(axis)
        ends = count - 1
        head = lax.slice_in_dim(cells, 0, width, axis=dim)
        tail = lax.slice_in_dim(cells, cells.shape[dim] - width, cells.shape[dim], axis=dim)
        cells = jnp.concatenate(
            [
                lax.ppermute(tail, axis, [(i, (i + 1) % count) for i in range(ends)]),
                cells,
                lax.ppermute(head, axis, [((i + 1) % count, i) for i in range(ends)]),
            ],
            axis=dim,
        )
    return cells


def derivative(extended, comp, along):
    field = extended[..., comp, :, :, :]
    if along == 0:
        return 0.5 * (field[..., 2:, 1:-1, 1:-1] - field[..., :-2, 1:-1, 1:-1])
    if along == 1:
        return 0.5 * (field[..., 1:-1, 2:, 1:-1] - field[..., 1:-1, :-2, 1:-1])
    return 0.5 * (field[..., 1:-1, 1:-1, 2:] - field[..., 1:-1, 1:-1, :-2])


def combine_stress(grads, shear_mod, lame_first, weight):
    trace = grads[0][0] + grads[1][1] + grads[2][2]
    normal_x = (lame_first * trace + 2.0 * shear_mod * grads[0][0]) * weight
    normal_y = (lame_first * trace + 2.0 * shear_mod * grads[1][1]) * weight
    normal_z = (lame_first * trace + 2.0 * shear_mod * grads[2][2]) * weight
    shear_xy = shear_mod * (grads[0][1] + grads[1][0]) * weight
    shear_yz = shear_mod * (grads[1][2] + grads[2][1]) * weight
    shear_zx = shear_mod * (grads[2][0] + grads[0][2]) * weight
    return jnp.stack([normal_x, normal_y, normal_z, shear_xy, shear_yz, shear_zx], axis=-4)


def stress_field(extended, shear_mod, lame_first, weight):
    extended = extended.astype(jnp.float32)
    grads = [[derivative(extended, comp, along) for along in range(3)] for comp in range(3)]
    return combine_stress(grads, shear_mod, lame_first, weight)


def material_moduli(material_ids, lame):
    shear_mod = jnp.zeros(material_ids.shape, jnp.float32)
    lame_first = jnp.zeros(material_ids.shape, jnp.float32)
    for material in range(lame.shape[1]):
        picked = material_ids == material
        shear_mod = jnp.where(picked, lame[0, material], shear_mod)
        lame_first = jnp.where(picked, lame[1, material], lame_first)
    return (shear_mod, lame_first)


def histories(load_history, blocks):
    cases, comps, rows, cols, single, slab = blocks.shape
    flat = blocks.reshape(cases, comps * rows * cols * single * slab)
    total = load_history.shape[0]
    step_len = min(128, total)
    top_mises = None
    for begin in range(0, total, step_len):
        factors = load_history[begin : begin + step_len]
        history = jnp.dot(factors, flat, preferred_element_type=jnp.float32).reshape(
            step_len, comps, -1
        )
        diff_one = history[:, 0] - history[:, 1]
        diff_two = history[:, 1] - history[:, 2]
        diff_three = history[:, 2] - history[:, 0]
        mises2 = 0.5 * (diff_one * diff_one + diff_two * diff_two + diff_three * diff_three)
        mises2 = mises2 + 3.0 * (
            history[:, 3] * history[:, 3]
            + history[:, 4] * history[:, 4]
            + history[:, 5] * history[:, 5]
        )
        hydro = (history[:, 0] + history[:, 1] + history[:, 2]) / 3.0
        block_mises = jnp.max(mises2, axis=0)
        block_high = jnp.max(hydro, axis=0)
        block_low = jnp.min(hydro, axis=0)
        if top_mises is None:
            top_mises, high, low = (block_mises, block_high, block_low)
        else:
            top_mises = jnp.maximum(top_mises, block_mises)
            high = jnp.maximum(high, block_high)
            low = jnp.minimum(low, block_low)
    peak = jnp.sqrt(top_mises).reshape(rows, cols, slab)
    spread = (high - low).reshape(rows, cols, slab)
    return (peak, spread)


def shards(displacements, material_ids, lame, slab_bounds, load_history):
    cases_here = displacements.shape[0]
    rows = displacements.shape[2]
    cols = displacements.shape[3]
    depth = displacements.shape[4]
    groups = lax.axis_size("case")
    slab = depth // groups
    shear_mod, lame_first = material_moduli(material_ids, lame)
    levels = jnp.arange(depth, dtype=jnp.int32)
    inside = (slab_bounds[0][:, None] <= levels[None, :]) & (
        levels[None, :] < slab_bounds[1][:, None]
    )
    weight = inside.astype(jnp.float32)[:, None, :]
    bordered = extended_2(displacements, (("bx", 2), ("by", 3)), 1)
    extended = jnp.pad(bordered, ((0, 0), (0, 0), (0, 0), (0, 0), (1, 1)))
    stress = stress_field(extended, shear_mod, lame_first, weight).astype(jnp.bfloat16)
    blocks = stress.reshape(cases_here, 6, rows, cols, groups, slab)
    peak, spread = histories(
        load_history, lax.all_to_all(blocks, "case", split_axis=4, concat_axis=0, tiled=True)
    )
    return (peak, spread)


F32 = jnp.float32
BF16 = jnp.bfloat16
TILE = 128
ROWS = 16
SIDES = 2


def pair_table(cases, groups):
    per = cases // groups
    place = np.array([(j % groups) * per + j // groups for j in range(cases)])
    shifts = cases // 2 + 1
    width = shifts * cases
    total = -(-3 * width // 256) * 256
    first = np.zeros((cases, total), np.float32)
    second = np.zeros((cases, total), np.float32)
    plain = np.zeros((cases, TILE), np.float32)
    for copy in range(3):
        for s in range(shifts):
            for j in range(cases):
                col = copy * width + s * cases + j
                first[place[j], col] = 1.0
                second[place[(j + s) % cases], col] = 1.0 if s in (0, cases // 2) else 2.0
        for j in range(cases):
            plain[place[j], copy * cases + j] = 1.0
    return shifts, width, total, first, second, plain


def prepare_kernel(width, slab, loads, first, second, plain, ids, lame, bounds, pairs, linear, moduli):
    over = (((0,), (0,)), ((), ()))
    table = loads[...]
    prod = lax.dot_general(table, first[...], over, preferred_element_type=F32)
    prod = prod * lax.dot_general(table, second[...], over, preferred_element_type=F32)
    high = prod.astype(BF16)
    low = (prod - high.astype(F32)).astype(BF16)
    col = lax.broadcasted_iota(jnp.int32, prod.shape, 1)
    pairs[...] = jnp.where(col < 2 * width, high.astype(F32), low.astype(F32)).astype(BF16)
    linear[...] = lax.dot_general(table, plain[...], over, preferred_element_type=F32).astype(BF16)
    group = lax.axis_index("case")
    rows, depth = ids.shape
    cols = ROWS // 2
    depth_first = pltpu.roll(ids[...], (depth - group * slab) % depth, 1)[:, :TILE]
    lane = lax.broadcasted_iota(jnp.int32, (ROWS, TILE), 1)
    row = lax.broadcasted_iota(jnp.int32, (ROWS, TILE), 0)
    level = group * slab + lane % slab
    tile = jnp.zeros((ROWS, TILE), jnp.int32)
    lower = jnp.zeros((ROWS, TILE), jnp.int32)
    upper = jnp.zeros((ROWS, TILE), jnp.int32)
    for i in range(TILE // slab):
        here = lane // slab == i
        piece = depth_first[i * ROWS : (i + 1) * ROWS]
        tile = jnp.where(here, piece if i == 0 else pltpu.roll(piece, i * slab, 1), tile)
        for p in range(2):
            spot = here & (row // cols == p)
            lower = jnp.where(spot, bounds[0, 2 * i + p], lower)
            upper = jnp.where(spot, bounds[1, 2 * i + p], upper)
    weight = jnp.where((lower <= level) & (level < upper), 1.0, 0.0).astype(F32)
    for part in range(2):
        value = jnp.zeros((ROWS, TILE), F32)
        for material in range(lame.shape[1]):
            value = jnp.where(tile == material, lame[part, material], value)
        moduli[part] = value * weight


def pack_kernel(slab, field, face_x, face_y, out):
    groups = out.shape[0]
    depth = field.shape[1]
    quarters = TILE // slab
    channels = field.shape[0] // (quarters * ROWS)
    parts = [
        [field[(m * quarters + i) * ROWS : (m * quarters + i + 1) * ROWS, :].astype(F32) for i in range(quarters)]
        for m in range(channels)
    ]
    lane = lax.broadcasted_iota(jnp.int32, (ROWS, depth), 1)
    ends = []
    for i in range(quarters):
        mixed = jnp.zeros((ROWS, depth), F32)
        for m in range(channels):
            below = pltpu.roll(parts[m][i], 2 * m + 1, 1)
            above = pltpu.roll(parts[m][i], (2 * m + 1 - slab) % depth, 1)
            mixed = jnp.where((lane % slab == 2 * m) & (lane >= slab), below, mixed)
            mixed = jnp.where((lane % slab == 2 * m + 1) & (lane < depth - slab), above, mixed)
        ends.append(mixed)
    half = ROWS // 2
    faces = [
        jnp.concatenate([face_x[m * half : (m + 1) * half, :].astype(F32), face_y[m * half : (m + 1) * half, :].astype(F32)], axis=0)
        for m in range(channels)
    ]
    for g in range(groups):
        cut = slice(g * slab, (g + 1) * slab)
        short = slice(g * slab, g * slab + slab // 2)
        for m in range(channels):
            out[g, m * ROWS : (m + 1) * ROWS, :] = jnp.concatenate([parts[m][i][:, cut] for i in range(quarters)], axis=1).astype(BF16)
        top = channels * ROWS
        out[g, top : top + ROWS, :] = jnp.concatenate([faces[q][:, cut] for q in range(4)], axis=1).astype(BF16)
        out[g, top + ROWS : top + 2 * ROWS, :] = jnp.concatenate(
            [faces[4][:, cut], faces[5][:, cut]] + [ends[i][:, short] for i in range(quarters)], axis=1
        ).astype(BF16)


def stress_kernel(shifts, slab, got, pairs, linear, moduli, peak, spread, plain, tiles, rhs_even, rhs_odd, sums_even, sums_odd, best, high, low):
    rhs, sums = (rhs_even, rhs_odd), (sums_even, sums_odd)
    groups, rows, _ = got.shape
    quarters = TILE // slab
    channels = rows // ROWS - 2
    per = channels // 3
    cases = per * groups
    cols = ROWS // 2
    width = shifts * cases
    has_lower_x = lax.axis_index("bx") == 1
    has_lower_y = lax.axis_index("by") == 1
    for g in range(groups):
        plain[g * rows : (g + 1) * rows, :] = got[g].astype(F32)

    def gather(row):
        return plain[pl.ds(row, groups, stride=rows), :]

    lane = lax.broadcasted_iota(jnp.int32, (groups, TILE), 1)
    quarter = lane // slab
    for k in range(3):
        for c in range(per):
            m = c * 3 + k
            here = slice(c * groups, (c + 1) * groups)
            for p in range(2):
                for y in range(cols):
                    tiles[k, p, y + 1, here, :] = gather(m * ROWS + p * cols + y)
                edge = jnp.zeros((groups, TILE), F32)
                for i in range(quarters):
                    face = gather((channels + m // 4) * ROWS + cols + 2 * i + p)
                    edge = jnp.where(quarter == i, pltpu.roll(face, (i - m % 4) * slab % TILE, 1), edge)
                tiles[k, p, 0, here, :] = jnp.where(has_lower_y, edge, 0.0)
                tiles[k, p, cols + 1, here, :] = jnp.where(has_lower_y, 0.0, edge)
    for buffer in rhs:
        buffer[3 * width :, :] = jnp.zeros((buffer.shape[0] - 3 * width, 2 * TILE), BF16)
    wide = lax.broadcasted_iota(jnp.int32, (cases, TILE), 1)

    def both(pieces):
        return jnp.concatenate(pieces, axis=0)

    def build(y, rhs, sums):
        stack = []
        face_rows = [gather((channels + j) * ROWS + y) for j in range(2)]
        for p in range(2):
            ends = gather((channels + 1) * ROWS + p * cols + y)
            spaced = jnp.zeros((groups, TILE), F32)
            for i in range(quarters):
                spaced = jnp.where(quarter == i, pltpu.roll(ends, (i * slab - TILE // 2 - i * (slab // 2)) % TILE, 1), spaced)
            grads = []
            for k in range(3):
                mine = tiles[k, p, y + 1]
                other = tiles[k, 1 - p, y + 1]
                beside = [face_rows[(c * 3 + k) // 4] for c in range(per)]
                if p == 0:
                    edge = both([pltpu.roll(beside[c], -((c * 3 + k) % 4) * slab % TILE, 1) for c in range(per)])
                    edge = jnp.where(has_lower_x, edge, 0.0)
                    before = jnp.where(wide < slab, edge, pltpu.roll(other, slab, 1))
                    after = other
                else:
                    edge = both([pltpu.roll(beside[c], (quarters - 1 - (c * 3 + k) % 4) * slab % TILE, 1) for c in range(per)])
                    edge = jnp.where(has_lower_x, 0.0, edge)
                    before = other
                    after = jnp.where(wide >= TILE - slab, edge, pltpu.roll(other, TILE - slab, 1))
                grad_x = 0.5 * (after - before)
                grad_y = 0.5 * (tiles[k, p, y + 2] - tiles[k, p, y])
                below = both([pltpu.roll(spaced, -2 * (c * 3 + k) % TILE, 1) for c in range(per)])
                above = both([pltpu.roll(spaced, (slab - 2 - 2 * (c * 3 + k)) % TILE, 1) for c in range(per)])
                below = jnp.where(wide % slab == 0, below, pltpu.roll(mine, 1, 1))
                above = jnp.where(wide % slab == slab - 1, above, pltpu.roll(mine, TILE - 1, 1))
                grads.append((grad_x, grad_y, 0.5 * (above - below)))
            shear = moduli[0, pl.ds(p * cols + y, 1), :]
            first = moduli[1, pl.ds(p * cols + y, 1), :]
            volume = first * (grads[0][0] + grads[1][1] + grads[2][2])
            twice = 2.0 * shear
            stack.append(
                [
                    volume + twice * grads[0][0],
                    volume + twice * grads[1][1],
                    volume + twice * grads[2][2],
                    shear * (grads[0][1] + grads[1][0]),
                    shear * (grads[1][2] + grads[2][1]),
                    shear * (grads[2][0] + grads[0][2]),
                ]
            )
        stress = [jnp.concatenate([stack[0][n], stack[1][n]], axis=1).astype(BF16) for n in range(6)]
        for n in range(3):
            sums[n * cases : (n + 1) * cases, :] = stress[n]
        exact = [s.astype(F32) for s in stress]
        root = math.sqrt(3.0)
        parts = [
            (0.5 * root) * (exact[0] - exact[1]),
            0.5 * (exact[0] + exact[1]) - exact[2],
            root * exact[3],
            root * exact[4],
            root * exact[5],
        ]
        for s in range(shifts):
            form = None
            for part in parts:
                term = part * (part if s == 0 else pltpu.roll(part, cases - s, 0))
                form = term if form is None else form + term
            upper = form.astype(BF16)
            lower = (form - upper.astype(F32)).astype(BF16)
            at = s * cases
            rhs[at : at + cases, :] = upper
            rhs[width + at : width + at + cases, :] = lower
            rhs[2 * width + at : 2 * width + at + cases, :] = upper
    def reduce(y, rhs, sums):
        mises2 = jnp.dot(pairs[...], rhs[...], preferred_element_type=F32)
        top = jnp.max(mises2, axis=0, keepdims=True)
        hydro = jnp.dot(linear[:, : 3 * cases], sums[...], preferred_element_type=F32)
        most = jnp.max(hydro, axis=0, keepdims=True)
        least = jnp.min(hydro, axis=0, keepdims=True)
        for p in range(2):
            cut = slice(p * TILE, (p + 1) * TILE)
            best[p, pl.ds(y, 1), :] = top[:, cut]
            high[p, pl.ds(y, 1), :] = most[:, cut]
            low[p, pl.ds(y, 1), :] = least[:, cut]

    build(0, rhs[0], sums[0])
    for y in range(cols):
        if y + 1 < cols:
            build(y + 1, rhs[(y + 1) % 2], sums[(y + 1) % 2])
        reduce(y, rhs[y % 2], sums[y % 2])
    for p in range(2):
        vm = jnp.sqrt(jnp.maximum(best[p], 0.0))
        hyd = high[p] * (1.0 / 3.0) - low[p] * (1.0 / 3.0)
        for i in range(quarters):
            cut = slice(i * slab, (i + 1) * slab)
            peak[2 * i + p] = vm[:, cut]
            spread[2 * i + p] = hyd[:, cut]


def swapped_faces(field):
    received = []
    for axis, dim in (("bx", 2), ("by", 3)):
        size = field.shape[dim]
        first = lax.slice_in_dim(field, 0, 1, axis=dim)
        last = lax.slice_in_dim(field, size - 1, size, axis=dim)
        face = jnp.where(lax.axis_index(axis) == 0, last, first)
        face = face.reshape(face.shape[0] * 3 * 8, -1)
        received.append(lax.ppermute(face, axis, [(0, 1), (1, 0)]))
    return received


def tiled_shards(displacements, material_ids, lame, slab_bounds, load_history):
    per, _, rows, cols, depth = displacements.shape
    groups = lax.axis_size("case")
    slab = depth // groups
    cases = per * groups
    steps = load_history.shape[0]
    channels = per * 3
    vmem = pl.BlockSpec(memory_space=pltpu.VMEM)
    smem = pl.BlockSpec(memory_space=pltpu.SMEM)
    shifts, width, total, first, second, plain = pair_table(cases, groups)
    params = pltpu.CompilerParams(vmem_limit_bytes=32 * 1024 * 1024)
    with jax.named_scope("prepare"):
        pairs, linear, moduli = pl.pallas_call(
            functools.partial(prepare_kernel, width, slab),
            out_shape=(
                jax.ShapeDtypeStruct((steps, total), BF16),
                jax.ShapeDtypeStruct((steps, TILE), BF16),
                jax.ShapeDtypeStruct((2, ROWS, TILE), F32),
            ),
            in_specs=[vmem] * 5 + [smem] * 2,
            out_specs=(vmem,) * 3,
            compiler_params=params,
        )(
            load_history.T,
            jnp.asarray(first, BF16),
            jnp.asarray(second, BF16),
            jnp.asarray(plain, BF16),
            material_ids.reshape(rows * cols, depth),
            lame,
            slab_bounds,
        )
    face_x, face_y = swapped_faces(displacements)
    lines = (channels + 2) * ROWS
    with jax.named_scope("pack"):
        packed = pl.pallas_call(
            functools.partial(pack_kernel, slab),
            out_shape=jax.ShapeDtypeStruct((groups, lines, TILE), BF16),
            in_specs=[vmem] * 3,
            out_specs=vmem,
            compiler_params=params,
        )(displacements.reshape(channels * rows * cols, depth), face_x, face_y)
    got = lax.all_to_all(packed, "case", split_axis=0, concat_axis=0, tiled=True)
    with jax.named_scope("stress"):
        return pl.pallas_call(
            functools.partial(stress_kernel, shifts, slab),
            out_shape=(jax.ShapeDtypeStruct((rows, cols, slab), F32),) * 2,
            in_specs=[vmem] * 4,
            out_specs=(vmem,) * 2,
            scratch_shapes=[
                pltpu.VMEM((groups * lines, TILE), F32),
                pltpu.VMEM((3, 2, cols + 2, cases, TILE), F32),
                pltpu.VMEM((total, 2 * TILE), BF16),
                pltpu.VMEM((total, 2 * TILE), BF16),
                pltpu.VMEM((3 * cases, 2 * TILE), BF16),
                pltpu.VMEM((3 * cases, 2 * TILE), BF16),
                pltpu.VMEM((2, cols, TILE), F32),
                pltpu.VMEM((2, cols, TILE), F32),
                pltpu.VMEM((2, cols, TILE), F32),
            ],
            compiler_params=params,
        )(got, pairs, linear, moduli)


def fits_tiles(mesh, displacements, load_history):
    groups, bricks_x, bricks_y = (mesh.shape[a] for a in ("case", "bx", "by"))
    cases, comps, rows, cols, depth = displacements.shape
    if bricks_x != 2 or bricks_y != 2 or cases % groups or depth % groups:
        return False
    per, rows, cols, slab = cases // groups, rows // 2, cols // 2, depth // groups
    return (
        groups == 8 and per == 2 and comps == 3 and rows == 8 and cols == 8 and slab == 32
        and load_history.shape[0] % 16 == 0
    )


def solution(mesh):
    in_specs = (P("case", None, "bx", "by", None), P("bx", "by", None), P(), P(None, "bx"), P())
    out_specs = (P("bx", "by", "case"), P("bx", "by", "case"))

    def run(displacements, material_ids, lame, slab_bounds, load_history):
        body = tiled_shards if fits_tiles(mesh, displacements, load_history) else shards
        placed = jax.shard_map(body, mesh=mesh, in_specs=in_specs, out_specs=out_specs, check_vma=False)
        return placed(displacements, material_ids, lame, slab_bounds, load_history)

    return run
```

```python
import functools
import math

import jax
import jax.numpy as jnp
import numpy as np
from jax import lax
from jax.experimental import pallas as pl
from jax.experimental.pallas import tpu as pltpu
from jax.sharding import PartitionSpec as P


def extended_2(cells, sides, width):
    for axis, dim in sides:
        count = lax.axis_size(axis)
        ends = count - 1
        head = lax.slice_in_dim(cells, 0, width, axis=dim)
        tail = lax.slice_in_dim(cells, cells.shape[dim] - width, cells.shape[dim], axis=dim)
        cells = jnp.concatenate(
            [
                lax.ppermute(tail, axis, [(i, (i + 1) % count) for i in range(ends)]),
                cells,
                lax.ppermute(head, axis, [((i + 1) % count, i) for i in range(ends)]),
            ],
            axis=dim,
        )
    return cells


def derivative(extended, comp, along):
    field = extended[..., comp, :, :, :]
    if along == 0:
        return 0.5 * (field[..., 2:, 1:-1, 1:-1] - field[..., :-2, 1:-1, 1:-1])
    if along == 1:
        return 0.5 * (field[..., 1:-1, 2:, 1:-1] - field[..., 1:-1, :-2, 1:-1])
    return 0.5 * (field[..., 1:-1, 1:-1, 2:] - field[..., 1:-1, 1:-1, :-2])


def combine_stress(grads, shear_mod, lame_first, weight):
    trace = grads[0][0] + grads[1][1] + grads[2][2]
    normal_x = (lame_first * trace + 2.0 * shear_mod * grads[0][0]) * weight
    normal_y = (lame_first * trace + 2.0 * shear_mod * grads[1][1]) * weight
    normal_z = (lame_first * trace + 2.0 * shear_mod * grads[2][2]) * weight
    shear_xy = shear_mod * (grads[0][1] + grads[1][0]) * weight
    shear_yz = shear_mod * (grads[1][2] + grads[2][1]) * weight
    shear_zx = shear_mod * (grads[2][0] + grads[0][2]) * weight
    return jnp.stack([normal_x, normal_y, normal_z, shear_xy, shear_yz, shear_zx], axis=-4)


def stress_field(extended, shear_mod, lame_first, weight):
    extended = extended.astype(jnp.float32)
    grads = [[derivative(extended, comp, along) for along in range(3)] for comp in range(3)]
    return combine_stress(grads, shear_mod, lame_first, weight)


def material_moduli(material_ids, lame):
    shear_mod = jnp.zeros(material_ids.shape, jnp.float32)
    lame_first = jnp.zeros(material_ids.shape, jnp.float32)
    for material in range(lame.shape[1]):
        picked = material_ids == material
        shear_mod = jnp.where(picked, lame[0, material], shear_mod)
        lame_first = jnp.where(picked, lame[1, material], lame_first)
    return (shear_mod, lame_first)


def histories(load_history, blocks):
    cases, comps, rows, cols, single, slab = blocks.shape
    flat = blocks.reshape(cases, comps * rows * cols * single * slab)
    total = load_history.shape[0]
    step_len = min(128, total)
    top_mises = None
    for begin in range(0, total, step_len):
        factors = load_history[begin : begin + step_len]
        history = jnp.dot(factors, flat, preferred_element_type=jnp.float32).reshape(
            step_len, comps, -1
        )
        diff_one = history[:, 0] - history[:, 1]
        diff_two = history[:, 1] - history[:, 2]
        diff_three = history[:, 2] - history[:, 0]
        mises2 = 0.5 * (diff_one * diff_one + diff_two * diff_two + diff_three * diff_three)
        mises2 = mises2 + 3.0 * (
            history[:, 3] * history[:, 3]
            + history[:, 4] * history[:, 4]
            + history[:, 5] * history[:, 5]
        )
        hydro = (history[:, 0] + history[:, 1] + history[:, 2]) / 3.0
        block_mises = jnp.max(mises2, axis=0)
        block_high = jnp.max(hydro, axis=0)
        block_low = jnp.min(hydro, axis=0)
        if top_mises is None:
            top_mises, high, low = (block_mises, block_high, block_low)
        else:
            top_mises = jnp.maximum(top_mises, block_mises)
            high = jnp.maximum(high, block_high)
            low = jnp.minimum(low, block_low)
    peak = jnp.sqrt(top_mises).reshape(rows, cols, slab)
    spread = (high - low).reshape(rows, cols, slab)
    return (peak, spread)


def shards(displacements, material_ids, lame, slab_bounds, load_history):
    cases_here = displacements.shape[0]
    rows = displacements.shape[2]
    cols = displacements.shape[3]
    depth = displacements.shape[4]
    groups = lax.axis_size("case")
    slab = depth // groups
    shear_mod, lame_first = material_moduli(material_ids, lame)
    levels = jnp.arange(depth, dtype=jnp.int32)
    inside = (slab_bounds[0][:, None] <= levels[None, :]) & (
        levels[None, :] < slab_bounds[1][:, None]
    )
    weight = inside.astype(jnp.float32)[:, None, :]
    bordered = extended_2(displacements, (("bx", 2), ("by", 3)), 1)
    extended = jnp.pad(bordered, ((0, 0), (0, 0), (0, 0), (0, 0), (1, 1)))
    stress = stress_field(extended, shear_mod, lame_first, weight).astype(jnp.bfloat16)
    blocks = stress.reshape(cases_here, 6, rows, cols, groups, slab)
    peak, spread = histories(
        load_history, lax.all_to_all(blocks, "case", split_axis=4, concat_axis=0, tiled=True)
    )
    return (peak, spread)


F32 = jnp.float32
BF16 = jnp.bfloat16
TILE = 128
ROWS = 16
SIDES = 2


def pair_table(cases, groups):
    per = cases // groups
    place = np.array([(j % groups) * per + j // groups for j in range(cases)])
    shifts = cases // 2 + 1
    width = shifts * cases
    total = -(-3 * width // 256) * 256
    first = np.zeros((cases, total), np.float32)
    second = np.zeros((cases, total), np.float32)
    plain = np.zeros((cases, TILE), np.float32)
    for copy in range(3):
        for s in range(shifts):
            for j in range(cases):
                col = copy * width + s * cases + j
                first[place[j], col] = 1.0
                second[place[(j + s) % cases], col] = 1.0 if s in (0, cases // 2) else 2.0
        for j in range(cases):
            plain[place[j], copy * cases + j] = 1.0
    return shifts, width, total, first, second, plain


def prepare_kernel(width, slab, loads, first, second, plain, ids, lame, bounds, pairs, linear, moduli):
    over = (((0,), (0,)), ((), ()))
    table = loads[...]
    prod = lax.dot_general(table, first[...], over, preferred_element_type=F32)
    prod = prod * lax.dot_general(table, second[...], over, preferred_element_type=F32)
    high = prod.astype(BF16)
    low = (prod - high.astype(F32)).astype(BF16)
    col = lax.broadcasted_iota(jnp.int32, prod.shape, 1)
    pairs[...] = jnp.where(col < 2 * width, high.astype(F32), low.astype(F32)).astype(BF16)
    linear[...] = lax.dot_general(table, plain[...], over, preferred_element_type=F32).astype(BF16)
    group = lax.axis_index("case")
    rows, depth = ids.shape
    cols = ROWS // 2
    depth_first = pltpu.roll(ids[...], (depth - group * slab) % depth, 1)[:, :TILE]
    lane = lax.broadcasted_iota(jnp.int32, (ROWS, TILE), 1)
    row = lax.broadcasted_iota(jnp.int32, (ROWS, TILE), 0)
    level = group * slab + lane % slab
    tile = jnp.zeros((ROWS, TILE), jnp.int32)
    lower = jnp.zeros((ROWS, TILE), jnp.int32)
    upper = jnp.zeros((ROWS, TILE), jnp.int32)
    for i in range(TILE // slab):
        here = lane // slab == i
        piece = depth_first[i * ROWS : (i + 1) * ROWS]
        tile = jnp.where(here, piece if i == 0 else pltpu.roll(piece, i * slab, 1), tile)
        for p in range(2):
            spot = here & (row // cols == p)
            lower = jnp.where(spot, bounds[0, 2 * i + p], lower)
            upper = jnp.where(spot, bounds[1, 2 * i + p], upper)
    weight = jnp.where((lower <= level) & (level < upper), 1.0, 0.0).astype(F32)
    for part in range(2):
        value = jnp.zeros((ROWS, TILE), F32)
        for material in range(lame.shape[1]):
            value = jnp.where(tile == material, lame[part, material], value)
        moduli[part] = value * weight


def pack_kernel(slab, field, out):
    groups = out.shape[0]
    depth = field.shape[1]
    quarters = TILE // slab
    channels = field.shape[0] // (quarters * ROWS)
    parts = [
        [field[(m * quarters + i) * ROWS : (m * quarters + i + 1) * ROWS, :].astype(F32) for i in range(quarters)]
        for m in range(channels)
    ]
    lane = lax.broadcasted_iota(jnp.int32, (ROWS, depth), 1)
    ends = []
    for i in range(quarters):
        mixed = jnp.zeros((ROWS, depth), F32)
        for m in range(channels):
            below = pltpu.roll(parts[m][i], 2 * m + 1, 1)
            above = pltpu.roll(parts[m][i], (2 * m + 1 - slab) % depth, 1)
            mixed = jnp.where((lane % slab == 2 * m) & (lane >= slab), below, mixed)
            mixed = jnp.where((lane % slab == 2 * m + 1) & (lane < depth - slab), above, mixed)
        ends.append(mixed)
    for g in range(groups):
        cut = slice(g * slab, (g + 1) * slab)
        for m, pieces in enumerate(parts + [ends]):
            out[g, m * ROWS : (m + 1) * ROWS, :] = jnp.concatenate([piece[:, cut] for piece in pieces], axis=1).astype(BF16)


def gather_kernel(slab, got, tiles, ends, face_x, face_y, plain):
    groups, rows, _ = got.shape
    quarters = TILE // slab
    per = (rows // ROWS - 1) // 3
    cases = per * groups
    cols = ROWS // 2
    brick_x = lax.axis_index("bx")
    brick_y = lax.axis_index("by")
    for g in range(groups):
        plain[g * rows : (g + 1) * rows, :] = got[g].astype(F32)

    def gather(row):
        return plain[pl.ds(row, groups, stride=rows), :]

    def column(k, p, y):
        return jnp.concatenate([gather((c * 3 + k) * ROWS + p * cols + y) for c in range(per)], axis=0)

    lane = lax.broadcasted_iota(jnp.int32, (cases, TILE), 1)
    for y in range(cols):
        packed = jnp.zeros((cases, TILE), F32)
        for k in range(3):
            even, odd = column(k, 0, y), column(k, 1, y)
            tiles[k, 0, y] = even
            tiles[k, 1, y] = odd
            even = pltpu.roll(even, k * slab, 1) if k else even
            odd = pltpu.roll(odd, (k + 1 - quarters) * slab % TILE, 1)
            packed = jnp.where(lane // slab == k, jnp.where(brick_x == 0, odd, even), packed)
            if y == 0:
                firsts = (tiles[k, 0, 0], tiles[k, 1, 0])
                for p in range(2):
                    face_y[k, p] = firsts[p].astype(BF16)
            if y == cols - 1:
                for p in range(2):
                    face_y[k, p] = jnp.where(brick_y == 0, tiles[k, p, y], face_y[k, p].astype(F32)).astype(BF16)
        face_x[y] = packed.astype(BF16)
        for p in range(2):
            ends[p, y] = gather(3 * per * ROWS + p * cols + y)


def column_steps(shifts, slab, tiles, ends, pairs, linear, moduli, face_x, face_y, best, high, low):
    cases = tiles.shape[3]
    groups = ends.shape[2]
    per = cases // groups
    quarters = TILE // slab
    cols = ROWS // 2
    width = shifts * cases
    wide = lax.broadcasted_iota(jnp.int32, (cases, TILE), 1)
    lower_y = lax.axis_index("by") == 1

    def both(pieces):
        return jnp.concatenate(pieces, axis=0)

    def stress_of(p, y, beside):
        last = jnp.where(p == 0, 0, quarters - 1)
        at_edge = wide // slab == last
        sign = jnp.where(p == 0, 0.5, -0.5).astype(F32)
        grads = []
        for k in range(3):
            mine = tiles[k, p, y]
            other = tiles[k, 1 - p, y]
            shifted = pltpu.roll(other, jnp.where(p == 0, slab, TILE - slab), 1)
            if beside:
                edge = pltpu.roll(face_x[y].astype(F32), lax.rem((last - k) * slab + TILE, TILE), 1)
            else:
                edge = jnp.zeros((cases, TILE), F32)
            grad_x = sign * (other - jnp.where(at_edge, edge, shifted))
            before = tiles[k, p, y - 1] if y else jnp.where(lower_y, face_y[k, p].astype(F32), 0.0)
            after = tiles[k, p, y + 1] if y + 1 < cols else jnp.where(lower_y, 0.0, face_y[k, p].astype(F32))
            outside = ends[p, y]
            below = both([pltpu.roll(outside, -2 * (c * 3 + k) % TILE, 1) for c in range(per)])
            above = both([pltpu.roll(outside, (slab - 2 - 2 * (c * 3 + k)) % TILE, 1) for c in range(per)])
            below = jnp.where(wide % slab == 0, below, pltpu.roll(mine, 1, 1))
            above = jnp.where(wide % slab == slab - 1, above, pltpu.roll(mine, TILE - 1, 1))
            grads.append((grad_x, 0.5 * (after - before), 0.5 * (above - below)))
        shear = moduli[0, pl.ds(p * cols + y, 1), :]
        first = moduli[1, pl.ds(p * cols + y, 1), :]
        volume = first * (grads[0][0] + grads[1][1] + grads[2][2])
        twice = 2.0 * shear
        return [
            volume + twice * grads[0][0],
            volume + twice * grads[1][1],
            volume + twice * grads[2][2],
            shear * (grads[0][1] + grads[1][0]),
            shear * (grads[1][2] + grads[2][1]),
            shear * (grads[2][0] + grads[0][2]),
        ]

    def build(step, rhs, sums):
        p, columns, beside, _ = step
        stack = [stress_of(p, y, beside) for y in columns]
        stress = [jnp.concatenate([stack[0][n], stack[1][n]], axis=1).astype(BF16) for n in range(6)]
        for n in range(3):
            sums[n * cases : (n + 1) * cases, :] = stress[n]
        exact = [s.astype(F32) for s in stress]
        root = math.sqrt(3.0)
        parts = [
            (0.5 * root) * (exact[0] - exact[1]),
            0.5 * (exact[0] + exact[1]) - exact[2],
            root * exact[3],
            root * exact[4],
            root * exact[5],
        ]
        for s in range(shifts):
            form = None
            for part in parts:
                term = part * (part if s == 0 else pltpu.roll(part, cases - s, 0))
                form = term if form is None else form + term
            upper = form.astype(BF16)
            lower = (form - upper.astype(F32)).astype(BF16)
            at = s * cases
            rhs[at : at + cases, :] = upper
            rhs[width + at : width + at + cases, :] = lower
            rhs[2 * width + at : 2 * width + at + cases, :] = upper

    def reduce(step, rhs, sums):
        _, columns, _, slot = step
        mises2 = jnp.dot(pairs[...], rhs[...], preferred_element_type=F32)
        hydro = jnp.dot(linear[:, : 3 * cases], sums[...], preferred_element_type=F32)
        tops = (jnp.max(mises2, axis=0, keepdims=True), jnp.max(hydro, axis=0, keepdims=True), jnp.min(hydro, axis=0, keepdims=True))
        for half, y in enumerate(columns):
            for into, row in zip((best, high, low), tops):
                into[slot, y : y + 1, :] = row[:, half * TILE : (half + 1) * TILE]

    return build, reduce


def run_steps(build, reduce, steps, width, rhs, sums):
    for buffer in rhs:
        buffer[3 * width :, :] = jnp.zeros((buffer.shape[0] - 3 * width, 2 * TILE), BF16)
    build(steps[0], rhs[0], sums[0])
    for n, step in enumerate(steps):
        if n + 1 < len(steps):
            build(steps[n + 1], rhs[(n + 1) % 2], sums[(n + 1) % 2])
        reduce(step, rhs[n % 2], sums[n % 2])


def inner_kernel(shifts, slab, tiles, ends, pairs, linear, moduli, best, high, low, rhs_even, rhs_odd, sums_even, sums_odd):
    p = lax.axis_index("bx")
    cols = ROWS // 2
    build, reduce = column_steps(shifts, slab, tiles, ends, pairs, linear, moduli, None, None, best, high, low)
    steps = [(p, (y, y + 1), False, 0) for y in range(1, cols - 1, 2)]
    run_steps(build, reduce, steps, shifts * tiles.shape[3], (rhs_even, rhs_odd), (sums_even, sums_odd))


def outer_kernel(
    shifts, slab, tiles, ends, pairs, linear, moduli, face_x, face_y, inner_best, inner_high, inner_low,
    peak, spread, rhs_even, rhs_odd, sums_even, sums_odd, best, high, low,
):
    p = lax.axis_index("bx")
    cols = ROWS // 2
    build, reduce = column_steps(shifts, slab, tiles, ends, pairs, linear, moduli, face_x, face_y, best, high, low)
    steps = [(p, (0, cols - 1), False, 0)] + [(1 - p, (y, y + 1), True, 1) for y in range(0, cols, 2)]
    run_steps(build, reduce, steps, shifts * tiles.shape[3], (rhs_even, rhs_odd), (sums_even, sums_odd))
    for into, inner in ((best, inner_best), (high, inner_high), (low, inner_low)):
        into[0, 1 : cols - 1, :] = inner[0, 1 : cols - 1, :]
    for slot, parity in ((0, p), (1, 1 - p)):
        vm = jnp.sqrt(jnp.maximum(best[slot], 0.0))
        hyd = high[slot] * (1.0 / 3.0) - low[slot] * (1.0 / 3.0)
        for i in range(TILE // slab):
            cut = slice(i * slab, (i + 1) * slab)
            peak[2 * i + parity] = vm[:, cut]
            spread[2 * i + parity] = hyd[:, cut]


def tiled_shards(displacements, material_ids, lame, slab_bounds, load_history):
    per, _, rows, cols, depth = displacements.shape
    groups = lax.axis_size("case")
    slab = depth // groups
    cases = per * groups
    steps = load_history.shape[0]
    channels = per * 3
    vmem = pl.BlockSpec(memory_space=pltpu.VMEM)
    smem = pl.BlockSpec(memory_space=pltpu.SMEM)
    shifts, width, total, first, second, plain = pair_table(cases, groups)
    params = pltpu.CompilerParams(vmem_limit_bytes=32 * 1024 * 1024)
    like = jax.ShapeDtypeStruct
    with jax.named_scope("prepare"):
        pairs, linear, moduli = pl.pallas_call(
            functools.partial(prepare_kernel, width, slab),
            out_shape=(like((steps, total), BF16), like((steps, TILE), BF16), like((2, ROWS, TILE), F32)),
            in_specs=[vmem] * 5 + [smem] * 2,
            out_specs=(vmem,) * 3,
            compiler_params=params,
        )(
            load_history.T,
            jnp.asarray(first, BF16),
            jnp.asarray(second, BF16),
            jnp.asarray(plain, BF16),
            material_ids.reshape(rows * cols, depth),
            lame,
            slab_bounds,
        )
    lines = (channels + 1) * ROWS
    with jax.named_scope("pack"):
        packed = pl.pallas_call(
            functools.partial(pack_kernel, slab),
            out_shape=like((groups, lines, TILE), BF16),
            in_specs=[vmem],
            out_specs=vmem,
            compiler_params=params,
        )(displacements.reshape(channels * rows * cols, depth))
    got = lax.all_to_all(packed, "case", split_axis=0, concat_axis=0, tiled=True)
    with jax.named_scope("gather"):
        tiles, ends, face_x, face_y = pl.pallas_call(
            functools.partial(gather_kernel, slab),
            out_shape=(
                like((3, 2, cols, cases, TILE), F32),
                like((2, cols, groups, TILE), F32),
                like((cols, cases, TILE), BF16),
                like((3, 2, cases, TILE), BF16),
            ),
            in_specs=[vmem],
            out_specs=(vmem,) * 4,
            scratch_shapes=[pltpu.VMEM((groups * lines, TILE), F32)],
            compiler_params=params,
        )(got)
    face_x = lax.ppermute(face_x, "bx", [(0, 1), (1, 0)])
    face_y = lax.ppermute(face_y, "by", [(0, 1), (1, 0)])
    buffers = [pltpu.VMEM((total, 2 * TILE), BF16)] * 2 + [pltpu.VMEM((3 * cases, 2 * TILE), BF16)] * 2
    with jax.named_scope("inner"):
        inner = pl.pallas_call(
            functools.partial(inner_kernel, shifts, slab),
            out_shape=(like((1, cols, TILE), F32),) * 3,
            in_specs=[vmem] * 5,
            out_specs=(vmem,) * 3,
            scratch_shapes=buffers,
            compiler_params=params,
        )(tiles, ends, pairs, linear, moduli)
    with jax.named_scope("outer"):
        return pl.pallas_call(
            functools.partial(outer_kernel, shifts, slab),
            out_shape=(like((rows, cols, slab), F32),) * 2,
            in_specs=[vmem] * 10,
            out_specs=(vmem,) * 2,
            scratch_shapes=buffers + [pltpu.VMEM((2, cols, TILE), F32)] * 3,
            compiler_params=params,
        )(tiles, ends, pairs, linear, moduli, face_x, face_y, *inner)


def fits_tiles(mesh, displacements, load_history):
    groups, bricks_x, bricks_y = (mesh.shape[a] for a in ("case", "bx", "by"))
    cases, comps, rows, cols, depth = displacements.shape
    if bricks_x != 2 or bricks_y != 2 or cases % groups or depth % groups:
        return False
    per, rows, cols, slab = cases // groups, rows // 2, cols // 2, depth // groups
    return (
        groups == 8 and per == 2 and comps == 3 and rows == 8 and cols == 8 and slab == 32
        and load_history.shape[0] % 16 == 0
    )


def solution(mesh):
    in_specs = (P("case", None, "bx", "by", None), P("bx", "by", None), P(), P(None, "bx"), P())
    out_specs = (P("bx", "by", "case"), P("bx", "by", "case"))

    def run(displacements, material_ids, lame, slab_bounds, load_history):
        body = tiled_shards if fits_tiles(mesh, displacements, load_history) else shards
        placed = jax.shard_map(body, mesh=mesh, in_specs=in_specs, out_specs=out_specs, check_vma=False)
        return placed(displacements, material_ids, lame, slab_bounds, load_history)

    return run
```

```python
import functools
import math

import jax
import jax.numpy as jnp
import numpy as np
from jax import lax
from jax.experimental import pallas as pl
from jax.experimental.pallas import tpu as pltpu
from jax.sharding import PartitionSpec as P


def extended_2(cells, sides, width):
    for axis, dim in sides:
        count = lax.axis_size(axis)
        ends = count - 1
        head = lax.slice_in_dim(cells, 0, width, axis=dim)
        tail = lax.slice_in_dim(cells, cells.shape[dim] - width, cells.shape[dim], axis=dim)
        cells = jnp.concatenate(
            [
                lax.ppermute(tail, axis, [(i, (i + 1) % count) for i in range(ends)]),
                cells,
                lax.ppermute(head, axis, [((i + 1) % count, i) for i in range(ends)]),
            ],
            axis=dim,
        )
    return cells


def derivative(extended, comp, along):
    field = extended[..., comp, :, :, :]
    if along == 0:
        return 0.5 * (field[..., 2:, 1:-1, 1:-1] - field[..., :-2, 1:-1, 1:-1])
    if along == 1:
        return 0.5 * (field[..., 1:-1, 2:, 1:-1] - field[..., 1:-1, :-2, 1:-1])
    return 0.5 * (field[..., 1:-1, 1:-1, 2:] - field[..., 1:-1, 1:-1, :-2])


def combine_stress(grads, shear_mod, lame_first, weight):
    trace = grads[0][0] + grads[1][1] + grads[2][2]
    normal_x = (lame_first * trace + 2.0 * shear_mod * grads[0][0]) * weight
    normal_y = (lame_first * trace + 2.0 * shear_mod * grads[1][1]) * weight
    normal_z = (lame_first * trace + 2.0 * shear_mod * grads[2][2]) * weight
    shear_xy = shear_mod * (grads[0][1] + grads[1][0]) * weight
    shear_yz = shear_mod * (grads[1][2] + grads[2][1]) * weight
    shear_zx = shear_mod * (grads[2][0] + grads[0][2]) * weight
    return jnp.stack([normal_x, normal_y, normal_z, shear_xy, shear_yz, shear_zx], axis=-4)


def stress_field(extended, shear_mod, lame_first, weight):
    extended = extended.astype(jnp.float32)
    grads = [[derivative(extended, comp, along) for along in range(3)] for comp in range(3)]
    return combine_stress(grads, shear_mod, lame_first, weight)


def material_moduli(material_ids, lame):
    shear_mod = jnp.zeros(material_ids.shape, jnp.float32)
    lame_first = jnp.zeros(material_ids.shape, jnp.float32)
    for material in range(lame.shape[1]):
        picked = material_ids == material
        shear_mod = jnp.where(picked, lame[0, material], shear_mod)
        lame_first = jnp.where(picked, lame[1, material], lame_first)
    return (shear_mod, lame_first)


def histories(load_history, blocks):
    cases, comps, rows, cols, single, slab = blocks.shape
    flat = blocks.reshape(cases, comps * rows * cols * single * slab)
    total = load_history.shape[0]
    step_len = min(128, total)
    top_mises = None
    for begin in range(0, total, step_len):
        factors = load_history[begin : begin + step_len]
        history = jnp.dot(factors, flat, preferred_element_type=jnp.float32).reshape(
            step_len, comps, -1
        )
        diff_one = history[:, 0] - history[:, 1]
        diff_two = history[:, 1] - history[:, 2]
        diff_three = history[:, 2] - history[:, 0]
        mises2 = 0.5 * (diff_one * diff_one + diff_two * diff_two + diff_three * diff_three)
        mises2 = mises2 + 3.0 * (
            history[:, 3] * history[:, 3]
            + history[:, 4] * history[:, 4]
            + history[:, 5] * history[:, 5]
        )
        hydro = (history[:, 0] + history[:, 1] + history[:, 2]) / 3.0
        block_mises = jnp.max(mises2, axis=0)
        block_high = jnp.max(hydro, axis=0)
        block_low = jnp.min(hydro, axis=0)
        if top_mises is None:
            top_mises, high, low = (block_mises, block_high, block_low)
        else:
            top_mises = jnp.maximum(top_mises, block_mises)
            high = jnp.maximum(high, block_high)
            low = jnp.minimum(low, block_low)
    peak = jnp.sqrt(top_mises).reshape(rows, cols, slab)
    spread = (high - low).reshape(rows, cols, slab)
    return (peak, spread)


def shards(displacements, material_ids, lame, slab_bounds, load_history):
    cases_here = displacements.shape[0]
    rows = displacements.shape[2]
    cols = displacements.shape[3]
    depth = displacements.shape[4]
    groups = lax.axis_size("case")
    slab = depth // groups
    shear_mod, lame_first = material_moduli(material_ids, lame)
    levels = jnp.arange(depth, dtype=jnp.int32)
    inside = (slab_bounds[0][:, None] <= levels[None, :]) & (
        levels[None, :] < slab_bounds[1][:, None]
    )
    weight = inside.astype(jnp.float32)[:, None, :]
    bordered = extended_2(displacements, (("bx", 2), ("by", 3)), 1)
    extended = jnp.pad(bordered, ((0, 0), (0, 0), (0, 0), (0, 0), (1, 1)))
    stress = stress_field(extended, shear_mod, lame_first, weight).astype(jnp.bfloat16)
    blocks = stress.reshape(cases_here, 6, rows, cols, groups, slab)
    peak, spread = histories(
        load_history, lax.all_to_all(blocks, "case", split_axis=4, concat_axis=0, tiled=True)
    )
    return (peak, spread)


F32 = jnp.float32
BF16 = jnp.bfloat16
TILE = 128
ROWS = 16
EXCHANGE_ORDER = (5, 6, 4, 1, 7, 3, 2, 0)


def pair_table(cases, order):
    groups = len(order)
    per = cases // groups
    place = np.array([order[j % groups] * per + j // groups for j in range(cases)])
    half = cases // 2
    main = half * cases
    first = np.zeros((cases, main + TILE), np.float32)
    second = np.zeros((cases, main + TILE), np.float32)
    plain = np.zeros((cases, TILE), np.float32)
    for j in range(cases):
        for s in range(half):
            first[place[j], s * cases + j] = 1.0
            second[place[(j + s) % cases], s * cases + j] = 2.0 if s else 1.0
        for copy in range(3):
            first[place[j], main + copy * cases + j] = 1.0
            second[place[(j + half) % cases], main + copy * cases + j] = 1.0
            plain[place[j], copy * cases + j] = 1.0
    return main, np.concatenate([first, second, plain], axis=1)


def prepare_kernel(main, slab, loads, picks, ids, lame, bounds, pairs, linear, moduli):
    over = (((0,), (0,)), ((), ()))
    table = loads[...]
    factor = lax.dot_general(table, picks[...], over, preferred_element_type=F32)
    wide = main + TILE
    prod = factor[:, :wide] * factor[:, wide : 2 * wide]
    most = prod[:, :main]
    high = most.astype(BF16)
    pairs[:, :main] = high
    pairs[:, main : 2 * main] = high
    pairs[:, 2 * main : 3 * main] = (most - high.astype(F32)).astype(BF16)
    last = prod[:, main:]
    high = last.astype(BF16).astype(F32)
    col = lax.broadcasted_iota(jnp.int32, last.shape, 1)
    pairs[:, 3 * main :] = jnp.where(col < 2 * table.shape[0], high, last - high).astype(BF16)
    linear[...] = factor[:, 2 * wide :].astype(BF16)
    group = lax.axis_index("case")
    rows, depth = ids.shape
    cols = ROWS // 2
    depth_first = pltpu.roll(ids[...], (depth - group * slab) % depth, 1)[:, :TILE]
    lane = lax.broadcasted_iota(jnp.int32, (ROWS, TILE), 1)
    row = lax.broadcasted_iota(jnp.int32, (ROWS, TILE), 0)
    level = group * slab + lane % slab
    tile = jnp.zeros((ROWS, TILE), jnp.int32)
    lower = jnp.zeros((ROWS, TILE), jnp.int32)
    upper = jnp.zeros((ROWS, TILE), jnp.int32)
    for i in range(TILE // slab):
        here = lane // slab == i
        piece = depth_first[i * ROWS : (i + 1) * ROWS]
        tile = jnp.where(here, piece if i == 0 else pltpu.roll(piece, i * slab, 1), tile)
        for p in range(2):
            spot = here & (row // cols == p)
            lower = jnp.where(spot, bounds[0:1, 2 * i + p : 2 * i + p + 1], lower)
            upper = jnp.where(spot, bounds[1:2, 2 * i + p : 2 * i + p + 1], upper)
    weight = jnp.where((lower <= level) & (level < upper), 1.0, 0.0).astype(F32)
    for part in range(2):
        value = jnp.zeros((ROWS, TILE), F32)
        for material in range(lame.shape[1]):
            value = jnp.where(tile == material, lame[part : part + 1, material : material + 1], value)
        moduli[part] = value * weight


def pack_kernel(slab, order, field, out):
    depth = field.shape[1]
    quarters = TILE // slab
    channels = field.shape[0] // (quarters * ROWS)
    parts = [
        [field[(m * quarters + i) * ROWS : (m * quarters + i + 1) * ROWS, :].astype(F32) for i in range(quarters)]
        for m in range(channels)
    ]
    lane = lax.broadcasted_iota(jnp.int32, (ROWS, depth), 1)
    ends = []
    for i in range(quarters):
        mixed = jnp.zeros((ROWS, depth), F32)
        for m in range(channels):
            below = pltpu.roll(parts[m][i], 2 * m + 1, 1)
            above = pltpu.roll(parts[m][i], (2 * m + 1 - slab) % depth, 1)
            mixed = jnp.where((lane % slab == 2 * m) & (lane >= slab), below, mixed)
            mixed = jnp.where((lane % slab == 2 * m + 1) & (lane < depth - slab), above, mixed)
        ends.append(mixed)
    cols = ROWS // 2
    for at, g in enumerate(order):
        cut = slice(g * slab, (g + 1) * slab)
        short = slice(g * slab, g * slab + slab // 2)
        for m, pieces in enumerate(parts):
            out[at, m * ROWS : (m + 1) * ROWS, :] = jnp.concatenate([piece[:, cut] for piece in pieces], axis=1).astype(BF16)
        outer = [end[p * cols : (p + 1) * cols, short] for p in range(2) for end in ends]
        out[at, channels * ROWS :, :] = jnp.concatenate(outer, axis=1).astype(BF16)


def gather_kernel(slab, got, tiles, ends, face_x, face_y, plain):
    groups, rows, _ = got.shape
    quarters = TILE // slab
    per = rows // ROWS // 3
    cases = per * groups
    cols = ROWS // 2
    brick_x = lax.axis_index("bx")
    brick_y = lax.axis_index("by")
    for g in range(groups):
        plain[g * rows : (g + 1) * rows, :] = got[g].astype(F32)

    def gather(row):
        return plain[pl.ds(row, groups, stride=rows), :]

    def column(k, p, y):
        return jnp.concatenate([gather((c * 3 + k) * ROWS + p * cols + y) for c in range(per)], axis=0)

    lane = lax.broadcasted_iota(jnp.int32, (cases, TILE), 1)
    for y in range(cols):
        packed = jnp.zeros((cases, TILE), F32)
        for k in range(3):
            even, odd = column(k, 0, y), column(k, 1, y)
            tiles[k, 0, y] = even
            tiles[k, 1, y] = odd
            even = pltpu.roll(even, k * slab, 1) if k else even
            odd = pltpu.roll(odd, (k + 1 - quarters) * slab % TILE, 1)
            packed = jnp.where(lane // slab == k, jnp.where(brick_x == 0, odd, even), packed)
            if y == 0:
                firsts = (tiles[k, 0, 0], tiles[k, 1, 0])
                for p in range(2):
                    face_y[k, p] = firsts[p].astype(BF16)
            if y == cols - 1:
                for p in range(2):
                    face_y[k, p] = jnp.where(brick_y == 0, tiles[k, p, y], face_y[k, p].astype(F32)).astype(BF16)
        face_x[y] = packed.astype(BF16)
        outer = gather(3 * per * ROWS + y)
        for p in range(2):
            spaced = jnp.zeros((groups, TILE), F32)
            for i in range(quarters):
                moved = pltpu.roll(outer, (i * slab - (p * quarters + i) * (slab // 2)) % TILE, 1)
                spaced = jnp.where(lane[:groups] // slab == i, moved, spaced)
            ends[p, y] = spaced


def column_steps(slab, tiles, ends, pairs, linear, moduli, face_x, face_y, best, high, low):
    cases = tiles.shape[3]
    groups = ends.shape[2]
    per = cases // groups
    quarters = TILE // slab
    cols = ROWS // 2
    main = cases // 2 * cases
    wide = lax.broadcasted_iota(jnp.int32, (cases, TILE), 1)
    lower_y = lax.axis_index("by") == 1

    def both(pieces):
        return jnp.concatenate(pieces, axis=0)

    def stress_of(p, y, beside):
        last = jnp.where(p == 0, 0, quarters - 1)
        at_edge = wide // slab == last
        sign = jnp.where(p == 0, 0.5, -0.5).astype(F32)
        grads = []
        for k in range(3):
            mine = tiles[k, p, y]
            other = tiles[k, 1 - p, y]
            shifted = pltpu.roll(other, jnp.where(p == 0, slab, TILE - slab), 1)
            if beside:
                edge = pltpu.roll(face_x[y].astype(F32), lax.rem((last - k) * slab + TILE, TILE), 1)
            else:
                edge = jnp.zeros((cases, TILE), F32)
            grad_x = sign * (other - jnp.where(at_edge, edge, shifted))
            before = tiles[k, p, y - 1] if y else jnp.where(lower_y, face_y[k, p].astype(F32), 0.0)
            after = tiles[k, p, y + 1] if y + 1 < cols else jnp.where(lower_y, 0.0, face_y[k, p].astype(F32))
            outside = ends[p, y]
            below = both([pltpu.roll(outside, -2 * (c * 3 + k) % TILE, 1) for c in range(per)])
            above = both([pltpu.roll(outside, (slab - 2 - 2 * (c * 3 + k)) % TILE, 1) for c in range(per)])
            below = jnp.where(wide % slab == 0, below, pltpu.roll(mine, 1, 1))
            above = jnp.where(wide % slab == slab - 1, above, pltpu.roll(mine, TILE - 1, 1))
            grads.append((grad_x, 0.5 * (after - before), 0.5 * (above - below)))
        shear = moduli[0, pl.ds(p * cols + y, 1), :]
        first = moduli[1, pl.ds(p * cols + y, 1), :]
        volume = first * (grads[0][0] + grads[1][1] + grads[2][2])
        twice = 2.0 * shear
        return [
            volume + twice * grads[0][0],
            volume + twice * grads[1][1],
            volume + twice * grads[2][2],
            shear * (grads[0][1] + grads[1][0]),
            shear * (grads[1][2] + grads[2][1]),
            shear * (grads[2][0] + grads[0][2]),
        ]

    def build(step, rhs, sums):
        p, columns, beside, _ = step
        stack = [stress_of(p, y, beside) for y in columns]
        stress = [jnp.concatenate([stack[0][n], stack[1][n]], axis=1).astype(BF16) for n in range(6)]
        for n in range(3):
            sums[n * cases : (n + 1) * cases, :] = stress[n]
        exact = [s.astype(F32) for s in stress]
        root = math.sqrt(3.0)
        parts = [
            (0.5 * root) * (exact[0] - exact[1]),
            0.5 * (exact[0] + exact[1]) - exact[2],
            root * exact[3],
            root * exact[4],
            root * exact[5],
        ]
        for s in range(cases // 2 + 1):
            form = None
            for part in parts:
                term = part * (part if s == 0 else pltpu.roll(part, cases - s, 0))
                form = term if form is None else form + term
            upper = form.astype(BF16)
            lower = (form - upper.astype(F32)).astype(BF16)
            at, apart = (s * cases, main) if s < cases // 2 else (3 * main, cases)
            rhs[at : at + cases, :] = upper
            rhs[at + apart : at + apart + cases, :] = lower
            rhs[at + 2 * apart : at + 2 * apart + cases, :] = upper

    def reduce(step, rhs, sums):
        _, columns, _, slot = step
        mises2 = jnp.dot(pairs[...], rhs[...], preferred_element_type=F32)
        hydro = jnp.dot(linear[:, : 3 * cases], sums[...], preferred_element_type=F32)
        tops = (jnp.max(mises2, axis=0, keepdims=True), jnp.max(hydro, axis=0, keepdims=True), jnp.min(hydro, axis=0, keepdims=True))
        for half, y in enumerate(columns):
            for into, row in zip((best, high, low), tops):
                into[slot, y : y + 1, :] = row[:, half * TILE : (half + 1) * TILE]

    return build, reduce


def run_steps(build, reduce, steps, used, rhs, sums):
    for buffer in rhs:
        buffer[used:, :] = jnp.zeros((buffer.shape[0] - used, 2 * TILE), BF16)
    build(steps[0], rhs[0], sums[0])
    for n, step in enumerate(steps):
        if n + 1 < len(steps):
            build(steps[n + 1], rhs[(n + 1) % 2], sums[(n + 1) % 2])
        reduce(step, rhs[n % 2], sums[n % 2])


def inner_kernel(slab, tiles, ends, pairs, linear, moduli, best, high, low, rhs_even, rhs_odd, sums_even, sums_odd):
    p = lax.axis_index("bx")
    cols = ROWS // 2
    build, reduce = column_steps(slab, tiles, ends, pairs, linear, moduli, None, None, best, high, low)
    steps = [(p, (y, y + 1), False, 0) for y in range(1, cols - 1, 2)]
    run_steps(build, reduce, steps, 3 * (tiles.shape[3] // 2 + 1) * tiles.shape[3], (rhs_even, rhs_odd), (sums_even, sums_odd))


def outer_kernel(
    slab, tiles, ends, pairs, linear, moduli, face_x, face_y, inner_best, inner_high, inner_low,
    peak, spread, rhs_even, rhs_odd, sums_even, sums_odd, best, high, low,
):
    p = lax.axis_index("bx")
    cols = ROWS // 2
    build, reduce = column_steps(slab, tiles, ends, pairs, linear, moduli, face_x, face_y, best, high, low)
    steps = [(p, (0, cols - 1), False, 0)] + [(1 - p, (y, y + 1), True, 1) for y in range(0, cols, 2)]
    run_steps(build, reduce, steps, 3 * (tiles.shape[3] // 2 + 1) * tiles.shape[3], (rhs_even, rhs_odd), (sums_even, sums_odd))
    for into, inner in ((best, inner_best), (high, inner_high), (low, inner_low)):
        into[0, 1 : cols - 1, :] = inner[0, 1 : cols - 1, :]
    for slot, parity in ((0, p), (1, 1 - p)):
        vm = jnp.sqrt(jnp.maximum(best[slot], 0.0))
        hyd = high[slot] * (1.0 / 3.0) - low[slot] * (1.0 / 3.0)
        for i in range(TILE // slab):
            cut = slice(i * slab, (i + 1) * slab)
            peak[2 * i + parity] = vm[:, cut]
            spread[2 * i + parity] = hyd[:, cut]


def tiled_shards(displacements, material_ids, lame, slab_bounds, load_history):
    per, _, rows, cols, depth = displacements.shape
    groups = lax.axis_size("case")
    order = list(EXCHANGE_ORDER)
    slab = depth // groups
    cases = per * groups
    steps = load_history.shape[0]
    channels = per * 3
    vmem = pl.BlockSpec(memory_space=pltpu.VMEM)
    main, picks = pair_table(cases, order)
    total = 3 * main + TILE
    params = pltpu.CompilerParams(vmem_limit_bytes=16 * 1024 * 1024)
    like = jax.ShapeDtypeStruct
    with jax.named_scope("prepare"):
        pairs, linear, moduli = pl.pallas_call(
            functools.partial(prepare_kernel, main, slab),
            out_shape=(like((steps, total), BF16), like((steps, TILE), BF16), like((2, ROWS, TILE), F32)),
            in_specs=[vmem] * 5,
            out_specs=(vmem,) * 3,
            compiler_params=params,
        )(
            load_history.T,
            jnp.asarray(picks, BF16),
            material_ids.reshape(rows * cols, depth),
            lame,
            slab_bounds,
        )
    lines = channels * ROWS + cols
    with jax.named_scope("pack"):
        packed = pl.pallas_call(
            functools.partial(pack_kernel, slab, order),
            out_shape=like((groups, lines, TILE), BF16),
            in_specs=[vmem],
            out_specs=vmem,
            compiler_params=params,
        )(displacements.reshape(channels * rows * cols, depth))
    got = lax.all_to_all(packed, "case", split_axis=0, concat_axis=0, axis_index_groups=[order], tiled=True)
    with jax.named_scope("gather"):
        tiles, ends, face_x, face_y = pl.pallas_call(
            functools.partial(gather_kernel, slab),
            out_shape=(
                like((3, 2, cols, cases, TILE), F32),
                like((2, cols, groups, TILE), F32),
                like((cols, cases, TILE), BF16),
                like((3, 2, cases, TILE), BF16),
            ),
            in_specs=[vmem],
            out_specs=(vmem,) * 4,
            scratch_shapes=[pltpu.VMEM((groups * lines, TILE), F32)],
            compiler_params=params,
        )(got)
    face_x = lax.ppermute(face_x, "bx", [(0, 1), (1, 0)])
    face_y = lax.ppermute(face_y, "by", [(0, 1), (1, 0)])
    buffers = [pltpu.VMEM((total, 2 * TILE), BF16)] * 2 + [pltpu.VMEM((3 * cases, 2 * TILE), BF16)] * 2
    with jax.named_scope("inner"):
        inner = pl.pallas_call(
            functools.partial(inner_kernel, slab),
            out_shape=(like((1, cols, TILE), F32),) * 3,
            in_specs=[vmem] * 5,
            out_specs=(vmem,) * 3,
            scratch_shapes=buffers,
            compiler_params=params,
        )(tiles, ends, pairs, linear, moduli)
    with jax.named_scope("outer"):
        return pl.pallas_call(
            functools.partial(outer_kernel, slab),
            out_shape=(like((rows, cols, slab), F32),) * 2,
            in_specs=[vmem] * 10,
            out_specs=(vmem,) * 2,
            scratch_shapes=buffers + [pltpu.VMEM((2, cols, TILE), F32)] * 3,
            compiler_params=params,
        )(tiles, ends, pairs, linear, moduli, face_x, face_y, *inner)


def fits_tiles(mesh, displacements, load_history):
    groups, bricks_x, bricks_y = (mesh.shape[a] for a in ("case", "bx", "by"))
    cases, comps, rows, cols, depth = displacements.shape
    if bricks_x != 2 or bricks_y != 2 or cases % groups or depth % groups:
        return False
    per, rows, cols, slab = cases // groups, rows // 2, cols // 2, depth // groups
    return (
        groups == len(EXCHANGE_ORDER) and per == 2 and comps == 3 and rows == 8 and cols == 8 and slab == 32
        and load_history.shape[0] % 16 == 0
    )


def solution(mesh):
    in_specs = (P("case", None, "bx", "by", None), P("bx", "by", None), P(), P(None, "bx"), P())
    out_specs = (P("bx", "by", "case"), P("bx", "by", "case"))

    def run(displacements, material_ids, lame, slab_bounds, load_history):
        body = tiled_shards if fits_tiles(mesh, displacements, load_history) else shards
        placed = jax.shard_map(body, mesh=mesh, in_specs=in_specs, out_specs=out_specs, check_vma=False)
        return placed(displacements, material_ids, lame, slab_bounds, load_history)

    return run
```

```python
import functools
import math

import jax
import jax.numpy as jnp
import numpy as np
from jax import lax
from jax.experimental import pallas as pl
from jax.experimental.pallas import tpu as pltpu
from jax.sharding import PartitionSpec as P


def extended_2(cells, sides, width):
    for axis, dim in sides:
        count = lax.axis_size(axis)
        ends = count - 1
        head = lax.slice_in_dim(cells, 0, width, axis=dim)
        tail = lax.slice_in_dim(cells, cells.shape[dim] - width, cells.shape[dim], axis=dim)
        cells = jnp.concatenate(
            [
                lax.ppermute(tail, axis, [(i, (i + 1) % count) for i in range(ends)]),
                cells,
                lax.ppermute(head, axis, [((i + 1) % count, i) for i in range(ends)]),
            ],
            axis=dim,
        )
    return cells


def derivative(extended, comp, along):
    field = extended[..., comp, :, :, :]
    if along == 0:
        return 0.5 * (field[..., 2:, 1:-1, 1:-1] - field[..., :-2, 1:-1, 1:-1])
    if along == 1:
        return 0.5 * (field[..., 1:-1, 2:, 1:-1] - field[..., 1:-1, :-2, 1:-1])
    return 0.5 * (field[..., 1:-1, 1:-1, 2:] - field[..., 1:-1, 1:-1, :-2])


def combine_stress(grads, shear_mod, lame_first, weight):
    trace = grads[0][0] + grads[1][1] + grads[2][2]
    normal_x = (lame_first * trace + 2.0 * shear_mod * grads[0][0]) * weight
    normal_y = (lame_first * trace + 2.0 * shear_mod * grads[1][1]) * weight
    normal_z = (lame_first * trace + 2.0 * shear_mod * grads[2][2]) * weight
    shear_xy = shear_mod * (grads[0][1] + grads[1][0]) * weight
    shear_yz = shear_mod * (grads[1][2] + grads[2][1]) * weight
    shear_zx = shear_mod * (grads[2][0] + grads[0][2]) * weight
    return jnp.stack([normal_x, normal_y, normal_z, shear_xy, shear_yz, shear_zx], axis=-4)


def stress_field(extended, shear_mod, lame_first, weight):
    extended = extended.astype(jnp.float32)
    grads = [[derivative(extended, comp, along) for along in range(3)] for comp in range(3)]
    return combine_stress(grads, shear_mod, lame_first, weight)


def material_moduli(material_ids, lame):
    shear_mod = jnp.zeros(material_ids.shape, jnp.float32)
    lame_first = jnp.zeros(material_ids.shape, jnp.float32)
    for material in range(lame.shape[1]):
        picked = material_ids == material
        shear_mod = jnp.where(picked, lame[0, material], shear_mod)
        lame_first = jnp.where(picked, lame[1, material], lame_first)
    return (shear_mod, lame_first)


def histories(load_history, blocks):
    cases, comps, rows, cols, single, slab = blocks.shape
    flat = blocks.reshape(cases, comps * rows * cols * single * slab)
    total = load_history.shape[0]
    step_len = min(128, total)
    top_mises = None
    for begin in range(0, total, step_len):
        factors = load_history[begin : begin + step_len]
        history = jnp.dot(factors, flat, preferred_element_type=jnp.float32).reshape(
            step_len, comps, -1
        )
        diff_one = history[:, 0] - history[:, 1]
        diff_two = history[:, 1] - history[:, 2]
        diff_three = history[:, 2] - history[:, 0]
        mises2 = 0.5 * (diff_one * diff_one + diff_two * diff_two + diff_three * diff_three)
        mises2 = mises2 + 3.0 * (
            history[:, 3] * history[:, 3]
            + history[:, 4] * history[:, 4]
            + history[:, 5] * history[:, 5]
        )
        hydro = (history[:, 0] + history[:, 1] + history[:, 2]) / 3.0
        block_mises = jnp.max(mises2, axis=0)
        block_high = jnp.max(hydro, axis=0)
        block_low = jnp.min(hydro, axis=0)
        if top_mises is None:
            top_mises, high, low = (block_mises, block_high, block_low)
        else:
            top_mises = jnp.maximum(top_mises, block_mises)
            high = jnp.maximum(high, block_high)
            low = jnp.minimum(low, block_low)
    peak = jnp.sqrt(top_mises).reshape(rows, cols, slab)
    spread = (high - low).reshape(rows, cols, slab)
    return (peak, spread)


def shards(displacements, material_ids, lame, slab_bounds, load_history):
    cases_here = displacements.shape[0]
    rows = displacements.shape[2]
    cols = displacements.shape[3]
    depth = displacements.shape[4]
    groups = lax.axis_size("case")
    slab = depth // groups
    shear_mod, lame_first = material_moduli(material_ids, lame)
    levels = jnp.arange(depth, dtype=jnp.int32)
    inside = (slab_bounds[0][:, None] <= levels[None, :]) & (
        levels[None, :] < slab_bounds[1][:, None]
    )
    weight = inside.astype(jnp.float32)[:, None, :]
    bordered = extended_2(displacements, (("bx", 2), ("by", 3)), 1)
    extended = jnp.pad(bordered, ((0, 0), (0, 0), (0, 0), (0, 0), (1, 1)))
    stress = stress_field(extended, shear_mod, lame_first, weight).astype(jnp.bfloat16)
    blocks = stress.reshape(cases_here, 6, rows, cols, groups, slab)
    peak, spread = histories(
        load_history, lax.all_to_all(blocks, "case", split_axis=4, concat_axis=0, tiled=True)
    )
    return (peak, spread)


F32 = jnp.float32
BF16 = jnp.bfloat16
TILE = 128
ROWS = 16
EXCHANGE_ORDER = (5, 6, 4, 1, 7, 3, 2, 0)


def pair_table(cases, order):
    groups = len(order)
    per = cases // groups
    place = np.array([order[j % groups] * per + j // groups for j in range(cases)])
    half = cases // 2
    main = half * cases
    first = np.zeros((cases, main + TILE), np.float32)
    second = np.zeros((cases, main + TILE), np.float32)
    plain = np.zeros((cases, TILE), np.float32)
    for j in range(cases):
        for s in range(half):
            first[place[j], s * cases + j] = 1.0
            second[place[(j + s) % cases], s * cases + j] = 2.0 if s else 1.0
        for copy in range(3):
            first[place[j], main + copy * cases + j] = 1.0
            second[place[(j + half) % cases], main + copy * cases + j] = 1.0
            plain[place[j], copy * cases + j] = 1.0
    return main, np.concatenate([first, second, plain], axis=1)


def prepare_kernel(main, slab, loads, picks, ids, lame, bounds, pairs, linear, moduli):
    over = (((0,), (0,)), ((), ()))
    table = loads[...]
    factor = lax.dot_general(table, picks[...], over, preferred_element_type=F32)
    wide = main + TILE
    prod = factor[:, :wide] * factor[:, wide : 2 * wide]
    most = prod[:, :main]
    high = most.astype(BF16)
    pairs[:, :main] = high
    pairs[:, main : 2 * main] = high
    pairs[:, 2 * main : 3 * main] = (most - high.astype(F32)).astype(BF16)
    last = prod[:, main:]
    high = last.astype(BF16).astype(F32)
    col = lax.broadcasted_iota(jnp.int32, last.shape, 1)
    pairs[:, 3 * main :] = jnp.where(col < 2 * table.shape[0], high, last - high).astype(BF16)
    linear[...] = factor[:, 2 * wide :].astype(BF16)
    group = lax.axis_index("case")
    rows, depth = ids.shape
    cols = ROWS // 2
    depth_first = pltpu.roll(ids[...], (depth - group * slab) % depth, 1)[:, :TILE]
    lane = lax.broadcasted_iota(jnp.int32, (ROWS, TILE), 1)
    row = lax.broadcasted_iota(jnp.int32, (ROWS, TILE), 0)
    level = group * slab + lane % slab
    tile = jnp.zeros((ROWS, TILE), jnp.int32)
    lower = jnp.zeros((ROWS, TILE), jnp.int32)
    upper = jnp.zeros((ROWS, TILE), jnp.int32)
    for i in range(TILE // slab):
        here = lane // slab == i
        piece = depth_first[i * ROWS : (i + 1) * ROWS]
        tile = jnp.where(here, piece if i == 0 else pltpu.roll(piece, i * slab, 1), tile)
        for p in range(2):
            spot = here & (row // cols == p)
            lower = jnp.where(spot, bounds[0:1, 2 * i + p : 2 * i + p + 1], lower)
            upper = jnp.where(spot, bounds[1:2, 2 * i + p : 2 * i + p + 1], upper)
    weight = jnp.where((lower <= level) & (level < upper), 1.0, 0.0).astype(F32)
    for part in range(2):
        value = jnp.zeros((ROWS, TILE), F32)
        for material in range(lame.shape[1]):
            value = jnp.where(tile == material, lame[part : part + 1, material : material + 1], value)
        moduli[part] = value * weight


def pack_field(slab, order, arrivals, field, out):
    depth = field.shape[1]
    quarters = TILE // slab
    height = quarters * ROWS
    channels = field.shape[0] // height
    parts = []
    for m in range(channels):
        parts.append([field[m * height + i * ROWS : m * height + (i + 1) * ROWS, :].astype(F32) for i in range(quarters)])
        for at, g in enumerate(order):
            pieces = [piece[:, g * slab : (g + 1) * slab] for piece in parts[m]]
            out[at, m * ROWS : (m + 1) * ROWS, :] = jnp.concatenate(pieces, axis=1).astype(BF16)
    lane = lax.broadcasted_iota(jnp.int32, (ROWS, depth), 1)
    ends = []
    for i in range(quarters):
        mixed = jnp.zeros((ROWS, depth), F32)
        for m in range(channels):
            below = pltpu.roll(parts[m][i], 2 * m + 1, 1)
            above = pltpu.roll(parts[m][i], (2 * m + 1 - slab) % depth, 1)
            mixed = jnp.where((lane % slab == 2 * m) & (lane >= slab), below, mixed)
            mixed = jnp.where((lane % slab == 2 * m + 1) & (lane < depth - slab), above, mixed)
        ends.append(mixed)
    cols = ROWS // 2
    for at, g in enumerate(order):
        short = slice(g * slab, g * slab + slab // 2)
        outer = [end[p * cols : (p + 1) * cols, short] for p in range(2) for end in ends]
        out[at, channels * ROWS :, :] = jnp.concatenate(outer, axis=1).astype(BF16)


def front_kernel(slab, order, source, *rest):
    count = (len(rest) - 4) // 2
    far, out, near = rest[:count], rest[count], rest[count + 1 : 2 * count + 1]
    field, arrived, landed = rest[2 * count + 1 :]
    height = TILE // slab * ROWS
    arrivals = []
    for m in range(field.shape[0] // height):
        rows = pl.ds(m * height, height)
        arrivals.append(pltpu.make_async_copy(source.at[rows, :], field.at[rows, :], arrived.at[m]))
    fetches = [pltpu.make_async_copy(a, b, landed.at[n]) for n, (a, b) in enumerate(zip(far, near))]
    for copy in arrivals + fetches:
        copy.start()
    for copy in arrivals:
        copy.wait()
    pack_field(slab, order, arrivals, field, out)
    for copy in fetches:
        copy.wait()


def gather_kernel(slab, got, tiles, ends, face_x, face_y, plain):
    groups, rows, _ = got.shape
    quarters = TILE // slab
    per = rows // ROWS // 3
    cases = per * groups
    cols = ROWS // 2
    brick_x = lax.axis_index("bx")
    brick_y = lax.axis_index("by")
    for g in range(groups):
        plain[g * rows : (g + 1) * rows, :] = got[g].astype(F32)

    def gather(row):
        return plain[pl.ds(row, groups, stride=rows), :]

    def column(k, p, y):
        return jnp.concatenate([gather((c * 3 + k) * ROWS + p * cols + y) for c in range(per)], axis=0)

    lane = lax.broadcasted_iota(jnp.int32, (cases, TILE), 1)
    for y in range(cols):
        packed = jnp.zeros((cases, TILE), F32)
        for k in range(3):
            even, odd = column(k, 0, y), column(k, 1, y)
            tiles[k, 0, y] = even
            tiles[k, 1, y] = odd
            even = pltpu.roll(even, k * slab, 1) if k else even
            odd = pltpu.roll(odd, (k + 1 - quarters) * slab % TILE, 1)
            packed = jnp.where(lane // slab == k, jnp.where(brick_x == 0, odd, even), packed)
            if y == 0:
                firsts = (tiles[k, 0, 0], tiles[k, 1, 0])
                for p in range(2):
                    face_y[k, p] = firsts[p].astype(BF16)
            if y == cols - 1:
                for p in range(2):
                    face_y[k, p] = jnp.where(brick_y == 0, tiles[k, p, y], face_y[k, p].astype(F32)).astype(BF16)
        face_x[y] = packed.astype(BF16)
        outer = gather(3 * per * ROWS + y)
        for p in range(2):
            spaced = jnp.zeros((groups, TILE), F32)
            for i in range(quarters):
                moved = pltpu.roll(outer, (i * slab - (p * quarters + i) * (slab // 2)) % TILE, 1)
                spaced = jnp.where(lane[:groups] // slab == i, moved, spaced)
            ends[p, y] = spaced


def column_steps(slab, tiles, ends, pairs, linear, moduli, face_x, face_y, best, high, low):
    cases = tiles.shape[3]
    groups = ends.shape[2]
    per = cases // groups
    quarters = TILE // slab
    cols = ROWS // 2
    main = cases // 2 * cases
    wide = lax.broadcasted_iota(jnp.int32, (cases, TILE), 1)
    lower_y = lax.axis_index("by") == 1

    def both(pieces):
        return jnp.concatenate(pieces, axis=0)

    def stress_of(p, y, beside):
        last = jnp.where(p == 0, 0, quarters - 1)
        at_edge = wide // slab == last
        sign = jnp.where(p == 0, 0.5, -0.5).astype(F32)
        grads = []
        for k in range(3):
            mine = tiles[k, p, y]
            other = tiles[k, 1 - p, y]
            shifted = pltpu.roll(other, jnp.where(p == 0, slab, TILE - slab), 1)
            if beside:
                edge = pltpu.roll(face_x[y].astype(F32), lax.rem((last - k) * slab + TILE, TILE), 1)
            else:
                edge = jnp.zeros((cases, TILE), F32)
            grad_x = sign * (other - jnp.where(at_edge, edge, shifted))
            before = tiles[k, p, y - 1] if y else jnp.where(lower_y, face_y[k, p].astype(F32), 0.0)
            after = tiles[k, p, y + 1] if y + 1 < cols else jnp.where(lower_y, 0.0, face_y[k, p].astype(F32))
            outside = ends[p, y]
            below = both([pltpu.roll(outside, -2 * (c * 3 + k) % TILE, 1) for c in range(per)])
            above = both([pltpu.roll(outside, (slab - 2 - 2 * (c * 3 + k)) % TILE, 1) for c in range(per)])
            below = jnp.where(wide % slab == 0, below, pltpu.roll(mine, 1, 1))
            above = jnp.where(wide % slab == slab - 1, above, pltpu.roll(mine, TILE - 1, 1))
            grads.append((grad_x, 0.5 * (after - before), 0.5 * (above - below)))
        shear = moduli[0, pl.ds(p * cols + y, 1), :]
        first = moduli[1, pl.ds(p * cols + y, 1), :]
        volume = first * (grads[0][0] + grads[1][1] + grads[2][2])
        twice = 2.0 * shear
        return [
            volume + twice * grads[0][0],
            volume + twice * grads[1][1],
            volume + twice * grads[2][2],
            shear * (grads[0][1] + grads[1][0]),
            shear * (grads[1][2] + grads[2][1]),
            shear * (grads[2][0] + grads[0][2]),
        ]

    def build(step, rhs, sums):
        p, columns, beside, _ = step
        stack = [stress_of(p, y, beside) for y in columns]
        stress = [jnp.concatenate([stack[0][n], stack[1][n]], axis=1).astype(BF16) for n in range(6)]
        for n in range(3):
            sums[n * cases : (n + 1) * cases, :] = stress[n]
        exact = [s.astype(F32) for s in stress]
        root = math.sqrt(3.0)
        parts = [
            (0.5 * root) * (exact[0] - exact[1]),
            0.5 * (exact[0] + exact[1]) - exact[2],
            root * exact[3],
            root * exact[4],
            root * exact[5],
        ]
        for s in range(cases // 2 + 1):
            form = None
            for part in parts:
                term = part * (part if s == 0 else pltpu.roll(part, cases - s, 0))
                form = term if form is None else form + term
            upper = form.astype(BF16)
            lower = (form - upper.astype(F32)).astype(BF16)
            at, apart = (s * cases, main) if s < cases // 2 else (3 * main, cases)
            rhs[at : at + cases, :] = upper
            rhs[at + apart : at + apart + cases, :] = lower
            rhs[at + 2 * apart : at + 2 * apart + cases, :] = upper

    def reduce(step, rhs, sums):
        _, columns, _, slot = step
        mises2 = jnp.dot(pairs[...], rhs[...], preferred_element_type=F32)
        hydro = jnp.dot(linear[:, : 3 * cases], sums[...], preferred_element_type=F32)
        tops = (jnp.max(mises2, axis=0, keepdims=True), jnp.max(hydro, axis=0, keepdims=True), jnp.min(hydro, axis=0, keepdims=True))
        for half, y in enumerate(columns):
            for into, row in zip((best, high, low), tops):
                into[slot, y : y + 1, :] = row[:, half * TILE : (half + 1) * TILE]

    return build, reduce


def run_steps(build, reduce, steps, used, rhs, sums):
    for buffer in rhs:
        buffer[used:, :] = jnp.zeros((buffer.shape[0] - used, 2 * TILE), BF16)
    build(steps[0], rhs[0], sums[0])
    for n, step in enumerate(steps):
        if n + 1 < len(steps):
            build(steps[n + 1], rhs[(n + 1) % 2], sums[(n + 1) % 2])
        reduce(step, rhs[n % 2], sums[n % 2])


def inner_kernel(slab, tiles, ends, pairs, linear, moduli, best, high, low, rhs_even, rhs_odd, sums_even, sums_odd):
    p = lax.axis_index("bx")
    cols = ROWS // 2
    build, reduce = column_steps(slab, tiles, ends, pairs, linear, moduli, None, None, best, high, low)
    steps = [(p, (y, y + 1), False, 0) for y in range(1, cols - 1, 2)]
    run_steps(build, reduce, steps, 3 * (tiles.shape[3] // 2 + 1) * tiles.shape[3], (rhs_even, rhs_odd), (sums_even, sums_odd))


def outer_kernel(
    slab, tiles, ends, pairs, linear, moduli, face_x, face_y, inner_best, inner_high, inner_low,
    peak, spread, rhs_even, rhs_odd, sums_even, sums_odd, best, high, low,
):
    p = lax.axis_index("bx")
    cols = ROWS // 2
    build, reduce = column_steps(slab, tiles, ends, pairs, linear, moduli, face_x, face_y, best, high, low)
    steps = [(p, (0, cols - 1), False, 0)] + [(1 - p, (y, y + 1), True, 1) for y in range(0, cols, 2)]
    run_steps(build, reduce, steps, 3 * (tiles.shape[3] // 2 + 1) * tiles.shape[3], (rhs_even, rhs_odd), (sums_even, sums_odd))
    for into, inner in ((best, inner_best), (high, inner_high), (low, inner_low)):
        into[0, 1 : cols - 1, :] = inner[0, 1 : cols - 1, :]
    for slot, parity in ((0, p), (1, 1 - p)):
        vm = jnp.sqrt(jnp.maximum(best[slot], 0.0))
        hyd = high[slot] * (1.0 / 3.0) - low[slot] * (1.0 / 3.0)
        for i in range(TILE // slab):
            cut = slice(i * slab, (i + 1) * slab)
            peak[2 * i + parity] = vm[:, cut]
            spread[2 * i + parity] = hyd[:, cut]


def tiled_shards(displacements, material_ids, lame, slab_bounds, load_history):
    per, _, rows, cols, depth = displacements.shape
    groups = lax.axis_size("case")
    order = list(EXCHANGE_ORDER)
    slab = depth // groups
    cases = per * groups
    steps = load_history.shape[0]
    channels = per * 3
    vmem = pl.BlockSpec(memory_space=pltpu.VMEM)
    main, picks = pair_table(cases, order)
    total = 3 * main + TILE
    params = pltpu.CompilerParams(vmem_limit_bytes=16 * 1024 * 1024)
    like = jax.ShapeDtypeStruct
    lines = channels * ROWS + cols
    far = [
        pltpu.with_memory_space_constraint(a, pltpu.HBM)
        for a in (
            displacements.reshape(channels * rows * cols, depth),
            load_history.T,
            jnp.asarray(picks, BF16),
            material_ids.reshape(rows * cols, depth),
            lame,
            slab_bounds,
        )
    ]
    with jax.named_scope("front"):
        packed, *near = pl.pallas_call(
            functools.partial(front_kernel, slab, order),
            out_shape=(pltpu.VMEM((groups, lines, TILE), BF16),) + tuple(pltpu.VMEM(a.shape, a.dtype) for a in far[1:]),
            in_specs=[pl.BlockSpec(memory_space=pltpu.HBM)] * len(far),
            out_specs=(vmem,) * len(far),
            scratch_shapes=[
                pltpu.VMEM(far[0].shape, BF16),
                pltpu.SemaphoreType.DMA((channels,)),
                pltpu.SemaphoreType.DMA((len(far) - 1,)),
            ],
            compiler_params=params,
        )(*far)
    with jax.named_scope("prepare"):
        pairs, linear, moduli = pl.pallas_call(
            functools.partial(prepare_kernel, main, slab),
            out_shape=(like((steps, total), BF16), like((steps, TILE), BF16), like((2, ROWS, TILE), F32)),
            in_specs=[vmem] * len(near),
            out_specs=(vmem,) * 3,
            compiler_params=params,
        )(*near)
    got = lax.all_to_all(packed, "case", split_axis=0, concat_axis=0, axis_index_groups=[order], tiled=True)
    with jax.named_scope("gather"):
        tiles, ends, face_x, face_y = pl.pallas_call(
            functools.partial(gather_kernel, slab),
            out_shape=(
                like((3, 2, cols, cases, TILE), F32),
                like((2, cols, groups, TILE), F32),
                like((cols, cases, TILE), BF16),
                like((3, 2, cases, TILE), BF16),
            ),
            in_specs=[vmem],
            out_specs=(vmem,) * 4,
            scratch_shapes=[pltpu.VMEM((groups * lines, TILE), F32)],
            compiler_params=params,
        )(got)
    face_x = lax.ppermute(face_x, "bx", [(0, 1), (1, 0)])
    face_y = lax.ppermute(face_y, "by", [(0, 1), (1, 0)])
    buffers = [pltpu.VMEM((total, 2 * TILE), BF16)] * 2 + [pltpu.VMEM((3 * cases, 2 * TILE), BF16)] * 2
    with jax.named_scope("inner"):
        inner = pl.pallas_call(
            functools.partial(inner_kernel, slab),
            out_shape=(like((1, cols, TILE), F32),) * 3,
            in_specs=[vmem] * 5,
            out_specs=(vmem,) * 3,
            scratch_shapes=buffers,
            compiler_params=params,
        )(tiles, ends, pairs, linear, moduli)
    with jax.named_scope("outer"):
        return pl.pallas_call(
            functools.partial(outer_kernel, slab),
            out_shape=(like((rows, cols, slab), F32),) * 2,
            in_specs=[vmem] * 10,
            out_specs=(vmem,) * 2,
            scratch_shapes=buffers + [pltpu.VMEM((2, cols, TILE), F32)] * 3,
            compiler_params=params,
        )(tiles, ends, pairs, linear, moduli, face_x, face_y, *inner)


def fits_tiles(mesh, displacements, load_history):
    groups, bricks_x, bricks_y = (mesh.shape[a] for a in ("case", "bx", "by"))
    cases, comps, rows, cols, depth = displacements.shape
    if bricks_x != 2 or bricks_y != 2 or cases % groups or depth % groups:
        return False
    per, rows, cols, slab = cases // groups, rows // 2, cols // 2, depth // groups
    return (
        groups == len(EXCHANGE_ORDER) and per == 2 and comps == 3 and rows == 8 and cols == 8 and slab == 32
        and load_history.shape[0] % 16 == 0
    )


def solution(mesh):
    in_specs = (P("case", None, "bx", "by", None), P("bx", "by", None), P(), P(None, "bx"), P())
    out_specs = (P("bx", "by", "case"), P("bx", "by", "case"))

    def run(displacements, material_ids, lame, slab_bounds, load_history):
        body = tiled_shards if fits_tiles(mesh, displacements, load_history) else shards
        placed = jax.shard_map(body, mesh=mesh, in_specs=in_specs, out_specs=out_specs, check_vma=False)
        return placed(displacements, material_ids, lame, slab_bounds, load_history)

    return run
```

```python
import functools
import math

import jax
import jax.numpy as jnp
import numpy as np
from jax import lax
from jax.experimental import pallas as pl
from jax.experimental.pallas import tpu as pltpu
from jax.sharding import PartitionSpec as P


def extended_2(cells, sides, width):
    for axis, dim in sides:
        count = lax.axis_size(axis)
        ends = count - 1
        head = lax.slice_in_dim(cells, 0, width, axis=dim)
        tail = lax.slice_in_dim(cells, cells.shape[dim] - width, cells.shape[dim], axis=dim)
        cells = jnp.concatenate(
            [
                lax.ppermute(tail, axis, [(i, (i + 1) % count) for i in range(ends)]),
                cells,
                lax.ppermute(head, axis, [((i + 1) % count, i) for i in range(ends)]),
            ],
            axis=dim,
        )
    return cells


def derivative(extended, comp, along):
    field = extended[..., comp, :, :, :]
    if along == 0:
        return 0.5 * (field[..., 2:, 1:-1, 1:-1] - field[..., :-2, 1:-1, 1:-1])
    if along == 1:
        return 0.5 * (field[..., 1:-1, 2:, 1:-1] - field[..., 1:-1, :-2, 1:-1])
    return 0.5 * (field[..., 1:-1, 1:-1, 2:] - field[..., 1:-1, 1:-1, :-2])


def combine_stress(grads, shear_mod, lame_first, weight):
    trace = grads[0][0] + grads[1][1] + grads[2][2]
    normal_x = (lame_first * trace + 2.0 * shear_mod * grads[0][0]) * weight
    normal_y = (lame_first * trace + 2.0 * shear_mod * grads[1][1]) * weight
    normal_z = (lame_first * trace + 2.0 * shear_mod * grads[2][2]) * weight
    shear_xy = shear_mod * (grads[0][1] + grads[1][0]) * weight
    shear_yz = shear_mod * (grads[1][2] + grads[2][1]) * weight
    shear_zx = shear_mod * (grads[2][0] + grads[0][2]) * weight
    return jnp.stack([normal_x, normal_y, normal_z, shear_xy, shear_yz, shear_zx], axis=-4)


def stress_field(extended, shear_mod, lame_first, weight):
    extended = extended.astype(jnp.float32)
    grads = [[derivative(extended, comp, along) for along in range(3)] for comp in range(3)]
    return combine_stress(grads, shear_mod, lame_first, weight)


def material_moduli(material_ids, lame):
    shear_mod = jnp.zeros(material_ids.shape, jnp.float32)
    lame_first = jnp.zeros(material_ids.shape, jnp.float32)
    for material in range(lame.shape[1]):
        picked = material_ids == material
        shear_mod = jnp.where(picked, lame[0, material], shear_mod)
        lame_first = jnp.where(picked, lame[1, material], lame_first)
    return (shear_mod, lame_first)


def histories(load_history, blocks):
    cases, comps, rows, cols, single, slab = blocks.shape
    flat = blocks.reshape(cases, comps * rows * cols * single * slab)
    total = load_history.shape[0]
    step_len = min(128, total)
    top_mises = None
    for begin in range(0, total, step_len):
        factors = load_history[begin : begin + step_len]
        history = jnp.dot(factors, flat, preferred_element_type=jnp.float32).reshape(
            step_len, comps, -1
        )
        diff_one = history[:, 0] - history[:, 1]
        diff_two = history[:, 1] - history[:, 2]
        diff_three = history[:, 2] - history[:, 0]
        mises2 = 0.5 * (diff_one * diff_one + diff_two * diff_two + diff_three * diff_three)
        mises2 = mises2 + 3.0 * (
            history[:, 3] * history[:, 3]
            + history[:, 4] * history[:, 4]
            + history[:, 5] * history[:, 5]
        )
        hydro = (history[:, 0] + history[:, 1] + history[:, 2]) / 3.0
        block_mises = jnp.max(mises2, axis=0)
        block_high = jnp.max(hydro, axis=0)
        block_low = jnp.min(hydro, axis=0)
        if top_mises is None:
            top_mises, high, low = (block_mises, block_high, block_low)
        else:
            top_mises = jnp.maximum(top_mises, block_mises)
            high = jnp.maximum(high, block_high)
            low = jnp.minimum(low, block_low)
    peak = jnp.sqrt(top_mises).reshape(rows, cols, slab)
    spread = (high - low).reshape(rows, cols, slab)
    return (peak, spread)


def shards(displacements, material_ids, lame, slab_bounds, load_history):
    cases_here = displacements.shape[0]
    rows = displacements.shape[2]
    cols = displacements.shape[3]
    depth = displacements.shape[4]
    groups = lax.axis_size("case")
    slab = depth // groups
    shear_mod, lame_first = material_moduli(material_ids, lame)
    levels = jnp.arange(depth, dtype=jnp.int32)
    inside = (slab_bounds[0][:, None] <= levels[None, :]) & (
        levels[None, :] < slab_bounds[1][:, None]
    )
    weight = inside.astype(jnp.float32)[:, None, :]
    bordered = extended_2(displacements, (("bx", 2), ("by", 3)), 1)
    extended = jnp.pad(bordered, ((0, 0), (0, 0), (0, 0), (0, 0), (1, 1)))
    stress = stress_field(extended, shear_mod, lame_first, weight).astype(jnp.bfloat16)
    blocks = stress.reshape(cases_here, 6, rows, cols, groups, slab)
    peak, spread = histories(
        load_history, lax.all_to_all(blocks, "case", split_axis=4, concat_axis=0, tiled=True)
    )
    return (peak, spread)


F32 = jnp.float32
BF16 = jnp.bfloat16
TILE = 128
ROWS = 16
EXCHANGE_ORDER = (5, 6, 4, 1, 7, 3, 2, 0)


def pair_table(cases, order):
    groups = len(order)
    per = cases // groups
    place = np.array([order[j % groups] * per + j // groups for j in range(cases)])
    half = cases // 2
    main = half * cases
    picks = np.zeros((cases, 2 * main), np.float32)
    for s in range(half):
        for j in range(cases):
            picks[place[j], s * cases + j] = 1.0
            picks[place[(j + s + 1) % cases], main + s * cases + j] = 2.0 if s + 1 < half else 1.0
    return main, picks


def prepare_kernel(main, slab, loads, picks, ids, lame, bounds, pairs, linear, moduli):
    over = (((0,), (0,)), ((), ()))
    cases = loads.shape[0]
    factor = lax.dot_general(loads[...], picks[...], over, preferred_element_type=F32)
    single, other = factor[:, :main], factor[:, main:]
    linear[...] = single[:, :TILE].astype(BF16)
    mixed = single * other
    high = mixed.astype(BF16)
    pairs[:, :main] = high
    pairs[:, main : 2 * main] = high
    pairs[:, 2 * main : 3 * main] = (mixed - high.astype(F32)).astype(BF16)
    square = single[:, :TILE] * single[:, :TILE]
    high = square.astype(BF16).astype(F32)
    col = lax.broadcasted_iota(jnp.int32, square.shape, 1)
    pairs[:, 3 * main :] = jnp.where(col < 2 * cases, high, square - high).astype(BF16)
    group = lax.axis_index("case")
    rows, depth = ids.shape
    cols = ROWS // 2
    depth_first = pltpu.roll(ids[...], (depth - group * slab) % depth, 1)[:, :TILE]
    lane = lax.broadcasted_iota(jnp.int32, (ROWS, TILE), 1)
    row = lax.broadcasted_iota(jnp.int32, (ROWS, TILE), 0)
    level = group * slab + lane % slab
    tile = jnp.zeros((ROWS, TILE), jnp.int32)
    lower = jnp.zeros((ROWS, TILE), jnp.int32)
    upper = jnp.zeros((ROWS, TILE), jnp.int32)
    for i in range(TILE // slab):
        here = lane // slab == i
        piece = depth_first[i * ROWS : (i + 1) * ROWS]
        tile = jnp.where(here, piece if i == 0 else pltpu.roll(piece, i * slab, 1), tile)
        for p in range(2):
            spot = here & (row // cols == p)
            lower = jnp.where(spot, bounds[0:1, 2 * i + p : 2 * i + p + 1], lower)
            upper = jnp.where(spot, bounds[1:2, 2 * i + p : 2 * i + p + 1], upper)
    weight = jnp.where((lower <= level) & (level < upper), 1.0, 0.0).astype(F32)
    for part in range(2):
        value = jnp.zeros((ROWS, TILE), F32)
        for material in range(lame.shape[1]):
            value = jnp.where(tile == material, lame[part : part + 1, material : material + 1], value)
        moduli[part] = value * weight


def pack_field(slab, order, arrivals, field, out):
    depth = field.shape[1]
    quarters = TILE // slab
    height = quarters * ROWS
    channels = field.shape[0] // height
    parts = []
    for m in range(channels):
        parts.append([field[m * height + i * ROWS : m * height + (i + 1) * ROWS, :].astype(F32) for i in range(quarters)])
        for at, g in enumerate(order):
            pieces = [piece[:, g * slab : (g + 1) * slab] for piece in parts[m]]
            out[at, m * ROWS : (m + 1) * ROWS, :] = jnp.concatenate(pieces, axis=1).astype(BF16)
    lane = lax.broadcasted_iota(jnp.int32, (ROWS, depth), 1)
    ends = []
    for i in range(quarters):
        mixed = jnp.zeros((ROWS, depth), F32)
        for m in range(channels):
            below = pltpu.roll(parts[m][i], 2 * m + 1, 1)
            above = pltpu.roll(parts[m][i], (2 * m + 1 - slab) % depth, 1)
            mixed = jnp.where((lane % slab == 2 * m) & (lane >= slab), below, mixed)
            mixed = jnp.where((lane % slab == 2 * m + 1) & (lane < depth - slab), above, mixed)
        ends.append(mixed)
    cols = ROWS // 2
    for at, g in enumerate(order):
        short = slice(g * slab, g * slab + slab // 2)
        outer = [end[p * cols : (p + 1) * cols, short] for p in range(2) for end in ends]
        out[at, channels * ROWS :, :] = jnp.concatenate(outer, axis=1).astype(BF16)


def front_kernel(slab, order, source, *rest):
    count = (len(rest) - 4) // 2
    far, out, near = rest[:count], rest[count], rest[count + 1 : 2 * count + 1]
    field, arrived, landed = rest[2 * count + 1 :]
    height = TILE // slab * ROWS
    arrivals = []
    for m in range(field.shape[0] // height):
        rows = pl.ds(m * height, height)
        arrivals.append(pltpu.make_async_copy(source.at[rows, :], field.at[rows, :], arrived.at[m]))
    fetches = [pltpu.make_async_copy(a, b, landed.at[n]) for n, (a, b) in enumerate(zip(far, near))]
    for copy in arrivals + fetches:
        copy.start()
    for copy in arrivals:
        copy.wait()
    pack_field(slab, order, arrivals, field, out)
    for copy in fetches:
        copy.wait()


def gather_kernel(slab, got, tiles, ends, face_x, face_y, plain):
    groups, rows, _ = got.shape
    quarters = TILE // slab
    per = rows // ROWS // 3
    cases = per * groups
    cols = ROWS // 2
    brick_x = lax.axis_index("bx")
    brick_y = lax.axis_index("by")
    for g in range(groups):
        plain[g * rows : (g + 1) * rows, :] = got[g].astype(F32)

    def gather(row):
        return plain[pl.ds(row, groups, stride=rows), :]

    def column(k, p, y):
        return jnp.concatenate([gather((c * 3 + k) * ROWS + p * cols + y) for c in range(per)], axis=0)

    lane = lax.broadcasted_iota(jnp.int32, (cases, TILE), 1)
    for y in range(cols):
        packed = jnp.zeros((cases, TILE), F32)
        for k in range(3):
            even, odd = column(k, 0, y), column(k, 1, y)
            tiles[k, 0, y] = even
            tiles[k, 1, y] = odd
            even = pltpu.roll(even, k * slab, 1) if k else even
            odd = pltpu.roll(odd, (k + 1 - quarters) * slab % TILE, 1)
            packed = jnp.where(lane // slab == k, jnp.where(brick_x == 0, odd, even), packed)
            if y == 0:
                firsts = (tiles[k, 0, 0], tiles[k, 1, 0])
                for p in range(2):
                    face_y[k, p] = firsts[p].astype(BF16)
            if y == cols - 1:
                for p in range(2):
                    face_y[k, p] = jnp.where(brick_y == 0, tiles[k, p, y], face_y[k, p].astype(F32)).astype(BF16)
        face_x[y] = packed.astype(BF16)
        outer = gather(3 * per * ROWS + y)
        for p in range(2):
            spaced = jnp.zeros((groups, TILE), F32)
            for i in range(quarters):
                moved = pltpu.roll(outer, (i * slab - (p * quarters + i) * (slab // 2)) % TILE, 1)
                spaced = jnp.where(lane[:groups] // slab == i, moved, spaced)
            ends[p, y] = spaced


def column_steps(slab, tiles, ends, pairs, linear, moduli, face_x, face_y, best, high, low):
    cases = tiles.shape[3]
    groups = ends.shape[2]
    per = cases // groups
    quarters = TILE // slab
    cols = ROWS // 2
    main = cases // 2 * cases
    wide = lax.broadcasted_iota(jnp.int32, (cases, TILE), 1)
    lower_y = lax.axis_index("by") == 1

    def both(pieces):
        return jnp.concatenate(pieces, axis=0)

    def stress_of(p, y, beside):
        last = jnp.where(p == 0, 0, quarters - 1)
        at_edge = wide // slab == last
        sign = jnp.where(p == 0, 0.5, -0.5).astype(F32)
        grads = []
        for k in range(3):
            mine = tiles[k, p, y]
            other = tiles[k, 1 - p, y]
            shifted = pltpu.roll(other, jnp.where(p == 0, slab, TILE - slab), 1)
            if beside:
                edge = pltpu.roll(face_x[y].astype(F32), lax.rem((last - k) * slab + TILE, TILE), 1)
            else:
                edge = jnp.zeros((cases, TILE), F32)
            grad_x = sign * (other - jnp.where(at_edge, edge, shifted))
            before = tiles[k, p, y - 1] if y else jnp.where(lower_y, face_y[k, p].astype(F32), 0.0)
            after = tiles[k, p, y + 1] if y + 1 < cols else jnp.where(lower_y, 0.0, face_y[k, p].astype(F32))
            outside = ends[p, y]
            below = both([pltpu.roll(outside, -2 * (c * 3 + k) % TILE, 1) for c in range(per)])
            above = both([pltpu.roll(outside, (slab - 2 - 2 * (c * 3 + k)) % TILE, 1) for c in range(per)])
            below = jnp.where(wide % slab == 0, below, pltpu.roll(mine, 1, 1))
            above = jnp.where(wide % slab == slab - 1, above, pltpu.roll(mine, TILE - 1, 1))
            grads.append((grad_x, 0.5 * (after - before), 0.5 * (above - below)))
        shear = moduli[0, pl.ds(p * cols + y, 1), :]
        first = moduli[1, pl.ds(p * cols + y, 1), :]
        volume = first * (grads[0][0] + grads[1][1] + grads[2][2])
        twice = 2.0 * shear
        return [
            volume + twice * grads[0][0],
            volume + twice * grads[1][1],
            volume + twice * grads[2][2],
            shear * (grads[0][1] + grads[1][0]),
            shear * (grads[1][2] + grads[2][1]),
            shear * (grads[2][0] + grads[0][2]),
        ]

    def build(step, rhs, sums):
        p, columns, beside, _ = step
        stack = [stress_of(p, y, beside) for y in columns]
        stress = [jnp.concatenate([stack[0][n], stack[1][n]], axis=1).astype(BF16) for n in range(6)]
        for n in range(3):
            sums[n * cases : (n + 1) * cases, :] = stress[n]
        exact = [s.astype(F32) for s in stress]
        root = math.sqrt(3.0)
        parts = [
            (0.5 * root) * (exact[0] - exact[1]),
            0.5 * (exact[0] + exact[1]) - exact[2],
            root * exact[3],
            root * exact[4],
            root * exact[5],
        ]
        for s in range(cases // 2 + 1):
            form = None
            for part in parts:
                term = part * (part if s == 0 else pltpu.roll(part, cases - s, 0))
                form = term if form is None else form + term
            upper = form.astype(BF16)
            lower = (form - upper.astype(F32)).astype(BF16)
            at, apart = ((s - 1) * cases, main) if s else (3 * main, cases)
            rhs[at : at + cases, :] = upper
            rhs[at + apart : at + apart + cases, :] = lower
            rhs[at + 2 * apart : at + 2 * apart + cases, :] = upper

    def reduce(step, rhs, sums):
        _, columns, _, slot = step
        mises2 = jnp.dot(pairs[...], rhs[...], preferred_element_type=F32)
        hydro = jnp.dot(linear[:, : 3 * cases], sums[...], preferred_element_type=F32)
        tops = (jnp.max(mises2, axis=0, keepdims=True), jnp.max(hydro, axis=0, keepdims=True), jnp.min(hydro, axis=0, keepdims=True))
        for half, y in enumerate(columns):
            for into, row in zip((best, high, low), tops):
                into[slot, y : y + 1, :] = row[:, half * TILE : (half + 1) * TILE]

    return build, reduce


def run_steps(build, reduce, steps, used, rhs, sums):
    for buffer in rhs:
        buffer[used:, :] = jnp.zeros((buffer.shape[0] - used, 2 * TILE), BF16)
    build(steps[0], rhs[0], sums[0])
    for n, step in enumerate(steps):
        if n + 1 < len(steps):
            build(steps[n + 1], rhs[(n + 1) % 2], sums[(n + 1) % 2])
        reduce(step, rhs[n % 2], sums[n % 2])


def inner_kernel(slab, tiles, ends, pairs, linear, moduli, best, high, low, rhs_even, rhs_odd, sums_even, sums_odd):
    p = lax.axis_index("bx")
    cols = ROWS // 2
    build, reduce = column_steps(slab, tiles, ends, pairs, linear, moduli, None, None, best, high, low)
    steps = [(p, (y, y + 1), False, 0) for y in range(1, cols - 1, 2)]
    run_steps(build, reduce, steps, 3 * (tiles.shape[3] // 2 + 1) * tiles.shape[3], (rhs_even, rhs_odd), (sums_even, sums_odd))


def outer_kernel(
    slab, tiles, ends, pairs, linear, moduli, face_x, face_y, inner_best, inner_high, inner_low,
    peak, spread, rhs_even, rhs_odd, sums_even, sums_odd, best, high, low,
):
    p = lax.axis_index("bx")
    cols = ROWS // 2
    build, reduce = column_steps(slab, tiles, ends, pairs, linear, moduli, face_x, face_y, best, high, low)
    steps = [(p, (0, cols - 1), False, 0)] + [(1 - p, (y, y + 1), True, 1) for y in range(0, cols, 2)]
    run_steps(build, reduce, steps, 3 * (tiles.shape[3] // 2 + 1) * tiles.shape[3], (rhs_even, rhs_odd), (sums_even, sums_odd))
    for into, inner in ((best, inner_best), (high, inner_high), (low, inner_low)):
        into[0, 1 : cols - 1, :] = inner[0, 1 : cols - 1, :]
    for slot, parity in ((0, p), (1, 1 - p)):
        vm = jnp.sqrt(jnp.maximum(best[slot], 0.0))
        hyd = high[slot] * (1.0 / 3.0) - low[slot] * (1.0 / 3.0)
        for i in range(TILE // slab):
            cut = slice(i * slab, (i + 1) * slab)
            peak[2 * i + parity] = vm[:, cut]
            spread[2 * i + parity] = hyd[:, cut]


def tiled_shards(displacements, material_ids, lame, slab_bounds, load_history):
    per, _, rows, cols, depth = displacements.shape
    groups = lax.axis_size("case")
    order = list(EXCHANGE_ORDER)
    slab = depth // groups
    cases = per * groups
    steps = load_history.shape[0]
    channels = per * 3
    vmem = pl.BlockSpec(memory_space=pltpu.VMEM)
    main, picks = pair_table(cases, order)
    total = 3 * main + TILE
    params = pltpu.CompilerParams(vmem_limit_bytes=16 * 1024 * 1024)
    like = jax.ShapeDtypeStruct
    lines = channels * ROWS + cols
    far = [
        pltpu.with_memory_space_constraint(a, pltpu.HBM)
        for a in (
            displacements.reshape(channels * rows * cols, depth),
            load_history.T,
            jnp.asarray(picks, BF16),
            material_ids.reshape(rows * cols, depth),
            lame,
            slab_bounds,
        )
    ]
    with jax.named_scope("front"):
        packed, *near = pl.pallas_call(
            functools.partial(front_kernel, slab, order),
            out_shape=(pltpu.VMEM((groups, lines, TILE), BF16),) + tuple(pltpu.VMEM(a.shape, a.dtype) for a in far[1:]),
            in_specs=[pl.BlockSpec(memory_space=pltpu.HBM)] * len(far),
            out_specs=(vmem,) * len(far),
            scratch_shapes=[
                pltpu.VMEM(far[0].shape, BF16),
                pltpu.SemaphoreType.DMA((channels,)),
                pltpu.SemaphoreType.DMA((len(far) - 1,)),
            ],
            compiler_params=params,
        )(*far)
    with jax.named_scope("prepare"):
        pairs, linear, moduli = pl.pallas_call(
            functools.partial(prepare_kernel, main, slab),
            out_shape=(like((steps, total), BF16), like((steps, TILE), BF16), like((2, ROWS, TILE), F32)),
            in_specs=[vmem] * len(near),
            out_specs=(vmem,) * 3,
            compiler_params=params,
        )(*near)
    got = lax.all_to_all(packed, "case", split_axis=0, concat_axis=0, axis_index_groups=[order], tiled=True)
    with jax.named_scope("gather"):
        tiles, ends, face_x, face_y = pl.pallas_call(
            functools.partial(gather_kernel, slab),
            out_shape=(
                like((3, 2, cols, cases, TILE), F32),
                like((2, cols, groups, TILE), F32),
                like((cols, cases, TILE), BF16),
                like((3, 2, cases, TILE), BF16),
            ),
            in_specs=[vmem],
            out_specs=(vmem,) * 4,
            scratch_shapes=[pltpu.VMEM((groups * lines, TILE), F32)],
            compiler_params=params,
        )(got)
    face_y = lax.ppermute(face_y, "by", [(0, 1), (1, 0)])
    face_x = lax.ppermute(face_x, "bx", [(0, 1), (1, 0)])
    buffers = [pltpu.VMEM((total, 2 * TILE), BF16)] * 2 + [pltpu.VMEM((3 * cases, 2 * TILE), BF16)] * 2
    with jax.named_scope("inner"):
        inner = pl.pallas_call(
            functools.partial(inner_kernel, slab),
            out_shape=(like((1, cols, TILE), F32),) * 3,
            in_specs=[vmem] * 5,
            out_specs=(vmem,) * 3,
            scratch_shapes=buffers,
            compiler_params=params,
        )(tiles, ends, pairs, linear, moduli)
    with jax.named_scope("outer"):
        return pl.pallas_call(
            functools.partial(outer_kernel, slab),
            out_shape=(like((rows, cols, slab), F32),) * 2,
            in_specs=[vmem] * 10,
            out_specs=(vmem,) * 2,
            scratch_shapes=buffers + [pltpu.VMEM((2, cols, TILE), F32)] * 3,
            compiler_params=params,
        )(tiles, ends, pairs, linear, moduli, face_x, face_y, *inner)


def fits_tiles(mesh, displacements, load_history):
    groups, bricks_x, bricks_y = (mesh.shape[a] for a in ("case", "bx", "by"))
    cases, comps, rows, cols, depth = displacements.shape
    if bricks_x != 2 or bricks_y != 2 or cases % groups or depth % groups:
        return False
    per, rows, cols, slab = cases // groups, rows // 2, cols // 2, depth // groups
    return (
        groups == len(EXCHANGE_ORDER) and per == 2 and comps == 3 and rows == 8 and cols == 8 and slab == 32
        and load_history.shape[0] % 16 == 0
    )


def solution(mesh):
    in_specs = (P("case", None, "bx", "by", None), P("bx", "by", None), P(), P(None, "bx"), P())
    out_specs = (P("bx", "by", "case"), P("bx", "by", "case"))

    def run(displacements, material_ids, lame, slab_bounds, load_history):
        body = tiled_shards if fits_tiles(mesh, displacements, load_history) else shards
        placed = jax.shard_map(body, mesh=mesh, in_specs=in_specs, out_specs=out_specs, check_vma=False)
        return placed(displacements, material_ids, lame, slab_bounds, load_history)

    return run
```

```python
import functools
import math

import jax
import jax.numpy as jnp
import numpy as np
from jax import lax
from jax.experimental import pallas as pl
from jax.experimental.pallas import tpu as pltpu
from jax.sharding import PartitionSpec as P


def extended_2(cells, sides, width):
    for axis, dim in sides:
        count = lax.axis_size(axis)
        ends = count - 1
        head = lax.slice_in_dim(cells, 0, width, axis=dim)
        tail = lax.slice_in_dim(cells, cells.shape[dim] - width, cells.shape[dim], axis=dim)
        cells = jnp.concatenate(
            [
                lax.ppermute(tail, axis, [(i, (i + 1) % count) for i in range(ends)]),
                cells,
                lax.ppermute(head, axis, [((i + 1) % count, i) for i in range(ends)]),
            ],
            axis=dim,
        )
    return cells


def derivative(extended, comp, along):
    field = extended[..., comp, :, :, :]
    if along == 0:
        return 0.5 * (field[..., 2:, 1:-1, 1:-1] - field[..., :-2, 1:-1, 1:-1])
    if along == 1:
        return 0.5 * (field[..., 1:-1, 2:, 1:-1] - field[..., 1:-1, :-2, 1:-1])
    return 0.5 * (field[..., 1:-1, 1:-1, 2:] - field[..., 1:-1, 1:-1, :-2])


def combine_stress(grads, shear_mod, lame_first, weight):
    trace = grads[0][0] + grads[1][1] + grads[2][2]
    normal_x = (lame_first * trace + 2.0 * shear_mod * grads[0][0]) * weight
    normal_y = (lame_first * trace + 2.0 * shear_mod * grads[1][1]) * weight
    normal_z = (lame_first * trace + 2.0 * shear_mod * grads[2][2]) * weight
    shear_xy = shear_mod * (grads[0][1] + grads[1][0]) * weight
    shear_yz = shear_mod * (grads[1][2] + grads[2][1]) * weight
    shear_zx = shear_mod * (grads[2][0] + grads[0][2]) * weight
    return jnp.stack([normal_x, normal_y, normal_z, shear_xy, shear_yz, shear_zx], axis=-4)


def stress_field(extended, shear_mod, lame_first, weight):
    extended = extended.astype(jnp.float32)
    grads = [[derivative(extended, comp, along) for along in range(3)] for comp in range(3)]
    return combine_stress(grads, shear_mod, lame_first, weight)


def material_moduli(material_ids, lame):
    shear_mod = jnp.zeros(material_ids.shape, jnp.float32)
    lame_first = jnp.zeros(material_ids.shape, jnp.float32)
    for material in range(lame.shape[1]):
        picked = material_ids == material
        shear_mod = jnp.where(picked, lame[0, material], shear_mod)
        lame_first = jnp.where(picked, lame[1, material], lame_first)
    return (shear_mod, lame_first)


def histories(load_history, blocks):
    cases, comps, rows, cols, single, slab = blocks.shape
    flat = blocks.reshape(cases, comps * rows * cols * single * slab)
    total = load_history.shape[0]
    step_len = min(128, total)
    top_mises = None
    for begin in range(0, total, step_len):
        factors = load_history[begin : begin + step_len]
        history = jnp.dot(factors, flat, preferred_element_type=jnp.float32).reshape(
            step_len, comps, -1
        )
        diff_one = history[:, 0] - history[:, 1]
        diff_two = history[:, 1] - history[:, 2]
        diff_three = history[:, 2] - history[:, 0]
        mises2 = 0.5 * (diff_one * diff_one + diff_two * diff_two + diff_three * diff_three)
        mises2 = mises2 + 3.0 * (
            history[:, 3] * history[:, 3]
            + history[:, 4] * history[:, 4]
            + history[:, 5] * history[:, 5]
        )
        hydro = (history[:, 0] + history[:, 1] + history[:, 2]) / 3.0
        block_mises = jnp.max(mises2, axis=0)
        block_high = jnp.max(hydro, axis=0)
        block_low = jnp.min(hydro, axis=0)
        if top_mises is None:
            top_mises, high, low = (block_mises, block_high, block_low)
        else:
            top_mises = jnp.maximum(top_mises, block_mises)
            high = jnp.maximum(high, block_high)
            low = jnp.minimum(low, block_low)
    peak = jnp.sqrt(top_mises).reshape(rows, cols, slab)
    spread = (high - low).reshape(rows, cols, slab)
    return (peak, spread)


def shards(displacements, material_ids, lame, slab_bounds, load_history):
    cases_here = displacements.shape[0]
    rows = displacements.shape[2]
    cols = displacements.shape[3]
    depth = displacements.shape[4]
    groups = lax.axis_size("case")
    slab = depth // groups
    shear_mod, lame_first = material_moduli(material_ids, lame)
    levels = jnp.arange(depth, dtype=jnp.int32)
    inside = (slab_bounds[0][:, None] <= levels[None, :]) & (
        levels[None, :] < slab_bounds[1][:, None]
    )
    weight = inside.astype(jnp.float32)[:, None, :]
    bordered = extended_2(displacements, (("bx", 2), ("by", 3)), 1)
    extended = jnp.pad(bordered, ((0, 0), (0, 0), (0, 0), (0, 0), (1, 1)))
    stress = stress_field(extended, shear_mod, lame_first, weight).astype(jnp.bfloat16)
    blocks = stress.reshape(cases_here, 6, rows, cols, groups, slab)
    peak, spread = histories(
        load_history, lax.all_to_all(blocks, "case", split_axis=4, concat_axis=0, tiled=True)
    )
    return (peak, spread)


F32 = jnp.float32
BF16 = jnp.bfloat16
TILE = 128
ROWS = 16
EXCHANGE_ORDER = (5, 6, 4, 1, 7, 3, 2, 0)


def pair_table(cases, order):
    groups = len(order)
    per = cases // groups
    place = np.array([order[j % groups] * per + j // groups for j in range(cases)])
    half = cases // 2
    main = half * cases
    picks = np.zeros((cases, 2 * main), np.float32)
    for s in range(half):
        for j in range(cases):
            picks[place[j], s * cases + j] = 1.0
            picks[place[(j + s + 1) % cases], main + s * cases + j] = 2.0 if s + 1 < half else 1.0
    return main, picks


def prepare_kernel(main, slab, loads, picks, ids, lame, bounds, pairs, linear, moduli):
    over = (((0,), (0,)), ((), ()))
    cases = loads.shape[0]
    factor = lax.dot_general(loads[...], picks[...], over, preferred_element_type=F32)
    single, other = factor[:, :main], factor[:, main:]
    linear[...] = single[:, :TILE].astype(BF16)
    mixed = single * other
    high = mixed.astype(BF16)
    pairs[:, :main] = high
    pairs[:, main : 2 * main] = high
    pairs[:, 2 * main : 3 * main] = (mixed - high.astype(F32)).astype(BF16)
    square = single[:, :TILE] * single[:, :TILE]
    high = square.astype(BF16).astype(F32)
    col = lax.broadcasted_iota(jnp.int32, square.shape, 1)
    pairs[:, 3 * main :] = jnp.where(col < 2 * cases, high, square - high).astype(BF16)
    group = lax.axis_index("case")
    rows, depth = ids.shape
    cols = ROWS // 2
    depth_first = pltpu.roll(ids[...], (depth - group * slab) % depth, 1)[:, :TILE]
    lane = lax.broadcasted_iota(jnp.int32, (ROWS, TILE), 1)
    row = lax.broadcasted_iota(jnp.int32, (ROWS, TILE), 0)
    level = group * slab + lane % slab
    tile = jnp.zeros((ROWS, TILE), jnp.int32)
    lower = jnp.zeros((ROWS, TILE), jnp.int32)
    upper = jnp.zeros((ROWS, TILE), jnp.int32)
    for i in range(TILE // slab):
        here = lane // slab == i
        piece = depth_first[i * ROWS : (i + 1) * ROWS]
        tile = jnp.where(here, piece if i == 0 else pltpu.roll(piece, i * slab, 1), tile)
        for p in range(2):
            spot = here & (row // cols == p)
            lower = jnp.where(spot, bounds[0:1, 2 * i + p : 2 * i + p + 1], lower)
            upper = jnp.where(spot, bounds[1:2, 2 * i + p : 2 * i + p + 1], upper)
    weight = jnp.where((lower <= level) & (level < upper), 1.0, 0.0).astype(F32)
    for part in range(2):
        value = jnp.zeros((ROWS, TILE), F32)
        for material in range(lame.shape[1]):
            value = jnp.where(tile == material, lame[part : part + 1, material : material + 1], value)
        moduli[part] = value * weight


def pack_field(slab, order, arrivals, field, out):
    depth = field.shape[1]
    quarters = TILE // slab
    height = quarters * ROWS
    channels = field.shape[0] // height
    parts = []
    for m in range(channels):
        parts.append([field[m * height + i * ROWS : m * height + (i + 1) * ROWS, :].astype(F32) for i in range(quarters)])
        for at, g in enumerate(order):
            pieces = [piece[:, g * slab : (g + 1) * slab] for piece in parts[m]]
            out[at, m * ROWS : (m + 1) * ROWS, :] = jnp.concatenate(pieces, axis=1).astype(BF16)
    lane = lax.broadcasted_iota(jnp.int32, (ROWS, depth), 1)
    ends = []
    for i in range(quarters):
        mixed = jnp.zeros((ROWS, depth), F32)
        for m in range(channels):
            below = pltpu.roll(parts[m][i], 2 * m + 1, 1)
            above = pltpu.roll(parts[m][i], (2 * m + 1 - slab) % depth, 1)
            mixed = jnp.where((lane % slab == 2 * m) & (lane >= slab), below, mixed)
            mixed = jnp.where((lane % slab == 2 * m + 1) & (lane < depth - slab), above, mixed)
        ends.append(mixed)
    cols = ROWS // 2
    for at, g in enumerate(order):
        short = slice(g * slab, g * slab + slab // 2)
        outer = [end[p * cols : (p + 1) * cols, short] for p in range(2) for end in ends]
        out[at, channels * ROWS :, :] = jnp.concatenate(outer, axis=1).astype(BF16)


def front_kernel(slab, order, source, *rest):
    count = (len(rest) - 4) // 2
    far, out, near = rest[:count], rest[count], rest[count + 1 : 2 * count + 1]
    field, arrived, landed = rest[2 * count + 1 :]
    height = TILE // slab * ROWS
    arrivals = []
    for m in range(field.shape[0] // height):
        rows = pl.ds(m * height, height)
        arrivals.append(pltpu.make_async_copy(source.at[rows, :], field.at[rows, :], arrived.at[m]))
    fetches = [pltpu.make_async_copy(a, b, landed.at[n]) for n, (a, b) in enumerate(zip(far, near))]
    for copy in arrivals + fetches:
        copy.start()
    for copy in arrivals:
        copy.wait()
    pack_field(slab, order, arrivals, field, out)
    for copy in fetches:
        copy.wait()


def gather_kernel(slab, got, tiles, ends, face_x, face_y, plain):
    groups, rows, _ = got.shape
    quarters = TILE // slab
    per = rows // ROWS // 3
    cases = per * groups
    cols = ROWS // 2
    brick_x = lax.axis_index("bx")
    brick_y = lax.axis_index("by")
    for g in range(groups):
        plain[g * rows : (g + 1) * rows, :] = got[g].astype(F32)

    def gather(row):
        return plain[pl.ds(row, groups, stride=rows), :]

    def column(k, p, y):
        return jnp.concatenate([gather((c * 3 + k) * ROWS + p * cols + y) for c in range(per)], axis=0)

    lane = lax.broadcasted_iota(jnp.int32, (cases, TILE), 1)
    packed = [jnp.zeros((cases, TILE), F32) for _ in range(3)]
    for y in range(cols):
        at = y % quarters
        for k in range(3):
            even, odd = column(k, 0, y), column(k, 1, y)
            tiles[k, 0, y] = even
            tiles[k, 1, y] = odd
            even = pltpu.roll(even, at * slab, 1) if at else even
            odd = pltpu.roll(odd, (at + 1 - quarters) * slab % TILE, 1) if at + 1 < quarters else odd
            packed[k] = jnp.where(lane // slab == at, jnp.where(brick_x == 0, odd, even), packed[k])
            if at == quarters - 1:
                face_x[k, y // quarters] = packed[k].astype(BF16)
            if y == 0:
                firsts = (tiles[k, 0, 0], tiles[k, 1, 0])
                for p in range(2):
                    face_y[k, p] = firsts[p].astype(BF16)
            if y == cols - 1:
                for p in range(2):
                    face_y[k, p] = jnp.where(brick_y == 0, tiles[k, p, y], face_y[k, p].astype(F32)).astype(BF16)
        outer = gather(3 * per * ROWS + y)
        for p in range(2):
            spaced = jnp.zeros((groups, TILE), F32)
            for i in range(quarters):
                moved = pltpu.roll(outer, (i * slab - (p * quarters + i) * (slab // 2)) % TILE, 1)
                spaced = jnp.where(lane[:groups] // slab == i, moved, spaced)
            ends[p, y] = spaced


def column_steps(slab, tiles, ends, pairs, linear, moduli, face_x, face_y, best, high, low):
    cases = tiles.shape[3]
    groups = ends.shape[2]
    per = cases // groups
    quarters = TILE // slab
    cols = ROWS // 2
    main = cases // 2 * cases
    wide = lax.broadcasted_iota(jnp.int32, (cases, TILE), 1)
    lower_y = lax.axis_index("by") == 1

    def both(pieces):
        return jnp.concatenate(pieces, axis=0)

    def stress_of(p, y, beside):
        last = jnp.where(p == 0, 0, quarters - 1)
        at_edge = wide // slab == last
        sign = jnp.where(p == 0, 0.5, -0.5).astype(F32)
        grads = []
        for k in range(3):
            mine = tiles[k, p, y]
            other = tiles[k, 1 - p, y]
            shifted = pltpu.roll(other, jnp.where(p == 0, slab, TILE - slab), 1)
            if beside:
                edge = pltpu.roll(face_x[k, y // quarters].astype(F32), lax.rem((last - y % quarters) * slab + TILE, TILE), 1)
            else:
                edge = jnp.zeros((cases, TILE), F32)
            grad_x = sign * (other - jnp.where(at_edge, edge, shifted))
            before = tiles[k, p, y - 1] if y else jnp.where(lower_y, face_y[k, p].astype(F32), 0.0)
            after = tiles[k, p, y + 1] if y + 1 < cols else jnp.where(lower_y, 0.0, face_y[k, p].astype(F32))
            outside = ends[p, y]
            below = both([pltpu.roll(outside, -2 * (c * 3 + k) % TILE, 1) for c in range(per)])
            above = both([pltpu.roll(outside, (slab - 2 - 2 * (c * 3 + k)) % TILE, 1) for c in range(per)])
            below = jnp.where(wide % slab == 0, below, pltpu.roll(mine, 1, 1))
            above = jnp.where(wide % slab == slab - 1, above, pltpu.roll(mine, TILE - 1, 1))
            grads.append((grad_x, 0.5 * (after - before), 0.5 * (above - below)))
        shear = moduli[0, pl.ds(p * cols + y, 1), :]
        first = moduli[1, pl.ds(p * cols + y, 1), :]
        volume = first * (grads[0][0] + grads[1][1] + grads[2][2])
        twice = 2.0 * shear
        return [
            volume + twice * grads[0][0],
            volume + twice * grads[1][1],
            volume + twice * grads[2][2],
            shear * (grads[0][1] + grads[1][0]),
            shear * (grads[1][2] + grads[2][1]),
            shear * (grads[2][0] + grads[0][2]),
        ]

    def build(step, rhs, sums):
        p, columns, beside, _ = step
        stack = [stress_of(p, y, beside) for y in columns]
        stress = [jnp.concatenate([stack[0][n], stack[1][n]], axis=1).astype(BF16) for n in range(6)]
        for n in range(3):
            sums[n * cases : (n + 1) * cases, :] = stress[n]
        exact = [s.astype(F32) for s in stress]
        root = math.sqrt(3.0)
        parts = [
            (0.5 * root) * (exact[0] - exact[1]),
            0.5 * (exact[0] + exact[1]) - exact[2],
            root * exact[3],
            root * exact[4],
            root * exact[5],
        ]
        for s in range(cases // 2 + 1):
            form = None
            for part in parts:
                term = part * (part if s == 0 else pltpu.roll(part, cases - s, 0))
                form = term if form is None else form + term
            upper = form.astype(BF16)
            lower = (form - upper.astype(F32)).astype(BF16)
            at, apart = ((s - 1) * cases, main) if s else (3 * main, cases)
            rhs[at : at + cases, :] = upper
            rhs[at + apart : at + apart + cases, :] = lower
            rhs[at + 2 * apart : at + 2 * apart + cases, :] = upper

    def reduce(step, rhs, sums):
        _, columns, _, slot = step
        mises2 = jnp.dot(pairs[...], rhs[...], preferred_element_type=F32)
        hydro = jnp.dot(linear[:, : 3 * cases], sums[...], preferred_element_type=F32)
        tops = (jnp.max(mises2, axis=0, keepdims=True), jnp.max(hydro, axis=0, keepdims=True), jnp.min(hydro, axis=0, keepdims=True))
        for half, y in enumerate(columns):
            for into, row in zip((best, high, low), tops):
                into[slot, y : y + 1, :] = row[:, half * TILE : (half + 1) * TILE]

    return build, reduce


def run_steps(build, reduce, steps, used, rhs, sums):
    for buffer in rhs:
        buffer[used:, :] = jnp.zeros((buffer.shape[0] - used, 2 * TILE), BF16)
    build(steps[0], rhs[0], sums[0])
    for n, step in enumerate(steps):
        if n + 1 < len(steps):
            build(steps[n + 1], rhs[(n + 1) % 2], sums[(n + 1) % 2])
        reduce(step, rhs[n % 2], sums[n % 2])


def inner_kernel(slab, tiles, ends, pairs, linear, moduli, best, high, low, rhs_even, rhs_odd, sums_even, sums_odd):
    p = lax.axis_index("bx")
    cols = ROWS // 2
    build, reduce = column_steps(slab, tiles, ends, pairs, linear, moduli, None, None, best, high, low)
    steps = [(p, (y, y + 1), False, 0) for y in range(1, cols - 1, 2)]
    run_steps(build, reduce, steps, 3 * (tiles.shape[3] // 2 + 1) * tiles.shape[3], (rhs_even, rhs_odd), (sums_even, sums_odd))


def outer_kernel(
    slab, tiles, ends, pairs, linear, moduli, face_x, face_y, inner_best, inner_high, inner_low,
    peak, spread, rhs_even, rhs_odd, sums_even, sums_odd, best, high, low,
):
    p = lax.axis_index("bx")
    cols = ROWS // 2
    build, reduce = column_steps(slab, tiles, ends, pairs, linear, moduli, face_x, face_y, best, high, low)
    steps = [(p, (0, cols - 1), False, 0)] + [(1 - p, (y, y + 1), True, 1) for y in range(0, cols, 2)]
    run_steps(build, reduce, steps, 3 * (tiles.shape[3] // 2 + 1) * tiles.shape[3], (rhs_even, rhs_odd), (sums_even, sums_odd))
    for into, inner in ((best, inner_best), (high, inner_high), (low, inner_low)):
        into[0, 1 : cols - 1, :] = inner[0, 1 : cols - 1, :]
    for slot, parity in ((0, p), (1, 1 - p)):
        vm = jnp.sqrt(jnp.maximum(best[slot], 0.0))
        hyd = high[slot] * (1.0 / 3.0) - low[slot] * (1.0 / 3.0)
        for i in range(TILE // slab):
            cut = slice(i * slab, (i + 1) * slab)
            peak[2 * i + parity] = vm[:, cut]
            spread[2 * i + parity] = hyd[:, cut]


def tiled_shards(displacements, material_ids, lame, slab_bounds, load_history):
    per, _, rows, cols, depth = displacements.shape
    groups = lax.axis_size("case")
    order = list(EXCHANGE_ORDER)
    slab = depth // groups
    cases = per * groups
    steps = load_history.shape[0]
    channels = per * 3
    vmem = pl.BlockSpec(memory_space=pltpu.VMEM)
    main, picks = pair_table(cases, order)
    total = 3 * main + TILE
    params = pltpu.CompilerParams(vmem_limit_bytes=16 * 1024 * 1024)
    like = jax.ShapeDtypeStruct
    lines = channels * ROWS + cols
    far = [
        pltpu.with_memory_space_constraint(a, pltpu.HBM)
        for a in (
            displacements.reshape(channels * rows * cols, depth),
            load_history.T,
            jnp.asarray(picks, BF16),
            material_ids.reshape(rows * cols, depth),
            lame,
            slab_bounds,
        )
    ]
    with jax.named_scope("front"):
        packed, *near = pl.pallas_call(
            functools.partial(front_kernel, slab, order),
            out_shape=(pltpu.VMEM((groups, lines, TILE), BF16),) + tuple(pltpu.VMEM(a.shape, a.dtype) for a in far[1:]),
            in_specs=[pl.BlockSpec(memory_space=pltpu.HBM)] * len(far),
            out_specs=(vmem,) * len(far),
            scratch_shapes=[
                pltpu.VMEM(far[0].shape, BF16),
                pltpu.SemaphoreType.DMA((channels,)),
                pltpu.SemaphoreType.DMA((len(far) - 1,)),
            ],
            compiler_params=params,
        )(*far)
    with jax.named_scope("prepare"):
        pairs, linear, moduli = pl.pallas_call(
            functools.partial(prepare_kernel, main, slab),
            out_shape=(like((steps, total), BF16), like((steps, TILE), BF16), like((2, ROWS, TILE), F32)),
            in_specs=[vmem] * len(near),
            out_specs=(vmem,) * 3,
            compiler_params=params,
        )(*near)
    got = lax.all_to_all(packed, "case", split_axis=0, concat_axis=0, axis_index_groups=[order], tiled=True)
    with jax.named_scope("gather"):
        tiles, ends, face_x, face_y = pl.pallas_call(
            functools.partial(gather_kernel, slab),
            out_shape=(
                like((3, 2, cols, cases, TILE), F32),
                like((2, cols, groups, TILE), F32),
                like((3, cols * slab // TILE, cases, TILE), BF16),
                like((3, 2, cases, TILE), BF16),
            ),
            in_specs=[vmem],
            out_specs=(vmem,) * 4,
            scratch_shapes=[pltpu.VMEM((groups * lines, TILE), F32)],
            compiler_params=params,
        )(got)
    face_y = lax.ppermute(face_y, "by", [(0, 1), (1, 0)])
    face_x = lax.ppermute(face_x, "bx", [(0, 1), (1, 0)])
    buffers = [pltpu.VMEM((total, 2 * TILE), BF16)] * 2 + [pltpu.VMEM((3 * cases, 2 * TILE), BF16)] * 2
    with jax.named_scope("inner"):
        inner = pl.pallas_call(
            functools.partial(inner_kernel, slab),
            out_shape=(like((1, cols, TILE), F32),) * 3,
            in_specs=[vmem] * 5,
            out_specs=(vmem,) * 3,
            scratch_shapes=buffers,
            compiler_params=params,
        )(tiles, ends, pairs, linear, moduli)
    with jax.named_scope("outer"):
        return pl.pallas_call(
            functools.partial(outer_kernel, slab),
            out_shape=(like((rows, cols, slab), F32),) * 2,
            in_specs=[vmem] * 10,
            out_specs=(vmem,) * 2,
            scratch_shapes=buffers + [pltpu.VMEM((2, cols, TILE), F32)] * 3,
            compiler_params=params,
        )(tiles, ends, pairs, linear, moduli, face_x, face_y, *inner)


def fits_tiles(mesh, displacements, load_history):
    groups, bricks_x, bricks_y = (mesh.shape[a] for a in ("case", "bx", "by"))
    cases, comps, rows, cols, depth = displacements.shape
    if bricks_x != 2 or bricks_y != 2 or cases % groups or depth % groups:
        return False
    per, rows, cols, slab = cases // groups, rows // 2, cols // 2, depth // groups
    return (
        groups == len(EXCHANGE_ORDER) and per == 2 and comps == 3 and rows == 8 and cols == 8 and slab == 32
        and load_history.shape[0] % 16 == 0
    )


def solution(mesh):
    in_specs = (P("case", None, "bx", "by", None), P("bx", "by", None), P(), P(None, "bx"), P())
    out_specs = (P("bx", "by", "case"), P("bx", "by", "case"))

    def run(displacements, material_ids, lame, slab_bounds, load_history):
        body = tiled_shards if fits_tiles(mesh, displacements, load_history) else shards
        placed = jax.shard_map(body, mesh=mesh, in_specs=in_specs, out_specs=out_specs, check_vma=False)
        return placed(displacements, material_ids, lame, slab_bounds, load_history)

    return run
```

```python
import functools
import math

import jax
import jax.numpy as jnp
import numpy as np
from jax import lax
from jax.experimental import pallas as pl
from jax.experimental.pallas import tpu as pltpu
from jax.sharding import PartitionSpec as P


def extended_2(cells, sides, width):
    for axis, dim in sides:
        count = lax.axis_size(axis)
        ends = count - 1
        head = lax.slice_in_dim(cells, 0, width, axis=dim)
        tail = lax.slice_in_dim(cells, cells.shape[dim] - width, cells.shape[dim], axis=dim)
        cells = jnp.concatenate(
            [
                lax.ppermute(tail, axis, [(i, (i + 1) % count) for i in range(ends)]),
                cells,
                lax.ppermute(head, axis, [((i + 1) % count, i) for i in range(ends)]),
            ],
            axis=dim,
        )
    return cells


def derivative(extended, comp, along):
    field = extended[..., comp, :, :, :]
    if along == 0:
        return 0.5 * (field[..., 2:, 1:-1, 1:-1] - field[..., :-2, 1:-1, 1:-1])
    if along == 1:
        return 0.5 * (field[..., 1:-1, 2:, 1:-1] - field[..., 1:-1, :-2, 1:-1])
    return 0.5 * (field[..., 1:-1, 1:-1, 2:] - field[..., 1:-1, 1:-1, :-2])


def combine_stress(grads, shear_mod, lame_first, weight):
    trace = grads[0][0] + grads[1][1] + grads[2][2]
    normal_x = (lame_first * trace + 2.0 * shear_mod * grads[0][0]) * weight
    normal_y = (lame_first * trace + 2.0 * shear_mod * grads[1][1]) * weight
    normal_z = (lame_first * trace + 2.0 * shear_mod * grads[2][2]) * weight
    shear_xy = shear_mod * (grads[0][1] + grads[1][0]) * weight
    shear_yz = shear_mod * (grads[1][2] + grads[2][1]) * weight
    shear_zx = shear_mod * (grads[2][0] + grads[0][2]) * weight
    return jnp.stack([normal_x, normal_y, normal_z, shear_xy, shear_yz, shear_zx], axis=-4)


def stress_field(extended, shear_mod, lame_first, weight):
    extended = extended.astype(jnp.float32)
    grads = [[derivative(extended, comp, along) for along in range(3)] for comp in range(3)]
    return combine_stress(grads, shear_mod, lame_first, weight)


def material_moduli(material_ids, lame):
    shear_mod = jnp.zeros(material_ids.shape, jnp.float32)
    lame_first = jnp.zeros(material_ids.shape, jnp.float32)
    for material in range(lame.shape[1]):
        picked = material_ids == material
        shear_mod = jnp.where(picked, lame[0, material], shear_mod)
        lame_first = jnp.where(picked, lame[1, material], lame_first)
    return (shear_mod, lame_first)


def histories(load_history, blocks):
    cases, comps, rows, cols, single, slab = blocks.shape
    flat = blocks.reshape(cases, comps * rows * cols * single * slab)
    total = load_history.shape[0]
    step_len = min(128, total)
    top_mises = None
    for begin in range(0, total, step_len):
        factors = load_history[begin : begin + step_len]
        history = jnp.dot(factors, flat, preferred_element_type=jnp.float32).reshape(
            step_len, comps, -1
        )
        diff_one = history[:, 0] - history[:, 1]
        diff_two = history[:, 1] - history[:, 2]
        diff_three = history[:, 2] - history[:, 0]
        mises2 = 0.5 * (diff_one * diff_one + diff_two * diff_two + diff_three * diff_three)
        mises2 = mises2 + 3.0 * (
            history[:, 3] * history[:, 3]
            + history[:, 4] * history[:, 4]
            + history[:, 5] * history[:, 5]
        )
        hydro = (history[:, 0] + history[:, 1] + history[:, 2]) / 3.0
        block_mises = jnp.max(mises2, axis=0)
        block_high = jnp.max(hydro, axis=0)
        block_low = jnp.min(hydro, axis=0)
        if top_mises is None:
            top_mises, high, low = (block_mises, block_high, block_low)
        else:
            top_mises = jnp.maximum(top_mises, block_mises)
            high = jnp.maximum(high, block_high)
            low = jnp.minimum(low, block_low)
    peak = jnp.sqrt(top_mises).reshape(rows, cols, slab)
    spread = (high - low).reshape(rows, cols, slab)
    return (peak, spread)


def shards(displacements, material_ids, lame, slab_bounds, load_history):
    cases_here = displacements.shape[0]
    rows = displacements.shape[2]
    cols = displacements.shape[3]
    depth = displacements.shape[4]
    groups = lax.axis_size("case")
    slab = depth // groups
    shear_mod, lame_first = material_moduli(material_ids, lame)
    levels = jnp.arange(depth, dtype=jnp.int32)
    inside = (slab_bounds[0][:, None] <= levels[None, :]) & (
        levels[None, :] < slab_bounds[1][:, None]
    )
    weight = inside.astype(jnp.float32)[:, None, :]
    bordered = extended_2(displacements, (("bx", 2), ("by", 3)), 1)
    extended = jnp.pad(bordered, ((0, 0), (0, 0), (0, 0), (0, 0), (1, 1)))
    stress = stress_field(extended, shear_mod, lame_first, weight).astype(jnp.bfloat16)
    blocks = stress.reshape(cases_here, 6, rows, cols, groups, slab)
    peak, spread = histories(
        load_history, lax.all_to_all(blocks, "case", split_axis=4, concat_axis=0, tiled=True)
    )
    return (peak, spread)


F32 = jnp.float32
BF16 = jnp.bfloat16
TILE = 128
ROWS = 16
EXCHANGE_ORDER = (5, 6, 4, 1, 7, 3, 2, 0)


def pair_table(cases, order):
    groups = len(order)
    per = cases // groups
    place = np.array([order[j % groups] * per + j // groups for j in range(cases)])
    half = cases // 2
    main = half * cases
    picks = np.zeros((cases, 2 * main), np.float32)
    for s in range(half):
        for j in range(cases):
            picks[place[j], s * cases + j] = 1.0
            picks[place[(j + s + 1) % cases], main + s * cases + j] = 2.0 if s + 1 < half else 1.0
    return main, picks


def prepare(main, slab, loads, picks, ids, lame, bounds, pairs, linear, moduli):
    over = (((0,), (0,)), ((), ()))
    cases = loads.shape[0]
    factor = lax.dot_general(loads[...], picks[...], over, preferred_element_type=F32)
    single, other = factor[:, :main], factor[:, main:]
    linear[...] = single[:, :TILE].astype(BF16)
    mixed = single * other
    high = mixed.astype(BF16)
    pairs[:, :main] = high
    pairs[:, main : 2 * main] = high
    pairs[:, 2 * main : 3 * main] = (mixed - high.astype(F32)).astype(BF16)
    square = single[:, :TILE] * single[:, :TILE]
    high = square.astype(BF16).astype(F32)
    col = lax.broadcasted_iota(jnp.int32, square.shape, 1)
    pairs[:, 3 * main :] = jnp.where(col < 2 * cases, high, square - high).astype(BF16)
    group = lax.axis_index("case")
    rows, depth = ids.shape
    cols = ROWS // 2
    depth_first = pltpu.roll(ids[...], (depth - group * slab) % depth, 1)[:, :TILE]
    lane = lax.broadcasted_iota(jnp.int32, (ROWS, TILE), 1)
    row = lax.broadcasted_iota(jnp.int32, (ROWS, TILE), 0)
    level = group * slab + lane % slab
    tile = jnp.zeros((ROWS, TILE), jnp.int32)
    lower = jnp.zeros((ROWS, TILE), jnp.int32)
    upper = jnp.zeros((ROWS, TILE), jnp.int32)
    for i in range(TILE // slab):
        here = lane // slab == i
        piece = depth_first[i * ROWS : (i + 1) * ROWS]
        tile = jnp.where(here, piece if i == 0 else pltpu.roll(piece, i * slab, 1), tile)
        for p in range(2):
            spot = here & (row // cols == p)
            lower = jnp.where(spot, bounds[0:1, 2 * i + p : 2 * i + p + 1], lower)
            upper = jnp.where(spot, bounds[1:2, 2 * i + p : 2 * i + p + 1], upper)
    weight = jnp.where((lower <= level) & (level < upper), 1.0, 0.0).astype(F32)
    for part in range(2):
        value = jnp.zeros((ROWS, TILE), F32)
        for material in range(lame.shape[1]):
            value = jnp.where(tile == material, lame[part : part + 1, material : material + 1], value)
        moduli[part] = value * weight


def pack_field(slab, order, arrivals, field, out):
    depth = field.shape[1]
    quarters = TILE // slab
    height = quarters * ROWS
    channels = field.shape[0] // height
    parts = []
    for m in range(channels):
        parts.append([field[m * height + i * ROWS : m * height + (i + 1) * ROWS, :].astype(F32) for i in range(quarters)])
        for at, g in enumerate(order):
            pieces = [piece[:, g * slab : (g + 1) * slab] for piece in parts[m]]
            out[at, m * ROWS : (m + 1) * ROWS, :] = jnp.concatenate(pieces, axis=1).astype(BF16)
    lane = lax.broadcasted_iota(jnp.int32, (ROWS, depth), 1)
    ends = []
    for i in range(quarters):
        mixed = jnp.zeros((ROWS, depth), F32)
        for m in range(channels):
            below = pltpu.roll(parts[m][i], 2 * m + 1, 1)
            above = pltpu.roll(parts[m][i], (2 * m + 1 - slab) % depth, 1)
            mixed = jnp.where((lane % slab == 2 * m) & (lane >= slab), below, mixed)
            mixed = jnp.where((lane % slab == 2 * m + 1) & (lane < depth - slab), above, mixed)
        ends.append(mixed)
    cols = ROWS // 2
    for at, g in enumerate(order):
        short = slice(g * slab, g * slab + slab // 2)
        outer = [end[p * cols : (p + 1) * cols, short] for p in range(2) for end in ends]
        out[at, channels * ROWS :, :] = jnp.concatenate(outer, axis=1).astype(BF16)


def front_kernel(slab, order, source, *rest):
    count = (len(rest) - 4) // 2
    far, out, near = rest[:count], rest[count], rest[count + 1 : 2 * count + 1]
    field, arrived, landed = rest[2 * count + 1 :]
    height = TILE // slab * ROWS
    arrivals = []
    for m in range(field.shape[0] // height):
        rows = pl.ds(m * height, height)
        arrivals.append(pltpu.make_async_copy(source.at[rows, :], field.at[rows, :], arrived.at[m]))
    fetches = [pltpu.make_async_copy(a, b, landed.at[n]) for n, (a, b) in enumerate(zip(far, near))]
    for copy in arrivals + fetches:
        copy.start()
    for copy in arrivals:
        copy.wait()
    pack_field(slab, order, arrivals, field, out)
    for copy in fetches:
        copy.wait()


def gather_kernel(slab, got, tiles, ends, face_y, plain):
    groups, rows, _ = got.shape
    quarters = TILE // slab
    per = rows // ROWS // 3
    cases = per * groups
    cols = ROWS // 2
    brick_y = lax.axis_index("by")
    for g in range(groups):
        plain[g * rows : (g + 1) * rows, :] = got[g].astype(F32)

    def gather(row):
        return plain[pl.ds(row, groups, stride=rows), :]

    def column(k, p, y):
        return jnp.concatenate([gather((c * 3 + k) * ROWS + p * cols + y) for c in range(per)], axis=0)

    lane = lax.broadcasted_iota(jnp.int32, (cases, TILE), 1)
    for y in range(cols):
        for k in range(3):
            tiles[k, 0, y] = column(k, 0, y)
            tiles[k, 1, y] = column(k, 1, y)
            if y == 0:
                firsts = (tiles[k, 0, 0], tiles[k, 1, 0])
                for p in range(2):
                    face_y[k, p] = firsts[p].astype(BF16)
            if y == cols - 1:
                for p in range(2):
                    face_y[k, p] = jnp.where(brick_y == 0, tiles[k, p, y], face_y[k, p].astype(F32)).astype(BF16)
        outer = gather(3 * per * ROWS + y)
        for p in range(2):
            spaced = jnp.zeros((groups, TILE), F32)
            for i in range(quarters):
                moved = pltpu.roll(outer, (i * slab - (p * quarters + i) * (slab // 2)) % TILE, 1)
                spaced = jnp.where(lane[:groups] // slab == i, moved, spaced)
            ends[p, y] = spaced


def face_kernel(slab, tiles, face_x):
    cases, cols = tiles.shape[3], tiles.shape[2]
    quarters = TILE // slab
    lane = lax.broadcasted_iota(jnp.int32, (cases, TILE), 1)
    p = 1 - lax.axis_index("bx")
    shift = jnp.where(p == 0, 0, slab)
    for k in range(3):
        for h in range(cols // quarters):
            packed = jnp.zeros((cases, TILE), F32)
            for at in range(quarters):
                moved = pltpu.roll(tiles[k, p, h * quarters + at], lax.rem(shift + at * slab, TILE), 1)
                packed = jnp.where(lane // slab == at, moved, packed)
            face_x[k, h] = packed.astype(BF16)


def column_steps(slab, tiles, ends, pairs, linear, moduli, face_x, face_y, best, high, low):
    cases = tiles.shape[3]
    groups = ends.shape[2]
    per = cases // groups
    quarters = TILE // slab
    cols = ROWS // 2
    main = cases // 2 * cases
    wide = lax.broadcasted_iota(jnp.int32, (cases, TILE), 1)
    lower_y = lax.axis_index("by") == 1

    def both(pieces):
        return jnp.concatenate(pieces, axis=0)

    def stress_of(p, y, beside):
        last = jnp.where(p == 0, 0, quarters - 1)
        at_edge = wide // slab == last
        sign = jnp.where(p == 0, 0.5, -0.5).astype(F32)
        grads = []
        for k in range(3):
            mine = tiles[k, p, y]
            other = tiles[k, 1 - p, y]
            shifted = pltpu.roll(other, jnp.where(p == 0, slab, TILE - slab), 1)
            if beside:
                edge = pltpu.roll(face_x[k, y // quarters].astype(F32), lax.rem((last - y % quarters) * slab + TILE, TILE), 1)
            else:
                edge = jnp.zeros((cases, TILE), F32)
            grad_x = sign * (other - jnp.where(at_edge, edge, shifted))
            before = tiles[k, p, y - 1] if y else jnp.where(lower_y, face_y[k, p].astype(F32), 0.0)
            after = tiles[k, p, y + 1] if y + 1 < cols else jnp.where(lower_y, 0.0, face_y[k, p].astype(F32))
            outside = ends[p, y]
            below = both([pltpu.roll(outside, -2 * (c * 3 + k) % TILE, 1) for c in range(per)])
            above = both([pltpu.roll(outside, (slab - 2 - 2 * (c * 3 + k)) % TILE, 1) for c in range(per)])
            below = jnp.where(wide % slab == 0, below, pltpu.roll(mine, 1, 1))
            above = jnp.where(wide % slab == slab - 1, above, pltpu.roll(mine, TILE - 1, 1))
            grads.append((grad_x, 0.5 * (after - before), 0.5 * (above - below)))
        shear = moduli[0, pl.ds(p * cols + y, 1), :]
        first = moduli[1, pl.ds(p * cols + y, 1), :]
        volume = first * (grads[0][0] + grads[1][1] + grads[2][2])
        twice = 2.0 * shear
        return [
            volume + twice * grads[0][0],
            volume + twice * grads[1][1],
            volume + twice * grads[2][2],
            shear * (grads[0][1] + grads[1][0]),
            shear * (grads[1][2] + grads[2][1]),
            shear * (grads[2][0] + grads[0][2]),
        ]

    def build(step, rhs, sums):
        p, columns, beside, _ = step
        stack = [stress_of(p, y, beside) for y in columns]
        stress = [jnp.concatenate([stack[0][n], stack[1][n]], axis=1).astype(BF16) for n in range(6)]
        for n in range(3):
            sums[n * cases : (n + 1) * cases, :] = stress[n]
        exact = [s.astype(F32) for s in stress]
        root = math.sqrt(3.0)
        parts = [
            (0.5 * root) * (exact[0] - exact[1]),
            0.5 * (exact[0] + exact[1]) - exact[2],
            root * exact[3],
            root * exact[4],
            root * exact[5],
        ]
        for s in range(cases // 2 + 1):
            form = None
            for part in parts:
                term = part * (part if s == 0 else pltpu.roll(part, cases - s, 0))
                form = term if form is None else form + term
            upper = form.astype(BF16)
            lower = (form - upper.astype(F32)).astype(BF16)
            at, apart = ((s - 1) * cases, main) if s else (3 * main, cases)
            rhs[at : at + cases, :] = upper
            rhs[at + apart : at + apart + cases, :] = lower
            rhs[at + 2 * apart : at + 2 * apart + cases, :] = upper

    def reduce(step, rhs, sums):
        _, columns, _, slot = step
        mises2 = jnp.dot(pairs[...], rhs[...], preferred_element_type=F32)
        hydro = jnp.dot(linear[:, : 3 * cases], sums[...], preferred_element_type=F32)
        tops = (jnp.max(mises2, axis=0, keepdims=True), jnp.max(hydro, axis=0, keepdims=True), jnp.min(hydro, axis=0, keepdims=True))
        for half, y in enumerate(columns):
            for into, row in zip((best, high, low), tops):
                into[slot, y : y + 1, :] = row[:, half * TILE : (half + 1) * TILE]

    return build, reduce


def run_steps(build, reduce, steps, used, rhs, sums):
    for buffer in rhs:
        buffer[used:, :] = jnp.zeros((buffer.shape[0] - used, 2 * TILE), BF16)
    build(steps[0], rhs[0], sums[0])
    for n, step in enumerate(steps):
        if n + 1 < len(steps):
            build(steps[n + 1], rhs[(n + 1) % 2], sums[(n + 1) % 2])
        reduce(step, rhs[n % 2], sums[n % 2])


def inner_kernel(
    main, slab, tiles, ends, loads, picks, ids, lame, bounds, face_y,
    pairs, linear, moduli, best, high, low, rhs_even, rhs_odd, sums_even, sums_odd,
):
    prepare(main, slab, loads, picks, ids, lame, bounds, pairs, linear, moduli)
    p = lax.axis_index("bx")
    cols = ROWS // 2
    build, reduce = column_steps(slab, tiles, ends, pairs, linear, moduli, None, face_y, best, high, low)
    steps = [(p, (y, y + 1), False, 0) for y in range(0, cols, 2)]
    run_steps(build, reduce, steps, 3 * (tiles.shape[3] // 2 + 1) * tiles.shape[3], (rhs_even, rhs_odd), (sums_even, sums_odd))


def outer_kernel(
    slab, tiles, ends, pairs, linear, moduli, face_x, face_y, inner_best, inner_high, inner_low,
    peak, spread, rhs_even, rhs_odd, sums_even, sums_odd, best, high, low,
):
    p = lax.axis_index("bx")
    cols = ROWS // 2
    build, reduce = column_steps(slab, tiles, ends, pairs, linear, moduli, face_x, face_y, best, high, low)
    steps = [(1 - p, (y, y + 1), True, 0) for y in range(0, cols, 2)]
    run_steps(build, reduce, steps, 3 * (tiles.shape[3] // 2 + 1) * tiles.shape[3], (rhs_even, rhs_odd), (sums_even, sums_odd))
    for parity, top, most, least in ((p, inner_best, inner_high, inner_low), (1 - p, best, high, low)):
        vm = jnp.sqrt(jnp.maximum(top[0], 0.0))
        hyd = most[0] * (1.0 / 3.0) - least[0] * (1.0 / 3.0)
        for i in range(TILE // slab):
            cut = slice(i * slab, (i + 1) * slab)
            peak[2 * i + parity] = vm[:, cut]
            spread[2 * i + parity] = hyd[:, cut]


def tiled_shards(displacements, material_ids, lame, slab_bounds, load_history):
    per, _, rows, cols, depth = displacements.shape
    groups = lax.axis_size("case")
    order = list(EXCHANGE_ORDER)
    slab = depth // groups
    cases = per * groups
    steps = load_history.shape[0]
    channels = per * 3
    vmem = pl.BlockSpec(memory_space=pltpu.VMEM)
    main, picks = pair_table(cases, order)
    total = 3 * main + TILE
    params = pltpu.CompilerParams(vmem_limit_bytes=16 * 1024 * 1024)
    like = jax.ShapeDtypeStruct
    lines = channels * ROWS + cols
    far = [
        pltpu.with_memory_space_constraint(a, pltpu.HBM)
        for a in (
            displacements.reshape(channels * rows * cols, depth),
            load_history.T,
            jnp.asarray(picks, BF16),
            material_ids.reshape(rows * cols, depth),
            lame,
            slab_bounds,
        )
    ]
    with jax.named_scope("front"):
        packed, *near = pl.pallas_call(
            functools.partial(front_kernel, slab, order),
            out_shape=(pltpu.VMEM((groups, lines, TILE), BF16),) + tuple(pltpu.VMEM(a.shape, a.dtype) for a in far[1:]),
            in_specs=[pl.BlockSpec(memory_space=pltpu.HBM)] * len(far),
            out_specs=(vmem,) * len(far),
            scratch_shapes=[
                pltpu.VMEM(far[0].shape, BF16),
                pltpu.SemaphoreType.DMA((channels,)),
                pltpu.SemaphoreType.DMA((len(far) - 1,)),
            ],
            compiler_params=params,
        )(*far)
    got = lax.all_to_all(packed, "case", split_axis=0, concat_axis=0, axis_index_groups=[order], tiled=True)
    with jax.named_scope("gather"):
        tiles, ends, face_y = pl.pallas_call(
            functools.partial(gather_kernel, slab),
            out_shape=(
                like((3, 2, cols, cases, TILE), F32),
                like((2, cols, groups, TILE), F32),
                like((3, 2, cases, TILE), BF16),
            ),
            in_specs=[vmem],
            out_specs=(vmem,) * 3,
            scratch_shapes=[pltpu.VMEM((groups * lines, TILE), F32)],
            compiler_params=params,
        )(got)
    face_y = lax.ppermute(face_y, "by", [(0, 1), (1, 0)])
    with jax.named_scope("face"):
        face_x = pl.pallas_call(
            functools.partial(face_kernel, slab),
            out_shape=like((3, cols * slab // TILE, cases, TILE), BF16),
            in_specs=[vmem],
            out_specs=vmem,
            compiler_params=params,
        )(tiles)
    face_x = lax.ppermute(face_x, "bx", [(0, 1), (1, 0)])
    buffers = [pltpu.VMEM((total, 2 * TILE), BF16)] * 2 + [pltpu.VMEM((3 * cases, 2 * TILE), BF16)] * 2
    with jax.named_scope("inner"):
        pairs, linear, moduli, *inner = pl.pallas_call(
            functools.partial(inner_kernel, main, slab),
            out_shape=(like((steps, total), BF16), like((steps, TILE), BF16), like((2, ROWS, TILE), F32))
            + (like((1, cols, TILE), F32),) * 3,
            in_specs=[vmem] * (3 + len(near)),
            out_specs=(vmem,) * 6,
            scratch_shapes=buffers,
            compiler_params=params,
        )(tiles, ends, *near, face_y)
    with jax.named_scope("outer"):
        return pl.pallas_call(
            functools.partial(outer_kernel, slab),
            out_shape=(like((rows, cols, slab), F32),) * 2,
            in_specs=[vmem] * 10,
            out_specs=(vmem,) * 2,
            scratch_shapes=buffers + [pltpu.VMEM((1, cols, TILE), F32)] * 3,
            compiler_params=params,
        )(tiles, ends, pairs, linear, moduli, face_x, face_y, *inner)


def fits_tiles(mesh, displacements, load_history):
    groups, bricks_x, bricks_y = (mesh.shape[a] for a in ("case", "bx", "by"))
    cases, comps, rows, cols, depth = displacements.shape
    if bricks_x != 2 or bricks_y != 2 or cases % groups or depth % groups:
        return False
    per, rows, cols, slab = cases // groups, rows // 2, cols // 2, depth // groups
    return (
        groups == len(EXCHANGE_ORDER) and per == 2 and comps == 3 and rows == 8 and cols == 8 and slab == 32
        and load_history.shape[0] % 16 == 0
    )


def solution(mesh):
    in_specs = (P("case", None, "bx", "by", None), P("bx", "by", None), P(), P(None, "bx"), P())
    out_specs = (P("bx", "by", "case"), P("bx", "by", "case"))

    def run(displacements, material_ids, lame, slab_bounds, load_history):
        body = tiled_shards if fits_tiles(mesh, displacements, load_history) else shards
        placed = jax.shard_map(body, mesh=mesh, in_specs=in_specs, out_specs=out_specs, check_vma=False)
        return placed(displacements, material_ids, lame, slab_bounds, load_history)

    return run
```

```python
import functools
import math

import jax
import jax.numpy as jnp
import numpy as np
from jax import lax
from jax.experimental import pallas as pl
from jax.experimental.pallas import tpu as pltpu
from jax.sharding import PartitionSpec as P


def extended_2(cells, sides, width):
    for axis, dim in sides:
        count = lax.axis_size(axis)
        ends = count - 1
        head = lax.slice_in_dim(cells, 0, width, axis=dim)
        tail = lax.slice_in_dim(cells, cells.shape[dim] - width, cells.shape[dim], axis=dim)
        cells = jnp.concatenate(
            [
                lax.ppermute(tail, axis, [(i, (i + 1) % count) for i in range(ends)]),
                cells,
                lax.ppermute(head, axis, [((i + 1) % count, i) for i in range(ends)]),
            ],
            axis=dim,
        )
    return cells


def derivative(extended, comp, along):
    field = extended[..., comp, :, :, :]
    if along == 0:
        return 0.5 * (field[..., 2:, 1:-1, 1:-1] - field[..., :-2, 1:-1, 1:-1])
    if along == 1:
        return 0.5 * (field[..., 1:-1, 2:, 1:-1] - field[..., 1:-1, :-2, 1:-1])
    return 0.5 * (field[..., 1:-1, 1:-1, 2:] - field[..., 1:-1, 1:-1, :-2])


def combine_stress(grads, shear_mod, lame_first, weight):
    trace = grads[0][0] + grads[1][1] + grads[2][2]
    normal_x = (lame_first * trace + 2.0 * shear_mod * grads[0][0]) * weight
    normal_y = (lame_first * trace + 2.0 * shear_mod * grads[1][1]) * weight
    normal_z = (lame_first * trace + 2.0 * shear_mod * grads[2][2]) * weight
    shear_xy = shear_mod * (grads[0][1] + grads[1][0]) * weight
    shear_yz = shear_mod * (grads[1][2] + grads[2][1]) * weight
    shear_zx = shear_mod * (grads[2][0] + grads[0][2]) * weight
    return jnp.stack([normal_x, normal_y, normal_z, shear_xy, shear_yz, shear_zx], axis=-4)


def stress_field(extended, shear_mod, lame_first, weight):
    extended = extended.astype(jnp.float32)
    grads = [[derivative(extended, comp, along) for along in range(3)] for comp in range(3)]
    return combine_stress(grads, shear_mod, lame_first, weight)


def material_moduli(material_ids, lame):
    shear_mod = jnp.zeros(material_ids.shape, jnp.float32)
    lame_first = jnp.zeros(material_ids.shape, jnp.float32)
    for material in range(lame.shape[1]):
        picked = material_ids == material
        shear_mod = jnp.where(picked, lame[0, material], shear_mod)
        lame_first = jnp.where(picked, lame[1, material], lame_first)
    return (shear_mod, lame_first)


def histories(load_history, blocks):
    cases, comps, rows, cols, single, slab = blocks.shape
    flat = blocks.reshape(cases, comps * rows * cols * single * slab)
    total = load_history.shape[0]
    step_len = min(128, total)
    top_mises = None
    for begin in range(0, total, step_len):
        factors = load_history[begin : begin + step_len]
        history = jnp.dot(factors, flat, preferred_element_type=jnp.float32).reshape(
            step_len, comps, -1
        )
        diff_one = history[:, 0] - history[:, 1]
        diff_two = history[:, 1] - history[:, 2]
        diff_three = history[:, 2] - history[:, 0]
        mises2 = 0.5 * (diff_one * diff_one + diff_two * diff_two + diff_three * diff_three)
        mises2 = mises2 + 3.0 * (
            history[:, 3] * history[:, 3]
            + history[:, 4] * history[:, 4]
            + history[:, 5] * history[:, 5]
        )
        hydro = (history[:, 0] + history[:, 1] + history[:, 2]) / 3.0
        block_mises = jnp.max(mises2, axis=0)
        block_high = jnp.max(hydro, axis=0)
        block_low = jnp.min(hydro, axis=0)
        if top_mises is None:
            top_mises, high, low = (block_mises, block_high, block_low)
        else:
            top_mises = jnp.maximum(top_mises, block_mises)
            high = jnp.maximum(high, block_high)
            low = jnp.minimum(low, block_low)
    peak = jnp.sqrt(top_mises).reshape(rows, cols, slab)
    spread = (high - low).reshape(rows, cols, slab)
    return (peak, spread)


def shards(displacements, material_ids, lame, slab_bounds, load_history):
    cases_here = displacements.shape[0]
    rows = displacements.shape[2]
    cols = displacements.shape[3]
    depth = displacements.shape[4]
    groups = lax.axis_size("case")
    slab = depth // groups
    shear_mod, lame_first = material_moduli(material_ids, lame)
    levels = jnp.arange(depth, dtype=jnp.int32)
    inside = (slab_bounds[0][:, None] <= levels[None, :]) & (
        levels[None, :] < slab_bounds[1][:, None]
    )
    weight = inside.astype(jnp.float32)[:, None, :]
    bordered = extended_2(displacements, (("bx", 2), ("by", 3)), 1)
    extended = jnp.pad(bordered, ((0, 0), (0, 0), (0, 0), (0, 0), (1, 1)))
    stress = stress_field(extended, shear_mod, lame_first, weight).astype(jnp.bfloat16)
    blocks = stress.reshape(cases_here, 6, rows, cols, groups, slab)
    peak, spread = histories(
        load_history, lax.all_to_all(blocks, "case", split_axis=4, concat_axis=0, tiled=True)
    )
    return (peak, spread)


F32 = jnp.float32
BF16 = jnp.bfloat16
TILE = 128
ROWS = 16
EXCHANGE_ORDER = (5, 6, 4, 1, 7, 3, 2, 0)


def pair_table(cases, order):
    groups = len(order)
    per = cases // groups
    place = np.array([order[j % groups] * per + j // groups for j in range(cases)])
    half = cases // 2
    main = half * cases
    picks = np.zeros((cases, 2 * main), np.float32)
    for s in range(half):
        for j in range(cases):
            picks[place[j], s * cases + j] = 1.0
            picks[place[(j + s + 1) % cases], main + s * cases + j] = 2.0 if s + 1 < half else 1.0
    return main, picks


def prepare(main, slab, loads, picks, ids, lame, bounds, pairs, linear, moduli):
    over = (((0,), (0,)), ((), ()))
    cases = loads.shape[0]
    factor = lax.dot_general(loads[...], picks[...], over, preferred_element_type=F32)
    single, other = factor[:, :main], factor[:, main:]
    linear[...] = single[:, :TILE].astype(BF16)
    mixed = single * other
    high = mixed.astype(BF16)
    pairs[:, :main] = high
    pairs[:, main : 2 * main] = high
    pairs[:, 2 * main : 3 * main] = (mixed - high.astype(F32)).astype(BF16)
    square = single[:, :TILE] * single[:, :TILE]
    high = square.astype(BF16).astype(F32)
    col = lax.broadcasted_iota(jnp.int32, square.shape, 1)
    pairs[:, 3 * main :] = jnp.where(col < 2 * cases, high, square - high).astype(BF16)
    group = lax.axis_index("case")
    rows, depth = ids.shape
    cols = ROWS // 2
    depth_first = pltpu.roll(ids[...], (depth - group * slab) % depth, 1)[:, :TILE]
    lane = lax.broadcasted_iota(jnp.int32, (ROWS, TILE), 1)
    row = lax.broadcasted_iota(jnp.int32, (ROWS, TILE), 0)
    level = group * slab + lane % slab
    tile = jnp.zeros((ROWS, TILE), jnp.int32)
    lower = jnp.zeros((ROWS, TILE), jnp.int32)
    upper = jnp.zeros((ROWS, TILE), jnp.int32)
    for i in range(TILE // slab):
        here = lane // slab == i
        piece = depth_first[i * ROWS : (i + 1) * ROWS]
        tile = jnp.where(here, piece if i == 0 else pltpu.roll(piece, i * slab, 1), tile)
        for p in range(2):
            spot = here & (row // cols == p)
            lower = jnp.where(spot, bounds[0:1, 2 * i + p : 2 * i + p + 1], lower)
            upper = jnp.where(spot, bounds[1:2, 2 * i + p : 2 * i + p + 1], upper)
    weight = jnp.where((lower <= level) & (level < upper), 1.0, 0.0).astype(F32)
    for part in range(2):
        value = jnp.zeros((ROWS, TILE), F32)
        for material in range(lame.shape[1]):
            value = jnp.where(tile == material, lame[part : part + 1, material : material + 1], value)
        moduli[part] = value * weight


def pack_field(slab, order, arrivals, field, out):
    depth = field.shape[1]
    quarters = TILE // slab
    height = quarters * ROWS
    channels = field.shape[0] // height
    parts = []
    for m in range(channels):
        parts.append([field[m * height + i * ROWS : m * height + (i + 1) * ROWS, :].astype(F32) for i in range(quarters)])
        for at, g in enumerate(order):
            pieces = [piece[:, g * slab : (g + 1) * slab] for piece in parts[m]]
            out[at, m * ROWS : (m + 1) * ROWS, :] = jnp.concatenate(pieces, axis=1).astype(BF16)
    lane = lax.broadcasted_iota(jnp.int32, (ROWS, depth), 1)
    ends = []
    for i in range(quarters):
        mixed = jnp.zeros((ROWS, depth), F32)
        for m in range(channels):
            below = pltpu.roll(parts[m][i], 2 * m + 1, 1)
            above = pltpu.roll(parts[m][i], (2 * m + 1 - slab) % depth, 1)
            mixed = jnp.where((lane % slab == 2 * m) & (lane >= slab), below, mixed)
            mixed = jnp.where((lane % slab == 2 * m + 1) & (lane < depth - slab), above, mixed)
        ends.append(mixed)
    cols = ROWS // 2
    for at, g in enumerate(order):
        short = slice(g * slab, g * slab + slab // 2)
        outer = [end[p * cols : (p + 1) * cols, short] for p in range(2) for end in ends]
        packed = jnp.concatenate(outer, axis=1)
        out[at, channels * ROWS :, :] = jnp.concatenate([packed, packed], axis=0).astype(BF16)


def front_kernel(slab, order, source, *rest):
    count = (len(rest) - 4) // 2
    far, out, near = rest[:count], rest[count], rest[count + 1 : 2 * count + 1]
    field, arrived, landed = rest[2 * count + 1 :]
    height = TILE // slab * ROWS
    arrivals = []
    for m in range(field.shape[0] // height):
        rows = pl.ds(m * height, height)
        arrivals.append(pltpu.make_async_copy(source.at[rows, :], field.at[rows, :], arrived.at[m]))
    fetches = [pltpu.make_async_copy(a, b, landed.at[n]) for n, (a, b) in enumerate(zip(far, near))]
    for copy in arrivals + fetches:
        copy.start()
    for copy in arrivals:
        copy.wait()
    pack_field(slab, order, arrivals, field, out)
    for copy in fetches:
        copy.wait()


def gather_kernel(slab, got, tiles, ends, face_y, plain):
    groups, rows, _ = got.shape
    quarters = TILE // slab
    per = rows // ROWS // 3
    cases = per * groups
    cols = ROWS // 2
    brick_y = lax.axis_index("by")
    for g in range(groups):
        plain[g * rows : (g + 1) * rows, :] = got[g].astype(F32)

    def gather(row):
        return plain[pl.ds(row, groups, stride=rows), :]

    def column(k, p, y):
        return jnp.concatenate([gather((c * 3 + k) * ROWS + p * cols + y) for c in range(per)], axis=0)

    lane = lax.broadcasted_iota(jnp.int32, (cases, TILE), 1)
    for y in range(cols):
        for k in range(3):
            tiles[k, 0, y] = column(k, 0, y)
            tiles[k, 1, y] = column(k, 1, y)
            if y == 0:
                firsts = (tiles[k, 0, 0], tiles[k, 1, 0])
                for p in range(2):
                    face_y[k, p] = firsts[p].astype(BF16)
            if y == cols - 1:
                for p in range(2):
                    face_y[k, p] = jnp.where(brick_y == 0, tiles[k, p, y], face_y[k, p].astype(F32)).astype(BF16)
        outer = gather(3 * per * ROWS + y)
        for p in range(2):
            spaced = jnp.zeros((groups, TILE), F32)
            for i in range(quarters):
                moved = pltpu.roll(outer, (i * slab - (p * quarters + i) * (slab // 2)) % TILE, 1)
                spaced = jnp.where(lane[:groups] // slab == i, moved, spaced)
            ends[p, y] = spaced


def face_kernel(slab, tiles, face_x):
    cases, cols = tiles.shape[3], tiles.shape[2]
    quarters = TILE // slab
    lane = lax.broadcasted_iota(jnp.int32, (cases, TILE), 1)
    p = 1 - lax.axis_index("bx")
    shift = jnp.where(p == 0, 0, slab)
    for k in range(3):
        for h in range(cols // quarters):
            packed = jnp.zeros((cases, TILE), F32)
            for at in range(quarters):
                moved = pltpu.roll(tiles[k, p, h * quarters + at], lax.rem(shift + at * slab, TILE), 1)
                packed = jnp.where(lane // slab == at, moved, packed)
            face_x[k, h] = packed.astype(BF16)


def column_steps(slab, tiles, ends, pairs, linear, moduli, face_x, face_y, best, high, low):
    cases = tiles.shape[3]
    groups = ends.shape[2]
    per = cases // groups
    quarters = TILE // slab
    cols = ROWS // 2
    main = cases // 2 * cases
    wide = lax.broadcasted_iota(jnp.int32, (cases, TILE), 1)
    lower_y = lax.axis_index("by") == 1

    def both(pieces):
        return jnp.concatenate(pieces, axis=0)

    def stress_of(p, y, beside):
        last = jnp.where(p == 0, 0, quarters - 1)
        at_edge = wide // slab == last
        sign = jnp.where(p == 0, 0.5, -0.5).astype(F32)
        grads = []
        for k in range(3):
            mine = tiles[k, p, y]
            other = tiles[k, 1 - p, y]
            shifted = pltpu.roll(other, jnp.where(p == 0, slab, TILE - slab), 1)
            if beside:
                edge = pltpu.roll(face_x[k, y // quarters].astype(F32), lax.rem((last - y % quarters) * slab + TILE, TILE), 1)
            else:
                edge = jnp.zeros((cases, TILE), F32)
            grad_x = sign * (other - jnp.where(at_edge, edge, shifted))
            before = tiles[k, p, y - 1] if y else jnp.where(lower_y, face_y[k, p].astype(F32), 0.0)
            after = tiles[k, p, y + 1] if y + 1 < cols else jnp.where(lower_y, 0.0, face_y[k, p].astype(F32))
            outside = ends[p, y]
            below = both([pltpu.roll(outside, -2 * (c * 3 + k) % TILE, 1) for c in range(per)])
            above = both([pltpu.roll(outside, (slab - 2 - 2 * (c * 3 + k)) % TILE, 1) for c in range(per)])
            below = jnp.where(wide % slab == 0, below, pltpu.roll(mine, 1, 1))
            above = jnp.where(wide % slab == slab - 1, above, pltpu.roll(mine, TILE - 1, 1))
            grads.append((grad_x, 0.5 * (after - before), 0.5 * (above - below)))
        shear = moduli[0, pl.ds(p * cols + y, 1), :]
        first = moduli[1, pl.ds(p * cols + y, 1), :]
        volume = first * (grads[0][0] + grads[1][1] + grads[2][2])
        twice = 2.0 * shear
        return [
            volume + twice * grads[0][0],
            volume + twice * grads[1][1],
            volume + twice * grads[2][2],
            shear * (grads[0][1] + grads[1][0]),
            shear * (grads[1][2] + grads[2][1]),
            shear * (grads[2][0] + grads[0][2]),
        ]

    def build(step, rhs, sums):
        p, columns, beside, _ = step
        stack = [stress_of(p, y, beside) for y in columns]
        stress = [jnp.concatenate([stack[0][n], stack[1][n]], axis=1).astype(BF16) for n in range(6)]
        for n in range(3):
            sums[n * cases : (n + 1) * cases, :] = stress[n]
        exact = [s.astype(F32) for s in stress]
        root = math.sqrt(3.0)
        parts = [
            (0.5 * root) * (exact[0] - exact[1]),
            0.5 * (exact[0] + exact[1]) - exact[2],
            root * exact[3],
            root * exact[4],
            root * exact[5],
        ]
        for s in range(cases // 2 + 1):
            form = None
            for part in parts:
                term = part * (part if s == 0 else pltpu.roll(part, cases - s, 0))
                form = term if form is None else form + term
            upper = form.astype(BF16)
            lower = (form - upper.astype(F32)).astype(BF16)
            at, apart = ((s - 1) * cases, main) if s else (3 * main, cases)
            rhs[at : at + cases, :] = upper
            rhs[at + apart : at + apart + cases, :] = lower
            rhs[at + 2 * apart : at + 2 * apart + cases, :] = upper

    def reduce(step, rhs, sums):
        _, columns, _, slot = step
        mises2 = jnp.dot(pairs[...], rhs[...], preferred_element_type=F32)
        hydro = jnp.dot(linear[:, : 3 * cases], sums[...], preferred_element_type=F32)
        tops = (jnp.max(mises2, axis=0, keepdims=True), jnp.max(hydro, axis=0, keepdims=True), jnp.min(hydro, axis=0, keepdims=True))
        for half, y in enumerate(columns):
            for into, row in zip((best, high, low), tops):
                into[slot, y : y + 1, :] = row[:, half * TILE : (half + 1) * TILE]

    return build, reduce


def run_steps(build, reduce, steps, used, rhs, sums):
    for buffer in rhs:
        buffer[used:, :] = jnp.zeros((buffer.shape[0] - used, 2 * TILE), BF16)
    build(steps[0], rhs[0], sums[0])
    for n, step in enumerate(steps):
        if n + 1 < len(steps):
            build(steps[n + 1], rhs[(n + 1) % 2], sums[(n + 1) % 2])
        reduce(step, rhs[n % 2], sums[n % 2])


def inner_kernel(
    main, slab, tiles, ends, loads, picks, ids, lame, bounds, face_y,
    pairs, linear, moduli, best, high, low, rhs_even, rhs_odd, sums_even, sums_odd,
):
    prepare(main, slab, loads, picks, ids, lame, bounds, pairs, linear, moduli)
    p = lax.axis_index("bx")
    cols = ROWS // 2
    build, reduce = column_steps(slab, tiles, ends, pairs, linear, moduli, None, face_y, best, high, low)
    steps = [(p, (y, y + 1), False, 0) for y in range(0, cols, 2)]
    run_steps(build, reduce, steps, 3 * (tiles.shape[3] // 2 + 1) * tiles.shape[3], (rhs_even, rhs_odd), (sums_even, sums_odd))


def outer_kernel(
    slab, tiles, ends, pairs, linear, moduli, face_x, face_y, inner_best, inner_high, inner_low,
    peak, spread, rhs_even, rhs_odd, sums_even, sums_odd, best, high, low,
):
    p = lax.axis_index("bx")
    cols = ROWS // 2
    build, reduce = column_steps(slab, tiles, ends, pairs, linear, moduli, face_x, face_y, best, high, low)
    steps = [(1 - p, (y, y + 1), True, 0) for y in range(0, cols, 2)]
    run_steps(build, reduce, steps, 3 * (tiles.shape[3] // 2 + 1) * tiles.shape[3], (rhs_even, rhs_odd), (sums_even, sums_odd))
    for parity, top, most, least in ((p, inner_best, inner_high, inner_low), (1 - p, best, high, low)):
        vm = jnp.sqrt(jnp.maximum(top[0], 0.0))
        hyd = most[0] * (1.0 / 3.0) - least[0] * (1.0 / 3.0)
        for i in range(TILE // slab):
            cut = slice(i * slab, (i + 1) * slab)
            peak[2 * i + parity] = vm[:, cut]
            spread[2 * i + parity] = hyd[:, cut]


def tiled_shards(displacements, material_ids, lame, slab_bounds, load_history):
    per, _, rows, cols, depth = displacements.shape
    groups = lax.axis_size("case")
    order = list(EXCHANGE_ORDER)
    slab = depth // groups
    cases = per * groups
    steps = load_history.shape[0]
    channels = per * 3
    vmem = pl.BlockSpec(memory_space=pltpu.VMEM)
    main, picks = pair_table(cases, order)
    total = 3 * main + TILE
    params = pltpu.CompilerParams(vmem_limit_bytes=16 * 1024 * 1024)
    like = jax.ShapeDtypeStruct
    lines = (channels + 1) * ROWS
    far = [
        pltpu.with_memory_space_constraint(a, pltpu.HBM)
        for a in (
            displacements.reshape(channels * rows * cols, depth),
            load_history.T,
            jnp.asarray(picks, BF16),
            material_ids.reshape(rows * cols, depth),
            lame,
            slab_bounds,
        )
    ]
    with jax.named_scope("front"):
        packed, *near = pl.pallas_call(
            functools.partial(front_kernel, slab, order),
            out_shape=(pltpu.VMEM((groups, lines, TILE), BF16),) + tuple(pltpu.VMEM(a.shape, a.dtype) for a in far[1:]),
            in_specs=[pl.BlockSpec(memory_space=pltpu.HBM)] * len(far),
            out_specs=(vmem,) * len(far),
            scratch_shapes=[
                pltpu.VMEM(far[0].shape, BF16),
                pltpu.SemaphoreType.DMA((channels,)),
                pltpu.SemaphoreType.DMA((len(far) - 1,)),
            ],
            compiler_params=params,
        )(*far)
    got = lax.all_to_all(packed, "case", split_axis=0, concat_axis=0, axis_index_groups=[order], tiled=True)
    with jax.named_scope("gather"):
        tiles, ends, face_y = pl.pallas_call(
            functools.partial(gather_kernel, slab),
            out_shape=(
                like((3, 2, cols, cases, TILE), F32),
                like((2, cols, groups, TILE), F32),
                like((3, 2, cases, TILE), BF16),
            ),
            in_specs=[vmem],
            out_specs=(vmem,) * 3,
            scratch_shapes=[pltpu.VMEM((groups * lines, TILE), F32)],
            compiler_params=params,
        )(got)
    face_y = lax.ppermute(face_y, "by", [(0, 1), (1, 0)])
    with jax.named_scope("face"):
        face_x = pl.pallas_call(
            functools.partial(face_kernel, slab),
            out_shape=like((3, cols * slab // TILE, cases, TILE), BF16),
            in_specs=[vmem],
            out_specs=vmem,
            compiler_params=params,
        )(tiles)
    face_x = lax.ppermute(face_x, "bx", [(0, 1), (1, 0)])
    buffers = [pltpu.VMEM((total, 2 * TILE), BF16)] * 2 + [pltpu.VMEM((3 * cases, 2 * TILE), BF16)] * 2
    with jax.named_scope("inner"):
        pairs, linear, moduli, *inner = pl.pallas_call(
            functools.partial(inner_kernel, main, slab),
            out_shape=(like((steps, total), BF16), like((steps, TILE), BF16), like((2, ROWS, TILE), F32))
            + (like((1, cols, TILE), F32),) * 3,
            in_specs=[vmem] * (3 + len(near)),
            out_specs=(vmem,) * 6,
            scratch_shapes=buffers,
            compiler_params=params,
        )(tiles, ends, *near, face_y)
    with jax.named_scope("outer"):
        return pl.pallas_call(
            functools.partial(outer_kernel, slab),
            out_shape=(like((rows, cols, slab), F32),) * 2,
            in_specs=[vmem] * 10,
            out_specs=(vmem,) * 2,
            scratch_shapes=buffers + [pltpu.VMEM((1, cols, TILE), F32)] * 3,
            compiler_params=params,
        )(tiles, ends, pairs, linear, moduli, face_x, face_y, *inner)


def fits_tiles(mesh, displacements, load_history):
    groups, bricks_x, bricks_y = (mesh.shape[a] for a in ("case", "bx", "by"))
    cases, comps, rows, cols, depth = displacements.shape
    if bricks_x != 2 or bricks_y != 2 or cases % groups or depth % groups:
        return False
    per, rows, cols, slab = cases // groups, rows // 2, cols // 2, depth // groups
    return (
        groups == len(EXCHANGE_ORDER) and per == 2 and comps == 3 and rows == 8 and cols == 8 and slab == 32
        and load_history.shape[0] % 16 == 0
    )


def solution(mesh):
    in_specs = (P("case", None, "bx", "by", None), P("bx", "by", None), P(), P(None, "bx"), P())
    out_specs = (P("bx", "by", "case"), P("bx", "by", "case"))

    def run(displacements, material_ids, lame, slab_bounds, load_history):
        body = tiled_shards if fits_tiles(mesh, displacements, load_history) else shards
        placed = jax.shard_map(body, mesh=mesh, in_specs=in_specs, out_specs=out_specs, check_vma=False)
        return placed(displacements, material_ids, lame, slab_bounds, load_history)

    return run
```

```python
import functools
import math

import jax
import jax.numpy as jnp
import numpy as np
from jax import lax
from jax.experimental import pallas as pl
from jax.experimental.pallas import tpu as pltpu
from jax.sharding import PartitionSpec as P


def extended_2(cells, sides, width):
    for axis, dim in sides:
        count = lax.axis_size(axis)
        ends = count - 1
        head = lax.slice_in_dim(cells, 0, width, axis=dim)
        tail = lax.slice_in_dim(cells, cells.shape[dim] - width, cells.shape[dim], axis=dim)
        cells = jnp.concatenate(
            [
                lax.ppermute(tail, axis, [(i, (i + 1) % count) for i in range(ends)]),
                cells,
                lax.ppermute(head, axis, [((i + 1) % count, i) for i in range(ends)]),
            ],
            axis=dim,
        )
    return cells


def derivative(extended, comp, along):
    field = extended[..., comp, :, :, :]
    if along == 0:
        return 0.5 * (field[..., 2:, 1:-1, 1:-1] - field[..., :-2, 1:-1, 1:-1])
    if along == 1:
        return 0.5 * (field[..., 1:-1, 2:, 1:-1] - field[..., 1:-1, :-2, 1:-1])
    return 0.5 * (field[..., 1:-1, 1:-1, 2:] - field[..., 1:-1, 1:-1, :-2])


def combine_stress(grads, shear_mod, lame_first, weight):
    trace = grads[0][0] + grads[1][1] + grads[2][2]
    normal_x = (lame_first * trace + 2.0 * shear_mod * grads[0][0]) * weight
    normal_y = (lame_first * trace + 2.0 * shear_mod * grads[1][1]) * weight
    normal_z = (lame_first * trace + 2.0 * shear_mod * grads[2][2]) * weight
    shear_xy = shear_mod * (grads[0][1] + grads[1][0]) * weight
    shear_yz = shear_mod * (grads[1][2] + grads[2][1]) * weight
    shear_zx = shear_mod * (grads[2][0] + grads[0][2]) * weight
    return jnp.stack([normal_x, normal_y, normal_z, shear_xy, shear_yz, shear_zx], axis=-4)


def stress_field(extended, shear_mod, lame_first, weight):
    extended = extended.astype(jnp.float32)
    grads = [[derivative(extended, comp, along) for along in range(3)] for comp in range(3)]
    return combine_stress(grads, shear_mod, lame_first, weight)


def material_moduli(material_ids, lame):
    shear_mod = jnp.zeros(material_ids.shape, jnp.float32)
    lame_first = jnp.zeros(material_ids.shape, jnp.float32)
    for material in range(lame.shape[1]):
        picked = material_ids == material
        shear_mod = jnp.where(picked, lame[0, material], shear_mod)
        lame_first = jnp.where(picked, lame[1, material], lame_first)
    return (shear_mod, lame_first)


def histories(load_history, blocks):
    cases, comps, rows, cols, single, slab = blocks.shape
    flat = blocks.reshape(cases, comps * rows * cols * single * slab)
    total = load_history.shape[0]
    step_len = min(128, total)
    top_mises = None
    for begin in range(0, total, step_len):
        factors = load_history[begin : begin + step_len]
        history = jnp.dot(factors, flat, preferred_element_type=jnp.float32).reshape(
            step_len, comps, -1
        )
        diff_one = history[:, 0] - history[:, 1]
        diff_two = history[:, 1] - history[:, 2]
        diff_three = history[:, 2] - history[:, 0]
        mises2 = 0.5 * (diff_one * diff_one + diff_two * diff_two + diff_three * diff_three)
        mises2 = mises2 + 3.0 * (
            history[:, 3] * history[:, 3]
            + history[:, 4] * history[:, 4]
            + history[:, 5] * history[:, 5]
        )
        hydro = (history[:, 0] + history[:, 1] + history[:, 2]) / 3.0
        block_mises = jnp.max(mises2, axis=0)
        block_high = jnp.max(hydro, axis=0)
        block_low = jnp.min(hydro, axis=0)
        if top_mises is None:
            top_mises, high, low = (block_mises, block_high, block_low)
        else:
            top_mises = jnp.maximum(top_mises, block_mises)
            high = jnp.maximum(high, block_high)
            low = jnp.minimum(low, block_low)
    peak = jnp.sqrt(top_mises).reshape(rows, cols, slab)
    spread = (high - low).reshape(rows, cols, slab)
    return (peak, spread)


def shards(displacements, material_ids, lame, slab_bounds, load_history):
    cases_here = displacements.shape[0]
    rows = displacements.shape[2]
    cols = displacements.shape[3]
    depth = displacements.shape[4]
    groups = lax.axis_size("case")
    slab = depth // groups
    shear_mod, lame_first = material_moduli(material_ids, lame)
    levels = jnp.arange(depth, dtype=jnp.int32)
    inside = (slab_bounds[0][:, None] <= levels[None, :]) & (
        levels[None, :] < slab_bounds[1][:, None]
    )
    weight = inside.astype(jnp.float32)[:, None, :]
    bordered = extended_2(displacements, (("bx", 2), ("by", 3)), 1)
    extended = jnp.pad(bordered, ((0, 0), (0, 0), (0, 0), (0, 0), (1, 1)))
    stress = stress_field(extended, shear_mod, lame_first, weight).astype(jnp.bfloat16)
    blocks = stress.reshape(cases_here, 6, rows, cols, groups, slab)
    peak, spread = histories(
        load_history, lax.all_to_all(blocks, "case", split_axis=4, concat_axis=0, tiled=True)
    )
    return (peak, spread)


F32 = jnp.float32
BF16 = jnp.bfloat16
TILE = 128
ROWS = 16
EXCHANGE_ORDER = (5, 6, 4, 1, 7, 3, 2, 0)


def pair_table(cases, order):
    groups = len(order)
    per = cases // groups
    place = np.array([order[j % groups] * per + j // groups for j in range(cases)])
    half = cases // 2
    main = half * cases
    picks = np.zeros((cases, 2 * main), np.float32)
    for s in range(half):
        for j in range(cases):
            picks[place[j], s * cases + j] = 1.0
            picks[place[(j + s + 1) % cases], main + s * cases + j] = 2.0 if s + 1 < half else 1.0
    return main, picks


def prepare(main, slab, loads, picks, ids, lame, bounds, pairs, linear, moduli):
    over = (((0,), (0,)), ((), ()))
    cases = loads.shape[0]
    factor = lax.dot_general(loads[...], picks[...], over, preferred_element_type=F32)
    single, other = factor[:, :main], factor[:, main:]
    linear[...] = single[:, :TILE].astype(BF16)
    mixed = single * other
    high = mixed.astype(BF16)
    pairs[:, :main] = high
    pairs[:, main : 2 * main] = high
    pairs[:, 2 * main : 3 * main] = (mixed - high.astype(F32)).astype(BF16)
    square = single[:, :TILE] * single[:, :TILE]
    high = square.astype(BF16).astype(F32)
    col = lax.broadcasted_iota(jnp.int32, square.shape, 1)
    pairs[:, 3 * main :] = jnp.where(col < 2 * cases, high, square - high).astype(BF16)
    group = lax.axis_index("case")
    rows, depth = ids.shape
    cols = ROWS // 2
    depth_first = pltpu.roll(ids[...], (depth - group * slab) % depth, 1)[:, :TILE]
    lane = lax.broadcasted_iota(jnp.int32, (ROWS, TILE), 1)
    row = lax.broadcasted_iota(jnp.int32, (ROWS, TILE), 0)
    level = group * slab + lane % slab
    tile = jnp.zeros((ROWS, TILE), jnp.int32)
    lower = jnp.zeros((ROWS, TILE), jnp.int32)
    upper = jnp.zeros((ROWS, TILE), jnp.int32)
    for i in range(TILE // slab):
        here = lane // slab == i
        piece = depth_first[i * ROWS : (i + 1) * ROWS]
        tile = jnp.where(here, piece if i == 0 else pltpu.roll(piece, i * slab, 1), tile)
        for p in range(2):
            spot = here & (row // cols == p)
            lower = jnp.where(spot, bounds[0:1, 2 * i + p : 2 * i + p + 1], lower)
            upper = jnp.where(spot, bounds[1:2, 2 * i + p : 2 * i + p + 1], upper)
    weight = jnp.where((lower <= level) & (level < upper), 1.0, 0.0).astype(F32)
    for part in range(2):
        value = jnp.zeros((ROWS, TILE), F32)
        for material in range(lame.shape[1]):
            value = jnp.where(tile == material, lame[part : part + 1, material : material + 1], value)
        moduli[part] = value * weight


def pack_field(slab, order, arrivals, field, out):
    depth = field.shape[1]
    quarters = TILE // slab
    height = quarters * ROWS
    channels = field.shape[0] // height
    parts = []
    for m in range(channels):
        parts.append([field[m * height + i * ROWS : m * height + (i + 1) * ROWS, :] for i in range(quarters)])
        for at, g in enumerate(order):
            pieces = [piece[:, g * slab : (g + 1) * slab] for piece in parts[m]]
            out[at, m * ROWS : (m + 1) * ROWS, :] = jnp.concatenate(pieces, axis=1)
    lane = lax.broadcasted_iota(jnp.int32, (ROWS, depth), 1)
    place = lane % slab
    inner = (place % 2 == 0) & (lane >= slab) | (place % 2 == 1) & (lane < depth - slab)
    ends = []
    for i in range(quarters):
        mixed = jnp.zeros((ROWS, depth), F32)
        for m in range(channels):
            plane = parts[m][i].astype(F32)
            below = pltpu.roll(plane, 2 * m + 1, 1)
            above = pltpu.roll(plane, (2 * m + 1 - slab) % depth, 1)
            mixed = jnp.where(place == 2 * m, below, jnp.where(place == 2 * m + 1, above, mixed))
        ends.append(jnp.where(inner, mixed, 0.0))
    cols = ROWS // 2
    for at, g in enumerate(order):
        short = slice(g * slab, g * slab + slab // 2)
        outer = [end[p * cols : (p + 1) * cols, short] for p in range(2) for end in ends]
        out[at, channels * ROWS :, :] = jnp.concatenate(outer, axis=1).astype(BF16)


def front_kernel(slab, order, source, *rest):
    count = (len(rest) - 4) // 2
    far, out, near = rest[:count], rest[count], rest[count + 1 : 2 * count + 1]
    field, arrived, landed = rest[2 * count + 1 :]
    height = TILE // slab * ROWS
    arrivals = []
    for m in range(field.shape[0] // height):
        rows = pl.ds(m * height, height)
        arrivals.append(pltpu.make_async_copy(source.at[rows, :], field.at[rows, :], arrived.at[m]))
    fetches = [pltpu.make_async_copy(a, b, landed.at[n]) for n, (a, b) in enumerate(zip(far, near))]
    for copy in arrivals + fetches:
        copy.start()
    for copy in arrivals:
        copy.wait()
    pack_field(slab, order, arrivals, field, out)
    for copy in fetches:
        copy.wait()


def gather_kernel(slab, got, tiles, ends, face_y, plain):
    groups, rows, _ = got.shape
    quarters = TILE // slab
    per = rows // ROWS // 3
    cases = per * groups
    cols = ROWS // 2
    brick_y = lax.axis_index("by")
    for g in range(groups):
        plain[g * rows : (g + 1) * rows, :] = got[g].astype(F32)

    def gather(row):
        return plain[pl.ds(row, groups, stride=rows), :]

    def column(k, p, y):
        return jnp.concatenate([gather((c * 3 + k) * ROWS + p * cols + y) for c in range(per)], axis=0)

    lane = lax.broadcasted_iota(jnp.int32, (cases, TILE), 1)
    for y in range(cols):
        for k in range(3):
            tiles[k, 0, y] = column(k, 0, y)
            tiles[k, 1, y] = column(k, 1, y)
            if y == 0:
                firsts = (tiles[k, 0, 0], tiles[k, 1, 0])
                for p in range(2):
                    face_y[k, p] = firsts[p].astype(BF16)
            if y == cols - 1:
                for p in range(2):
                    face_y[k, p] = jnp.where(brick_y == 0, tiles[k, p, y], face_y[k, p].astype(F32)).astype(BF16)
        outer = gather(3 * per * ROWS + y)
        for p in range(2):
            spaced = jnp.zeros((groups, TILE), F32)
            for i in range(quarters):
                moved = pltpu.roll(outer, (i * slab - (p * quarters + i) * (slab // 2)) % TILE, 1)
                spaced = jnp.where(lane[:groups] // slab == i, moved, spaced)
            ends[p, y] = spaced


def face_kernel(slab, tiles, face_x):
    cases, cols = tiles.shape[3], tiles.shape[2]
    quarters = TILE // slab
    lane = lax.broadcasted_iota(jnp.int32, (cases, TILE), 1)
    p = 1 - lax.axis_index("bx")
    shift = jnp.where(p == 0, 0, slab)
    for k in range(3):
        for h in range(cols // quarters):
            packed = jnp.zeros((cases, TILE), F32)
            for at in range(quarters):
                moved = pltpu.roll(tiles[k, p, h * quarters + at], lax.rem(shift + at * slab, TILE), 1)
                packed = jnp.where(lane // slab == at, moved, packed)
            face_x[k, h] = packed.astype(BF16)


def column_steps(slab, tiles, ends, pairs, linear, moduli, face_x, face_y, best, high, low):
    cases = tiles.shape[3]
    groups = ends.shape[2]
    per = cases // groups
    quarters = TILE // slab
    cols = ROWS // 2
    main = cases // 2 * cases
    wide = lax.broadcasted_iota(jnp.int32, (cases, TILE), 1)
    lower_y = lax.axis_index("by") == 1

    def both(pieces):
        return jnp.concatenate(pieces, axis=0)

    def stress_of(p, y, beside):
        last = jnp.where(p == 0, 0, quarters - 1)
        at_edge = wide // slab == last
        sign = jnp.where(p == 0, 0.5, -0.5).astype(F32)
        grads = []
        for k in range(3):
            mine = tiles[k, p, y]
            other = tiles[k, 1 - p, y]
            shifted = pltpu.roll(other, jnp.where(p == 0, slab, TILE - slab), 1)
            if beside:
                edge = pltpu.roll(face_x[k, y // quarters].astype(F32), lax.rem((last - y % quarters) * slab + TILE, TILE), 1)
            else:
                edge = jnp.zeros((cases, TILE), F32)
            grad_x = sign * (other - jnp.where(at_edge, edge, shifted))
            before = tiles[k, p, y - 1] if y else jnp.where(lower_y, face_y[k, p].astype(F32), 0.0)
            after = tiles[k, p, y + 1] if y + 1 < cols else jnp.where(lower_y, 0.0, face_y[k, p].astype(F32))
            outside = ends[p, y]
            below = both([pltpu.roll(outside, -2 * (c * 3 + k) % TILE, 1) for c in range(per)])
            above = both([pltpu.roll(outside, (slab - 2 - 2 * (c * 3 + k)) % TILE, 1) for c in range(per)])
            below = jnp.where(wide % slab == 0, below, pltpu.roll(mine, 1, 1))
            above = jnp.where(wide % slab == slab - 1, above, pltpu.roll(mine, TILE - 1, 1))
            grads.append((grad_x, 0.5 * (after - before), 0.5 * (above - below)))
        shear = moduli[0, pl.ds(p * cols + y, 1), :]
        first = moduli[1, pl.ds(p * cols + y, 1), :]
        volume = first * (grads[0][0] + grads[1][1] + grads[2][2])
        twice = 2.0 * shear
        return [
            volume + twice * grads[0][0],
            volume + twice * grads[1][1],
            volume + twice * grads[2][2],
            shear * (grads[0][1] + grads[1][0]),
            shear * (grads[1][2] + grads[2][1]),
            shear * (grads[2][0] + grads[0][2]),
        ]

    def build(step, rhs, sums):
        p, columns, beside, _ = step
        stack = [stress_of(p, y, beside) for y in columns]
        stress = [jnp.concatenate([stack[0][n], stack[1][n]], axis=1).astype(BF16) for n in range(6)]
        for n in range(3):
            sums[n * cases : (n + 1) * cases, :] = stress[n]
        exact = [s.astype(F32) for s in stress]
        root = math.sqrt(3.0)
        parts = [
            (0.5 * root) * (exact[0] - exact[1]),
            0.5 * (exact[0] + exact[1]) - exact[2],
            root * exact[3],
            root * exact[4],
            root * exact[5],
        ]
        for s in range(cases // 2 + 1):
            form = None
            for part in parts:
                term = part * (part if s == 0 else pltpu.roll(part, cases - s, 0))
                form = term if form is None else form + term
            upper = form.astype(BF16)
            lower = (form - upper.astype(F32)).astype(BF16)
            at, apart = ((s - 1) * cases, main) if s else (3 * main, cases)
            rhs[at : at + cases, :] = upper
            rhs[at + apart : at + apart + cases, :] = lower
            rhs[at + 2 * apart : at + 2 * apart + cases, :] = upper

    def reduce(step, rhs, sums):
        _, columns, _, slot = step
        mises2 = jnp.dot(pairs[...], rhs[...], preferred_element_type=F32)
        hydro = jnp.dot(linear[:, : 3 * cases], sums[...], preferred_element_type=F32)
        tops = (jnp.max(mises2, axis=0, keepdims=True), jnp.max(hydro, axis=0, keepdims=True), jnp.min(hydro, axis=0, keepdims=True))
        for half, y in enumerate(columns):
            for into, row in zip((best, high, low), tops):
                into[slot, y : y + 1, :] = row[:, half * TILE : (half + 1) * TILE]

    return build, reduce


def run_steps(build, reduce, steps, used, rhs, sums):
    for buffer in rhs:
        buffer[used:, :] = jnp.zeros((buffer.shape[0] - used, 2 * TILE), BF16)
    build(steps[0], rhs[0], sums[0])
    for n, step in enumerate(steps):
        if n + 1 < len(steps):
            build(steps[n + 1], rhs[(n + 1) % 2], sums[(n + 1) % 2])
        reduce(step, rhs[n % 2], sums[n % 2])


def inner_kernel(
    main, slab, tiles, ends, loads, picks, ids, lame, bounds, face_y,
    pairs, linear, moduli, best, high, low, rhs_even, rhs_odd, sums_even, sums_odd,
):
    prepare(main, slab, loads, picks, ids, lame, bounds, pairs, linear, moduli)
    p = lax.axis_index("bx")
    cols = ROWS // 2
    build, reduce = column_steps(slab, tiles, ends, pairs, linear, moduli, None, face_y, best, high, low)
    steps = [(p, (y, y + 1), False, 0) for y in range(0, cols, 2)]
    run_steps(build, reduce, steps, 3 * (tiles.shape[3] // 2 + 1) * tiles.shape[3], (rhs_even, rhs_odd), (sums_even, sums_odd))


def outer_kernel(
    slab, tiles, ends, pairs, linear, moduli, face_x, face_y, inner_best, inner_high, inner_low,
    peak, spread, rhs_even, rhs_odd, sums_even, sums_odd, best, high, low,
):
    p = lax.axis_index("bx")
    cols = ROWS // 2
    build, reduce = column_steps(slab, tiles, ends, pairs, linear, moduli, face_x, face_y, best, high, low)
    steps = [(1 - p, (y, y + 1), True, 0) for y in range(0, cols, 2)]
    run_steps(build, reduce, steps, 3 * (tiles.shape[3] // 2 + 1) * tiles.shape[3], (rhs_even, rhs_odd), (sums_even, sums_odd))
    for parity, top, most, least in ((p, inner_best, inner_high, inner_low), (1 - p, best, high, low)):
        vm = jnp.sqrt(jnp.maximum(top[0], 0.0))
        hyd = most[0] * (1.0 / 3.0) - least[0] * (1.0 / 3.0)
        for i in range(TILE // slab):
            cut = slice(i * slab, (i + 1) * slab)
            peak[2 * i + parity] = vm[:, cut]
            spread[2 * i + parity] = hyd[:, cut]


def tiled_shards(displacements, material_ids, lame, slab_bounds, load_history):
    per, _, rows, cols, depth = displacements.shape
    groups = lax.axis_size("case")
    order = list(EXCHANGE_ORDER)
    slab = depth // groups
    cases = per * groups
    steps = load_history.shape[0]
    channels = per * 3
    vmem = pl.BlockSpec(memory_space=pltpu.VMEM)
    main, picks = pair_table(cases, order)
    total = 3 * main + TILE
    params = pltpu.CompilerParams(vmem_limit_bytes=16 * 1024 * 1024)
    like = jax.ShapeDtypeStruct
    lines = channels * ROWS + cols
    far = [
        pltpu.with_memory_space_constraint(a, pltpu.HBM)
        for a in (
            displacements.reshape(channels * rows * cols, depth),
            load_history.T,
            jnp.asarray(picks, BF16),
            material_ids.reshape(rows * cols, depth),
            lame,
            slab_bounds,
        )
    ]
    with jax.named_scope("front"):
        packed, *near = pl.pallas_call(
            functools.partial(front_kernel, slab, order),
            out_shape=(pltpu.VMEM((groups, lines, TILE), BF16),) + tuple(pltpu.VMEM(a.shape, a.dtype) for a in far[1:]),
            in_specs=[pl.BlockSpec(memory_space=pltpu.HBM)] * len(far),
            out_specs=(vmem,) * len(far),
            scratch_shapes=[
                pltpu.VMEM(far[0].shape, BF16),
                pltpu.SemaphoreType.DMA((channels,)),
                pltpu.SemaphoreType.DMA((len(far) - 1,)),
            ],
            compiler_params=params,
        )(*far)
    got = lax.all_to_all(packed, "case", split_axis=0, concat_axis=0, axis_index_groups=[order], tiled=True)
    with jax.named_scope("gather"):
        tiles, ends, face_y = pl.pallas_call(
            functools.partial(gather_kernel, slab),
            out_shape=(
                like((3, 2, cols, cases, TILE), F32),
                like((2, cols, groups, TILE), F32),
                like((3, 2, cases, TILE), BF16),
            ),
            in_specs=[vmem],
            out_specs=(vmem,) * 3,
            scratch_shapes=[pltpu.VMEM((groups * lines, TILE), F32)],
            compiler_params=params,
        )(got)
    face_y = lax.ppermute(face_y, "by", [(0, 1), (1, 0)])
    with jax.named_scope("face"):
        face_x = pl.pallas_call(
            functools.partial(face_kernel, slab),
            out_shape=like((3, cols * slab // TILE, cases, TILE), BF16),
            in_specs=[vmem],
            out_specs=vmem,
            compiler_params=params,
        )(tiles)
    face_x = lax.ppermute(face_x, "bx", [(0, 1), (1, 0)])
    buffers = [pltpu.VMEM((total, 2 * TILE), BF16)] * 2 + [pltpu.VMEM((3 * cases, 2 * TILE), BF16)] * 2
    with jax.named_scope("inner"):
        pairs, linear, moduli, *inner = pl.pallas_call(
            functools.partial(inner_kernel, main, slab),
            out_shape=(like((steps, total), BF16), like((steps, TILE), BF16), like((2, ROWS, TILE), F32))
            + (like((1, cols, TILE), F32),) * 3,
            in_specs=[vmem] * (3 + len(near)),
            out_specs=(vmem,) * 6,
            scratch_shapes=buffers,
            compiler_params=params,
        )(tiles, ends, *near, face_y)
    with jax.named_scope("outer"):
        return pl.pallas_call(
            functools.partial(outer_kernel, slab),
            out_shape=(like((rows, cols, slab), F32),) * 2,
            in_specs=[vmem] * 10,
            out_specs=(vmem,) * 2,
            scratch_shapes=buffers + [pltpu.VMEM((1, cols, TILE), F32)] * 3,
            compiler_params=params,
        )(tiles, ends, pairs, linear, moduli, face_x, face_y, *inner)


def fits_tiles(mesh, displacements, load_history):
    groups, bricks_x, bricks_y = (mesh.shape[a] for a in ("case", "bx", "by"))
    cases, comps, rows, cols, depth = displacements.shape
    if bricks_x != 2 or bricks_y != 2 or cases % groups or depth % groups:
        return False
    per, rows, cols, slab = cases // groups, rows // 2, cols // 2, depth // groups
    return (
        groups == len(EXCHANGE_ORDER) and per == 2 and comps == 3 and rows == 8 and cols == 8 and slab == 32
        and load_history.shape[0] % 16 == 0
    )


def solution(mesh):
    in_specs = (P("case", None, "bx", "by", None), P("bx", "by", None), P(), P(None, "bx"), P())
    out_specs = (P("bx", "by", "case"), P("bx", "by", "case"))

    def run(displacements, material_ids, lame, slab_bounds, load_history):
        body = tiled_shards if fits_tiles(mesh, displacements, load_history) else shards
        placed = jax.shard_map(body, mesh=mesh, in_specs=in_specs, out_specs=out_specs, check_vma=False)
        return placed(displacements, material_ids, lame, slab_bounds, load_history)

    return run
```

```python
import functools
import math

import jax
import jax.numpy as jnp
import numpy as np
from jax import lax
from jax.experimental import pallas as pl
from jax.experimental.pallas import tpu as pltpu
from jax.sharding import PartitionSpec as P


def extended_2(cells, sides, width):
    for axis, dim in sides:
        count = lax.axis_size(axis)
        ends = count - 1
        head = lax.slice_in_dim(cells, 0, width, axis=dim)
        tail = lax.slice_in_dim(cells, cells.shape[dim] - width, cells.shape[dim], axis=dim)
        cells = jnp.concatenate(
            [
                lax.ppermute(tail, axis, [(i, (i + 1) % count) for i in range(ends)]),
                cells,
                lax.ppermute(head, axis, [((i + 1) % count, i) for i in range(ends)]),
            ],
            axis=dim,
        )
    return cells


def derivative(extended, comp, along):
    field = extended[..., comp, :, :, :]
    if along == 0:
        return 0.5 * (field[..., 2:, 1:-1, 1:-1] - field[..., :-2, 1:-1, 1:-1])
    if along == 1:
        return 0.5 * (field[..., 1:-1, 2:, 1:-1] - field[..., 1:-1, :-2, 1:-1])
    return 0.5 * (field[..., 1:-1, 1:-1, 2:] - field[..., 1:-1, 1:-1, :-2])


def combine_stress(grads, shear_mod, lame_first, weight):
    trace = grads[0][0] + grads[1][1] + grads[2][2]
    normal_x = (lame_first * trace + 2.0 * shear_mod * grads[0][0]) * weight
    normal_y = (lame_first * trace + 2.0 * shear_mod * grads[1][1]) * weight
    normal_z = (lame_first * trace + 2.0 * shear_mod * grads[2][2]) * weight
    shear_xy = shear_mod * (grads[0][1] + grads[1][0]) * weight
    shear_yz = shear_mod * (grads[1][2] + grads[2][1]) * weight
    shear_zx = shear_mod * (grads[2][0] + grads[0][2]) * weight
    return jnp.stack([normal_x, normal_y, normal_z, shear_xy, shear_yz, shear_zx], axis=-4)


def stress_field(extended, shear_mod, lame_first, weight):
    extended = extended.astype(jnp.float32)
    grads = [[derivative(extended, comp, along) for along in range(3)] for comp in range(3)]
    return combine_stress(grads, shear_mod, lame_first, weight)


def material_moduli(material_ids, lame):
    shear_mod = jnp.zeros(material_ids.shape, jnp.float32)
    lame_first = jnp.zeros(material_ids.shape, jnp.float32)
    for material in range(lame.shape[1]):
        picked = material_ids == material
        shear_mod = jnp.where(picked, lame[0, material], shear_mod)
        lame_first = jnp.where(picked, lame[1, material], lame_first)
    return (shear_mod, lame_first)


def histories(load_history, blocks):
    cases, comps, rows, cols, single, slab = blocks.shape
    flat = blocks.reshape(cases, comps * rows * cols * single * slab)
    total = load_history.shape[0]
    step_len = min(128, total)
    top_mises = None
    for begin in range(0, total, step_len):
        factors = load_history[begin : begin + step_len]
        history = jnp.dot(factors, flat, preferred_element_type=jnp.float32).reshape(
            step_len, comps, -1
        )
        diff_one = history[:, 0] - history[:, 1]
        diff_two = history[:, 1] - history[:, 2]
        diff_three = history[:, 2] - history[:, 0]
        mises2 = 0.5 * (diff_one * diff_one + diff_two * diff_two + diff_three * diff_three)
        mises2 = mises2 + 3.0 * (
            history[:, 3] * history[:, 3]
            + history[:, 4] * history[:, 4]
            + history[:, 5] * history[:, 5]
        )
        hydro = (history[:, 0] + history[:, 1] + history[:, 2]) / 3.0
        block_mises = jnp.max(mises2, axis=0)
        block_high = jnp.max(hydro, axis=0)
        block_low = jnp.min(hydro, axis=0)
        if top_mises is None:
            top_mises, high, low = (block_mises, block_high, block_low)
        else:
            top_mises = jnp.maximum(top_mises, block_mises)
            high = jnp.maximum(high, block_high)
            low = jnp.minimum(low, block_low)
    peak = jnp.sqrt(top_mises).reshape(rows, cols, slab)
    spread = (high - low).reshape(rows, cols, slab)
    return (peak, spread)


def shards(displacements, material_ids, lame, slab_bounds, load_history):
    cases_here = displacements.shape[0]
    rows = displacements.shape[2]
    cols = displacements.shape[3]
    depth = displacements.shape[4]
    groups = lax.axis_size("case")
    slab = depth // groups
    shear_mod, lame_first = material_moduli(material_ids, lame)
    levels = jnp.arange(depth, dtype=jnp.int32)
    inside = (slab_bounds[0][:, None] <= levels[None, :]) & (
        levels[None, :] < slab_bounds[1][:, None]
    )
    weight = inside.astype(jnp.float32)[:, None, :]
    bordered = extended_2(displacements, (("bx", 2), ("by", 3)), 1)
    extended = jnp.pad(bordered, ((0, 0), (0, 0), (0, 0), (0, 0), (1, 1)))
    stress = stress_field(extended, shear_mod, lame_first, weight).astype(jnp.bfloat16)
    blocks = stress.reshape(cases_here, 6, rows, cols, groups, slab)
    peak, spread = histories(
        load_history, lax.all_to_all(blocks, "case", split_axis=4, concat_axis=0, tiled=True)
    )
    return (peak, spread)


F32 = jnp.float32
BF16 = jnp.bfloat16
TILE = 128
ROWS = 16
EXCHANGE_ORDER = (5, 6, 4, 1, 7, 3, 2, 0)


def pair_table(cases, order):
    groups = len(order)
    per = cases // groups
    place = np.array([order[j % groups] * per + j // groups for j in range(cases)])
    half = cases // 2
    main = half * cases
    picks = np.zeros((cases, 2 * main), np.float32)
    for s in range(half):
        for j in range(cases):
            picks[place[j], s * cases + j] = 1.0
            picks[place[(j + s + 1) % cases], main + s * cases + j] = 2.0 if s + 1 < half else 1.0
    return main, picks


def prepare(main, slab, loads, picks, ids, lame, bounds, pairs, linear, moduli):
    over = (((0,), (0,)), ((), ()))
    cases = loads.shape[0]
    factor = lax.dot_general(loads[...], picks[...], over, preferred_element_type=F32)
    single, other = factor[:, :main], factor[:, main:]
    linear[...] = single[:, :TILE].astype(BF16)
    mixed = single * other
    high = mixed.astype(BF16)
    pairs[:, :main] = high
    pairs[:, main : 2 * main] = high
    pairs[:, 2 * main : 3 * main] = (mixed - high.astype(F32)).astype(BF16)
    square = single[:, :TILE] * single[:, :TILE]
    high = square.astype(BF16).astype(F32)
    col = lax.broadcasted_iota(jnp.int32, square.shape, 1)
    pairs[:, 3 * main :] = jnp.where(col < 2 * cases, high, square - high).astype(BF16)
    group = lax.axis_index("case")
    rows, depth = ids.shape
    cols = ROWS // 2
    depth_first = pltpu.roll(ids[...], (depth - group * slab) % depth, 1)[:, :TILE]
    lane = lax.broadcasted_iota(jnp.int32, (ROWS, TILE), 1)
    row = lax.broadcasted_iota(jnp.int32, (ROWS, TILE), 0)
    level = group * slab + lane % slab
    tile = jnp.zeros((ROWS, TILE), jnp.int32)
    lower = jnp.zeros((ROWS, TILE), jnp.int32)
    upper = jnp.zeros((ROWS, TILE), jnp.int32)
    for i in range(TILE // slab):
        here = lane // slab == i
        piece = depth_first[i * ROWS : (i + 1) * ROWS]
        tile = jnp.where(here, piece if i == 0 else pltpu.roll(piece, i * slab, 1), tile)
        for p in range(2):
            spot = here & (row // cols == p)
            lower = jnp.where(spot, bounds[0:1, 2 * i + p : 2 * i + p + 1], lower)
            upper = jnp.where(spot, bounds[1:2, 2 * i + p : 2 * i + p + 1], upper)
    weight = jnp.where((lower <= level) & (level < upper), 1.0, 0.0).astype(F32)
    for part in range(2):
        value = jnp.zeros((ROWS, TILE), F32)
        for material in range(lame.shape[1]):
            value = jnp.where(tile == material, lame[part : part + 1, material : material + 1], value)
        moduli[part] = value * weight


def pack_field(slab, order, arrivals, field, out):
    depth = field.shape[1]
    quarters = TILE // slab
    height = quarters * ROWS
    channels = field.shape[0] // height
    parts = []
    for m in range(channels):
        parts.append([field[m * height + i * ROWS : m * height + (i + 1) * ROWS, :] for i in range(quarters)])
        for at, g in enumerate(order):
            pieces = [piece[:, g * slab : (g + 1) * slab] for piece in parts[m]]
            out[at, m * ROWS : (m + 1) * ROWS, :] = jnp.concatenate(pieces, axis=1)
    lane = lax.broadcasted_iota(jnp.int32, (ROWS, depth), 1)
    place = lane % slab
    inner = (place % 2 == 0) & (lane >= slab) | (place % 2 == 1) & (lane < depth - slab)
    ends = []
    for i in range(quarters):
        mixed = jnp.zeros((ROWS, depth), F32)
        for m in range(channels):
            plane = parts[m][i].astype(F32)
            below = pltpu.roll(plane, 2 * m + 1, 1)
            above = pltpu.roll(plane, (2 * m + 1 - slab) % depth, 1)
            mixed = jnp.where(place == 2 * m, below, jnp.where(place == 2 * m + 1, above, mixed))
        ends.append(jnp.where(inner, mixed, 0.0))
    cols = ROWS // 2
    for at, g in enumerate(order):
        short = slice(g * slab, g * slab + slab // 2)
        outer = [end[p * cols : (p + 1) * cols, short] for p in range(2) for end in ends]
        out[at, channels * ROWS :, :] = jnp.concatenate(outer, axis=1).astype(BF16)


def front_kernel(slab, order, source, *rest):
    count = (len(rest) - 4) // 2
    far, out, near = rest[:count], rest[count], rest[count + 1 : 2 * count + 1]
    field, arrived, landed = rest[2 * count + 1 :]
    height = TILE // slab * ROWS
    arrivals = []
    for m in range(field.shape[0] // height):
        rows = pl.ds(m * height, height)
        arrivals.append(pltpu.make_async_copy(source.at[rows, :], field.at[rows, :], arrived.at[m]))
    fetches = [pltpu.make_async_copy(a, b, landed.at[n]) for n, (a, b) in enumerate(zip(far, near))]
    for copy in arrivals + fetches:
        copy.start()
    for copy in arrivals:
        copy.wait()
    pack_field(slab, order, arrivals, field, out)
    for copy in fetches:
        copy.wait()


def gather_kernel(slab, got, tiles, ends, face_y, plain):
    groups, rows, _ = got.shape
    quarters = TILE // slab
    per = rows // ROWS // 3
    cases = per * groups
    cols = ROWS // 2
    brick_y = lax.axis_index("by")
    for g in range(groups):
        plain[g * rows : (g + 1) * rows, :] = got[g].astype(F32)

    def gather(row):
        return plain[pl.ds(row, groups, stride=rows), :]

    def column(k, p, y):
        return jnp.concatenate([gather((c * 3 + k) * ROWS + p * cols + y) for c in range(per)], axis=0)

    lane = lax.broadcasted_iota(jnp.int32, (cases, TILE), 1)
    for y in range(cols):
        for k in range(3):
            tiles[k, 0, y] = column(k, 0, y)
            tiles[k, 1, y] = column(k, 1, y)
            if y == 0:
                firsts = (tiles[k, 0, 0], tiles[k, 1, 0])
                for p in range(2):
                    face_y[k, p] = firsts[p].astype(BF16)
            if y == cols - 1:
                for p in range(2):
                    face_y[k, p] = jnp.where(brick_y == 0, tiles[k, p, y], face_y[k, p].astype(F32)).astype(BF16)
        outer = gather(3 * per * ROWS + y)
        for p in range(2):
            spaced = jnp.zeros((groups, TILE), F32)
            for i in range(quarters):
                moved = pltpu.roll(outer, (i * slab - (p * quarters + i) * (slab // 2)) % TILE, 1)
                spaced = jnp.where(lane[:groups] // slab == i, moved, spaced)
            ends[p, y] = spaced


def face_kernel(slab, tiles, face_x):
    cases, cols = tiles.shape[3], tiles.shape[2]
    quarters = TILE // slab
    lane = lax.broadcasted_iota(jnp.int32, (cases, TILE), 1)
    p = 1 - lax.axis_index("bx")
    shift = jnp.where(p == 0, 0, slab)
    for k in range(3):
        for h in range(cols // quarters):
            packed = jnp.zeros((cases, TILE), F32)
            for at in range(quarters):
                moved = pltpu.roll(tiles[k, p, h * quarters + at], lax.rem(shift + at * slab, TILE), 1)
                packed = jnp.where(lane // slab == at, moved, packed)
            face_x[k, h] = packed.astype(BF16)


def column_steps(slab, tiles, ends, pairs, linear, moduli, face_x, face_y, best, high, low):
    cases = tiles.shape[3]
    groups = ends.shape[2]
    per = cases // groups
    quarters = TILE // slab
    cols = ROWS // 2
    main = cases // 2 * cases
    wide = lax.broadcasted_iota(jnp.int32, (cases, TILE), 1)
    lower_y = lax.axis_index("by") == 1

    def both(pieces):
        return jnp.concatenate(pieces, axis=0)

    def stress_of(p, y, beside):
        last = jnp.where(p == 0, 0, quarters - 1)
        at_edge = wide // slab == last
        sign = jnp.where(p == 0, 0.5, -0.5).astype(F32)
        grads = []
        for k in range(3):
            mine = tiles[k, p, y]
            other = tiles[k, 1 - p, y]
            shifted = pltpu.roll(other, jnp.where(p == 0, slab, TILE - slab), 1)
            if beside:
                edge = pltpu.roll(face_x[k, y // quarters].astype(F32), lax.rem((last - y % quarters) * slab + TILE, TILE), 1)
            else:
                edge = jnp.zeros((cases, TILE), F32)
            grad_x = sign * (other - jnp.where(at_edge, edge, shifted))
            before = tiles[k, p, y - 1] if y else jnp.where(lower_y, face_y[k, p].astype(F32), 0.0)
            after = tiles[k, p, y + 1] if y + 1 < cols else jnp.where(lower_y, 0.0, face_y[k, p].astype(F32))
            outside = ends[p, y]
            below = both([pltpu.roll(outside, -2 * (c * 3 + k) % TILE, 1) for c in range(per)])
            above = both([pltpu.roll(outside, (slab - 2 - 2 * (c * 3 + k)) % TILE, 1) for c in range(per)])
            below = jnp.where(wide % slab == 0, below, pltpu.roll(mine, 1, 1))
            above = jnp.where(wide % slab == slab - 1, above, pltpu.roll(mine, TILE - 1, 1))
            grads.append((grad_x, 0.5 * (after - before), 0.5 * (above - below)))
        shear = moduli[0, pl.ds(p * cols + y, 1), :]
        first = moduli[1, pl.ds(p * cols + y, 1), :]
        volume = first * (grads[0][0] + grads[1][1] + grads[2][2])
        twice = 2.0 * shear
        return [
            volume + twice * grads[0][0],
            volume + twice * grads[1][1],
            volume + twice * grads[2][2],
            shear * (grads[0][1] + grads[1][0]),
            shear * (grads[1][2] + grads[2][1]),
            shear * (grads[2][0] + grads[0][2]),
        ]

    def build(step, rhs, sums):
        p, columns, beside, _ = step
        stack = [stress_of(p, y, beside) for y in columns]
        stress = [jnp.concatenate([stack[0][n], stack[1][n]], axis=1).astype(BF16) for n in range(6)]
        for n in range(3):
            sums[n * cases : (n + 1) * cases, :] = stress[n]
        exact = [s.astype(F32) for s in stress]
        root = math.sqrt(3.0)
        parts = [
            (0.5 * root) * (exact[0] - exact[1]),
            0.5 * (exact[0] + exact[1]) - exact[2],
            root * exact[3],
            root * exact[4],
            root * exact[5],
        ]
        for s in range(cases // 2 + 1):
            form = None
            for part in parts:
                term = part * (part if s == 0 else pltpu.roll(part, cases - s, 0))
                form = term if form is None else form + term
            upper = form.astype(BF16)
            lower = (form - upper.astype(F32)).astype(BF16)
            at, apart = ((s - 1) * cases, main) if s else (3 * main, cases)
            rhs[at : at + cases, :] = upper
            rhs[at + apart : at + apart + cases, :] = lower
            rhs[at + 2 * apart : at + 2 * apart + cases, :] = upper

    def reduce(step, rhs, sums):
        _, columns, _, slot = step
        hydro = jnp.dot(linear[:, : 3 * cases], sums[...], preferred_element_type=F32)
        most, least = jnp.max(hydro, axis=0, keepdims=True), jnp.min(hydro, axis=0, keepdims=True)
        half = pairs.shape[0] // 2
        top = None
        for at in (0, half):
            mises2 = jnp.dot(pairs[at : at + half, :], rhs[...], preferred_element_type=F32)
            found = jnp.max(mises2, axis=0, keepdims=True)
            top = found if top is None else jnp.maximum(top, found)
        tops = (top, most, least)
        for half, y in enumerate(columns):
            for into, row in zip((best, high, low), tops):
                into[slot, y : y + 1, :] = row[:, half * TILE : (half + 1) * TILE]

    return build, reduce


def run_steps(build, reduce, steps, used, rhs, sums):
    for buffer in rhs:
        buffer[used:, :] = jnp.zeros((buffer.shape[0] - used, 2 * TILE), BF16)
    build(steps[0], rhs[0], sums[0])
    for n, step in enumerate(steps):
        if n + 1 < len(steps):
            build(steps[n + 1], rhs[(n + 1) % 2], sums[(n + 1) % 2])
        reduce(step, rhs[n % 2], sums[n % 2])


def inner_kernel(
    main, slab, tiles, ends, loads, picks, ids, lame, bounds, face_y,
    pairs, linear, moduli, best, high, low, rhs_even, rhs_odd, sums_even, sums_odd,
):
    prepare(main, slab, loads, picks, ids, lame, bounds, pairs, linear, moduli)
    p = lax.axis_index("bx")
    cols = ROWS // 2
    build, reduce = column_steps(slab, tiles, ends, pairs, linear, moduli, None, face_y, best, high, low)
    steps = [(p, (y, y + 1), False, 0) for y in range(0, cols, 2)]
    run_steps(build, reduce, steps, 3 * (tiles.shape[3] // 2 + 1) * tiles.shape[3], (rhs_even, rhs_odd), (sums_even, sums_odd))


def outer_kernel(
    slab, tiles, ends, pairs, linear, moduli, face_x, face_y, inner_best, inner_high, inner_low,
    peak, spread, rhs_even, rhs_odd, sums_even, sums_odd, best, high, low,
):
    p = lax.axis_index("bx")
    cols = ROWS // 2
    build, reduce = column_steps(slab, tiles, ends, pairs, linear, moduli, face_x, face_y, best, high, low)
    steps = [(1 - p, (y, y + 1), True, 0) for y in range(0, cols, 2)]
    run_steps(build, reduce, steps, 3 * (tiles.shape[3] // 2 + 1) * tiles.shape[3], (rhs_even, rhs_odd), (sums_even, sums_odd))
    for parity, top, most, least in ((p, inner_best, inner_high, inner_low), (1 - p, best, high, low)):
        vm = jnp.sqrt(jnp.maximum(top[0], 0.0))
        hyd = most[0] * (1.0 / 3.0) - least[0] * (1.0 / 3.0)
        for i in range(TILE // slab):
            cut = slice(i * slab, (i + 1) * slab)
            peak[2 * i + parity] = vm[:, cut]
            spread[2 * i + parity] = hyd[:, cut]


def tiled_shards(displacements, material_ids, lame, slab_bounds, load_history):
    per, _, rows, cols, depth = displacements.shape
    groups = lax.axis_size("case")
    order = list(EXCHANGE_ORDER)
    slab = depth // groups
    cases = per * groups
    steps = load_history.shape[0]
    channels = per * 3
    vmem = pl.BlockSpec(memory_space=pltpu.VMEM)
    main, picks = pair_table(cases, order)
    total = 3 * main + TILE
    params = pltpu.CompilerParams(vmem_limit_bytes=16 * 1024 * 1024)
    like = jax.ShapeDtypeStruct
    lines = channels * ROWS + cols
    far = [
        pltpu.with_memory_space_constraint(a, pltpu.HBM)
        for a in (
            displacements.reshape(channels * rows * cols, depth),
            load_history.T,
            jnp.asarray(picks, BF16),
            material_ids.reshape(rows * cols, depth),
            lame,
            slab_bounds,
        )
    ]
    with jax.named_scope("front"):
        packed, *near = pl.pallas_call(
            functools.partial(front_kernel, slab, order),
            out_shape=(pltpu.VMEM((groups, lines, TILE), BF16),) + tuple(pltpu.VMEM(a.shape, a.dtype) for a in far[1:]),
            in_specs=[pl.BlockSpec(memory_space=pltpu.HBM)] * len(far),
            out_specs=(vmem,) * len(far),
            scratch_shapes=[
                pltpu.VMEM(far[0].shape, BF16),
                pltpu.SemaphoreType.DMA((channels,)),
                pltpu.SemaphoreType.DMA((len(far) - 1,)),
            ],
            compiler_params=params,
        )(*far)
    got = lax.all_to_all(packed, "case", split_axis=0, concat_axis=0, axis_index_groups=[order], tiled=True)
    with jax.named_scope("gather"):
        tiles, ends, face_y = pl.pallas_call(
            functools.partial(gather_kernel, slab),
            out_shape=(
                like((3, 2, cols, cases, TILE), F32),
                like((2, cols, groups, TILE), F32),
                like((3, 2, cases, TILE), BF16),
            ),
            in_specs=[vmem],
            out_specs=(vmem,) * 3,
            scratch_shapes=[pltpu.VMEM((groups * lines, TILE), F32)],
            compiler_params=params,
        )(got)
    face_y = lax.ppermute(face_y, "by", [(0, 1), (1, 0)])
    with jax.named_scope("face"):
        face_x = pl.pallas_call(
            functools.partial(face_kernel, slab),
            out_shape=like((3, cols * slab // TILE, cases, TILE), BF16),
            in_specs=[vmem],
            out_specs=vmem,
            compiler_params=params,
        )(tiles)
    face_x = lax.ppermute(face_x, "bx", [(0, 1), (1, 0)])
    buffers = [pltpu.VMEM((total, 2 * TILE), BF16)] * 2 + [pltpu.VMEM((3 * cases, 2 * TILE), BF16)] * 2
    with jax.named_scope("inner"):
        pairs, linear, moduli, *inner = pl.pallas_call(
            functools.partial(inner_kernel, main, slab),
            out_shape=(like((steps, total), BF16), like((steps, TILE), BF16), like((2, ROWS, TILE), F32))
            + (like((1, cols, TILE), F32),) * 3,
            in_specs=[vmem] * (3 + len(near)),
            out_specs=(vmem,) * 6,
            scratch_shapes=buffers,
            compiler_params=params,
        )(tiles, ends, *near, face_y)
    with jax.named_scope("outer"):
        return pl.pallas_call(
            functools.partial(outer_kernel, slab),
            out_shape=(like((rows, cols, slab), F32),) * 2,
            in_specs=[vmem] * 10,
            out_specs=(vmem,) * 2,
            scratch_shapes=buffers + [pltpu.VMEM((1, cols, TILE), F32)] * 3,
            compiler_params=params,
        )(tiles, ends, pairs, linear, moduli, face_x, face_y, *inner)


def fits_tiles(mesh, displacements, load_history):
    groups, bricks_x, bricks_y = (mesh.shape[a] for a in ("case", "bx", "by"))
    cases, comps, rows, cols, depth = displacements.shape
    if bricks_x != 2 or bricks_y != 2 or cases % groups or depth % groups:
        return False
    per, rows, cols, slab = cases // groups, rows // 2, cols // 2, depth // groups
    return (
        groups == len(EXCHANGE_ORDER) and per == 2 and comps == 3 and rows == 8 and cols == 8 and slab == 32
        and load_history.shape[0] % 16 == 0
    )


def solution(mesh):
    in_specs = (P("case", None, "bx", "by", None), P("bx", "by", None), P(), P(None, "bx"), P())
    out_specs = (P("bx", "by", "case"), P("bx", "by", "case"))

    def run(displacements, material_ids, lame, slab_bounds, load_history):
        body = tiled_shards if fits_tiles(mesh, displacements, load_history) else shards
        placed = jax.shard_map(body, mesh=mesh, in_specs=in_specs, out_specs=out_specs, check_vma=False)
        return placed(displacements, material_ids, lame, slab_bounds, load_history)

    return run
```
